128 devices in a mesh: lon: 16 (over y_hi, z, core), lat: 8 (over y_lo, x).
Axes of the slice: x: 4, y: 4 (y_hi: 2, y_lo: 2; y = y_hi * 2 + y_lo), z: 4, core: 2. Of those that a mesh axis runs over, the one named last changes fastest.
Arguments:
- fields: bfloat16 [4, 48, 384, 192], P(None, 'lat', 'lon'), may hold values from -6 to 6
- cotangent: bfloat16 [4, 48, 384, 192], P(None, 'lat', 'lon'), may hold values from -6 to 6
- bias_table: float32 [8, 2, 6, 3312], P('lat'), may hold values from -4 to 310
- gain_one: float32 [192], replicated, may hold values from 0.5 to 1.5
- w_qkv: bfloat16 [192, 576], replicated, may hold values from -2 to 2
- w_proj: bfloat16 [192, 192], replicated, may hold values from -0.4375 to 0.4375
- gain_two: float32 [192], replicated, may hold values from 0.5 to 1.5
- w_in: bfloat16 [192, 768], replicated, may hold values from -0.4375 to 0.4375
- w_out: bfloat16 [768, 192], replicated, may hold values from -0.21875 to 0.21875
Outputs:
- block_out: bfloat16 [4, 48, 384, 192], P(None, 'lat', 'lon')
- grad_fields: bfloat16 [4, 48, 384, 192], P(None, 'lat', 'lon')
- grad_gain_one: float32 [192], replicated
- grad_w_qkv: float32 [192, 576], replicated
- grad_table: float32 [8, 2, 6, 3312], P('lat')
- grad_w_proj: float32 [192, 192], replicated
- grad_gain_two: float32 [192], replicated
- grad_w_in: float32 [192, 768], replicated
- grad_w_out: float32 [768, 192], replicated
The draws below stay inside these ranges and needn't reach their ends.
All inputs are finite; a program needn't handle non-finite values.
Results may differ from the reference program's by a relative error of at most 0.012.
Values may be sent and summed in bfloat16 or wider, within the bound.
A program may use at most 128 MiB of HBM per device.

```python
import jax
import jax.numpy as jnp
import numpy as np
from jax import lax

C = 192
HEADS = 6
FFH = 768
LEV = 4
POS = 3312
LEVW = 2
NLAT = 48
NLON = 384
LATW = 8


def draw_w_qkv(key, part):
    key = jax.random.fold_in(key, 7)
    key_one = jax.random.fold_in(key, 0)
    base_draw = jax.random.normal(key_one, (C, 3 * C), jnp.float32) * C ** (-0.5)
    return jnp.clip(base_draw, -2.0, 2.0).astype(jnp.bfloat16)


def draw_bias_table(key, part):
    key = jax.random.fold_in(key, 9)
    key_one = jax.random.fold_in(key, 0)
    table_shape = (LATW, LEVW, HEADS, POS)
    return jnp.clip(jax.random.normal(key_one, table_shape, jnp.float32), -4.0, 4.0)


def level_of(own_key, extent, cuts, smallest, high):
    def one(position, parts):
        draws = jax.random.uniform(jax.random.fold_in(jax.random.fold_in(own_key, 6), position), (parts,), jnp.float32, smallest / len(cuts), high / len(cuts))
        return jnp.repeat(jnp.exp(draws), extent[position] // parts).reshape((-1,) + (1,) * (len(extent) - position - 1))

    factor_of = one(*cuts[0])
    for cut in cuts[1:]:
        factor_of = factor_of * one(*cut)
    return factor_of


def scatter_about(own_key, shape, scale, reach, cuts=(), dtype=jnp.bfloat16):
    gain = level_of(own_key, shape, cuts, -0.22, 0.18) if cuts else 1.0
    drawn = jax.random.normal(own_key, shape, jnp.float32) * scale * gain
    return jnp.minimum(jnp.maximum(drawn, -reach), reach).astype(dtype)


def setup_inputs(seed: int = 0) -> dict:
    key_list = jax.random.split(jax.random.key(seed), 10)
    fields = scatter_about(key_list[0], (LEV, NLAT, NLON, C), 1.0, 6.0, ((1, 8), (2, 16)))
    cotangent = scatter_about(key_list[1], (LEV, NLAT, NLON, C), 1.0, 6.0, ((1, 8), (2, 16)))
    bias_table = draw_bias_table(jax.random.fold_in(key_list[9], 71), 0)
    gain_one = jnp.clip(1.0 + 0.1 * jax.random.normal(key_list[3], (C,), jnp.float32), 0.5, 1.5)
    w_qkv = draw_w_qkv(jax.random.fold_in(key_list[9], 71), 0)
    w_proj = scatter_about(key_list[5], (C, C), C ** -0.5, 0.4375)
    gain_two = jnp.clip(1.0 + 0.1 * jax.random.normal(key_list[6], (C,), jnp.float32), 0.5, 1.5)
    w_in = scatter_about(key_list[7], (C, FFH), C ** -0.5, 0.4375)
    w_out = scatter_about(key_list[8], (FFH, C), FFH ** -0.5, 0.21875)
    return dict(fields=fields, cotangent=cotangent, bias_table=bias_table, gain_one=gain_one, w_qkv=w_qkv, w_proj=w_proj, gain_two=gain_two, w_in=w_in, w_out=w_out)


def contract(formula, left_op, right_op):
    return jnp.einsum(formula, left_op.astype(jnp.float32), right_op.astype(jnp.float32))

def weight_grad(left_op, right_op):
    return lax.dot_general(left_op, right_op, (((0,), (0,)), ((), ())), preferred_element_type=jnp.float32)

def layer_norm(values, gain_vec):
    center = values - lax.optimization_barrier(jnp.mean(values, axis=-1, keepdims=True))
    spread = lax.optimization_barrier(jnp.mean(center * center, axis=-1, keepdims=True))
    return center * lax.rsqrt(spread + 1e-05) * gain_vec

def gelu_exact(values):
    return jax.nn.gelu(values, approximate=False)

def position_table():
    token_ids = np.arange(144)
    level_pos = token_ids // 72
    lat_pos = token_ids // 12 % 6
    lon_pos = token_ids % 12
    table_idx = ((level_pos[:, None] * 2 + level_pos[None, :]) * 36 + lat_pos[:, None] * 6 + lat_pos[None, :]) * 23 + lon_pos[:, None] - lon_pos[None, :] + 11
    return jnp.asarray(table_idx.reshape(-1).astype(np.int32))

def to_windows(grid_cells):
    levels, lat_rows, lon_cols, feat_dim = grid_cells.shape
    blocks = grid_cells.reshape(levels // 2, 2, lat_rows // 6, 6, lon_cols // 12, 12, feat_dim)
    blocks = blocks.transpose(2, 0, 4, 1, 3, 5, 6)
    return blocks.reshape(lat_rows // 6, levels // 2, lon_cols // 12, 144, feat_dim)

def from_windows(blocks, levels, lat_rows, lon_cols):
    feat_dim = blocks.shape[-1]
    grid_cells = blocks.reshape(lat_rows // 6, levels // 2, lon_cols // 12, 2, 6, 12, feat_dim)
    return grid_cells.transpose(1, 3, 0, 4, 2, 5, 6).reshape(levels, lat_rows, lon_cols, feat_dim)

def block_pass(fields, cotangent, lat_wrap, bias_table, gain_one, w_qkv, w_proj, gain_two, w_in, w_out):
    levels, lat_rows, lon_cols, width = fields.shape
    depth_dim = width // HEADS
    flat_in = fields.reshape(-1, width).astype(jnp.float32)
    normed_one = layer_norm(flat_in, gain_one).astype(jnp.bfloat16)
    qkv_flat = jnp.dot(normed_one, w_qkv, preferred_element_type=jnp.float32).astype(jnp.bfloat16)
    level_ids = lax.broadcasted_iota(jnp.int32, (levels, lat_rows, lon_cols, 1), 0)
    wrap_ids = jnp.broadcast_to(lat_wrap.reshape(1, lat_rows, 1, 1), (levels, lat_rows, lon_cols, 1))
    region = to_windows((level_ids == levels - 1).astype(jnp.int32) * 2 + wrap_ids)[..., 0]
    windows = to_windows(qkv_flat.reshape(levels, lat_rows, lon_cols, 3 * width))
    win_rows, win_levels, win_cols = (windows.shape[0], windows.shape[1], windows.shape[2])
    qkv_parts = windows.reshape(win_rows, win_levels, win_cols, 144, 3, HEADS, depth_dim)
    queries = qkv_parts[:, :, :, :, 0]
    key_vecs = qkv_parts[:, :, :, :, 1]
    values = qkv_parts[:, :, :, :, 2]
    score_scale = depth_dim ** (-0.5)
    index_table = position_table()
    scores = contract('abcihd,abcjhd->abchij', queries, key_vecs) * score_scale
    pos_bias = jnp.take(bias_table, index_table, axis=3).reshape(win_rows, win_levels, 1, HEADS, 144, 144)
    same_region = (region[:, :, :, :, None] == region[:, :, :, None, :])[:, :, :, None]
    scores = jnp.where(same_region, scores + pos_bias, -1000000000.0)
    row_max = lax.optimization_barrier(jnp.max(scores, axis=-1, keepdims=True))
    exp_scores = jnp.exp(scores - row_max)
    attn_probs = exp_scores / lax.optimization_barrier(jnp.sum(exp_scores, axis=-1, keepdims=True))
    probs_b = attn_probs.astype(jnp.bfloat16)
    mixed_heads = contract('abchij,abcjhd->abcihd', probs_b, values).astype(jnp.bfloat16)
    attended = from_windows(mixed_heads.reshape(win_rows, win_levels, win_cols, 144, width), levels, lat_rows, lon_cols).reshape(-1, width)
    branch = flat_in + jnp.dot(attended, w_proj, preferred_element_type=jnp.float32)
    normed_two = layer_norm(branch, gain_two).astype(jnp.bfloat16)
    pre_act = jnp.dot(normed_two, w_in, preferred_element_type=jnp.float32)
    act_full, gelu_back = jax.vjp(gelu_exact, pre_act)
    act_b = act_full.astype(jnp.bfloat16)
    block_out = (branch + jnp.dot(act_b, w_out, preferred_element_type=jnp.float32)).astype(jnp.bfloat16).reshape(fields.shape)
    grad_out = cotangent.reshape(-1, width)
    g_w_out = weight_grad(act_b, grad_out)
    d_act = jnp.dot(grad_out, w_out.T, preferred_element_type=jnp.float32)
    d_pre = gelu_back(d_act)[0].astype(jnp.bfloat16)
    g_w_in = weight_grad(normed_two, d_pre)
    d_normed_two = jnp.dot(d_pre, w_in.T, preferred_element_type=jnp.float32)
    unused_two, second_back = jax.vjp(layer_norm, branch, gain_two)
    d_branch_norm, g_gain_two = second_back(d_normed_two)
    d_branch = grad_out.astype(jnp.float32) + d_branch_norm
    d_branch_b = d_branch.astype(jnp.bfloat16)
    g_w_proj = weight_grad(attended, d_branch_b)
    d_attended = jnp.dot(d_branch_b, w_proj.T, preferred_element_type=jnp.float32).astype(jnp.bfloat16)
    d_mixed = to_windows(d_attended.reshape(levels, lat_rows, lon_cols, width)).reshape(win_rows, win_levels, win_cols, 144, HEADS, depth_dim)
    d_probs = contract('abcihd,abcjhd->abchij', d_mixed, values)
    d_values = contract('abchij,abcihd->abcjhd', probs_b, d_mixed).astype(jnp.bfloat16)
    d_scores = attn_probs * (d_probs - lax.optimization_barrier(jnp.sum(d_probs * attn_probs, axis=-1, keepdims=True)))
    d_bias = lax.optimization_barrier(jnp.sum(d_scores, axis=2)).reshape(win_rows, win_levels, HEADS, 144 * 144)
    table_sums = jax.ops.segment_sum(jnp.moveaxis(d_bias, 3, 0), index_table, num_segments=bias_table.shape[3])
    g_table = jnp.moveaxis(table_sums, 0, 3)
    d_scores_b = d_scores.astype(jnp.bfloat16)
    d_queries = (contract('abchij,abcjhd->abcihd', d_scores_b, key_vecs) * score_scale).astype(jnp.bfloat16)
    d_keys = (contract('abchij,abcihd->abcjhd', d_scores_b, queries) * score_scale).astype(jnp.bfloat16)
    d_windows = jnp.stack([d_queries, d_keys, d_values], axis=4).reshape(win_rows, win_levels, win_cols, 144, 3 * width)
    d_qkv = from_windows(d_windows, levels, lat_rows, lon_cols).reshape(-1, 3 * width)
    g_w_qkv = weight_grad(normed_one, d_qkv)
    d_normed_one = jnp.dot(d_qkv, w_qkv.T, preferred_element_type=jnp.float32)
    unused_one, first_back = jax.vjp(layer_norm, flat_in, gain_one)
    d_input, g_gain_one = first_back(d_normed_one)
    grad_fields = (d_branch + d_input).astype(jnp.bfloat16).reshape(fields.shape)
    return (block_out, grad_fields, (g_gain_one, g_w_qkv, g_table, g_w_proj, g_gain_two, g_w_in, g_w_out))

def group_rows(grid_cells):
    return grid_cells.reshape(LEV, LATW, 6, NLON, C).transpose(1, 0, 2, 3, 4)

def ungroup_rows(grouped):
    return grouped.transpose(1, 0, 2, 3, 4).reshape(LEV, NLAT, NLON, C)

def reference(fields, cotangent, bias_table, gain_one, w_qkv, w_proj, gain_two, w_in, w_out):
    shifted_in = jnp.roll(fields, (-1, -3, -6), axis=(0, 1, 2))
    shifted_cot = jnp.roll(cotangent, (-1, -3, -6), axis=(0, 1, 2))
    wrap_rows = (jnp.arange(LATW)[:, None] * 6 + jnp.arange(6)[None, :] >= NLAT - 3).astype(jnp.int32)

    def one_group(inputs):
        field_rows, cot_rows, table_rows, wrap_flags = inputs
        return block_pass(field_rows, cot_rows, wrap_flags, table_rows[None], gain_one, w_qkv, w_proj, gain_two, w_in, w_out)
    out_groups, grad_groups, grads = lax.map(one_group, (group_rows(shifted_in), group_rows(shifted_cot), bias_table, wrap_rows))
    block_out = jnp.roll(ungroup_rows(out_groups), (1, 3, 6), axis=(0, 1, 2))
    grad_fields = jnp.roll(ungroup_rows(grad_groups), (1, 3, 6), axis=(0, 1, 2))
    g_gain_one, g_w_qkv, g_table, g_w_proj, g_gain_two, g_w_in, g_w_out = grads
    return (block_out, grad_fields, lax.optimization_barrier(jnp.sum(g_gain_one, axis=0)), lax.optimization_barrier(jnp.sum(g_w_qkv, axis=0)), g_table[:, 0], lax.optimization_barrier(jnp.sum(g_w_proj, axis=0)), lax.optimization_barrier(jnp.sum(g_gain_two, axis=0)), lax.optimization_barrier(jnp.sum(g_w_in, axis=0)), lax.optimization_barrier(jnp.sum(g_w_out, axis=0)))
```

```python
import functools

import jax
import jax.numpy as jnp
import numpy as np
from jax import lax
from jax.experimental import pallas as pl
from jax.experimental.pallas import tpu as pltpu
from jax.sharding import PartitionSpec as P

HEADS = 6
C = 192
FFH = 768
TOK = 144
WIN = 4
ROWS = WIN * TOK
STACK = HEADS * TOK
POS = 3312
SEG = 138
PACK = 2048
TABLE = 256
MESH = pl.DeviceIdType.MESH
F32 = jnp.float32
BF16 = jnp.bfloat16


def placement_in():
    out = np.zeros((TOK, 240), np.float32)
    for half in range(2):
        for lat in range(6):
            for col in range(12):
                lon = half * 12 + col + 6
                source = lat * 24 + lon if lon < 24 else 144 + lat * 16 + lon - 24
                out[half * 72 + lat * 12 + col, source] = 1
    return out


def placement_out():
    out = np.zeros((240, TOK), np.float32)
    for lat in range(6):
        for col in range(24):
            source = col // 12 * 72 + lat * 12 + col % 12
            out[lat * 24 + col, source] = 1
            if col >= 18:
                out[144 + lat * 16 + col - 18, source] = 1
    return out


def placement_end():
    out = np.zeros((TOK, 240), np.float32)
    for lat in range(6):
        for lon in range(24):
            source = lat * 24 + lon - 6 if lon >= 6 else 144 + lat * 16 + lon
            out[lat * 24 + lon, source] = 1
    return out


def spread_matrix():
    out = np.zeros((512, 256), np.float32)
    for level in range(2):
        for lat in range(6):
            for col in range(12):
                out[level * 256 + lat * 23 + 11 - col, level * 72 + lat * 12 + col] = 1
    return out


def region_masks():
    ids = np.arange(TOK)
    level, lat = ids // 72, ids // 12 % 6 >= 3
    out = np.zeros((2, TOK, TOK), np.float32)
    out[0] = level[:, None] != level[None, :]
    out[1] = lat[:, None] != lat[None, :]
    return out


def head_masks():
    out = np.zeros((8, C), np.float32)
    for head in range(HEADS):
        out[head, head * 32 : head * 32 + 32] = 1
    return out


def mm(left, right):
    return lax.dot_general(left, right, (((1,), (0,)), ((), ())), preferred_element_type=F32)


def mm_nt(left, right):
    return lax.dot_general(left, right, (((1,), (1,)), ((), ())), preferred_element_type=F32)


def mm_tn(left, right):
    return lax.dot_general(left, right, (((0,), (0,)), ((), ())), preferred_element_type=F32)


def norm(values):
    center = values - jnp.mean(values, axis=-1, keepdims=True)
    spread = jnp.mean(center * center, axis=-1, keepdims=True)
    inverse = lax.rsqrt(spread + 1e-05)
    return center * inverse, inverse


def norm_grad(d_normed, gain, unit, inverse):
    d_unit = d_normed * gain
    mean_one = jnp.mean(d_unit, axis=-1, keepdims=True)
    mean_two = jnp.mean(d_unit * unit, axis=-1, keepdims=True)
    return inverse * (d_unit - mean_one - unit * mean_two)


def split_heads(value, heads):
    return jnp.concatenate([value * heads[h : h + 1, :] for h in range(HEADS)], axis=0)


def join_heads(stacked, heads):
    total = stacked[0:TOK, :] * heads[0:1, :]
    for h in range(1, HEADS):
        total = total + stacked[h * TOK : (h + 1) * TOK, :] * heads[h : h + 1, :]
    return total


def segment(cell, other):
    return ((2 * (cell // 6) + other) * 36 + 6 * (cell % 6)) * 23


def expand_bias(bias_ref, spread_ref, masks_ref, parts, flat, stage, bias, last):
    flat[...] = jnp.zeros_like(flat)
    for lev in range(2):
        flat[lev * 8 : lev * 8 + HEADS, 0:POS] = bias_ref[0, lev]
    for lev in range(2):
        for cell in range(12):
            for other in range(2):
                start = segment(cell, other)
                for half in range(2):
                    parts[2 * other + half, pl.ds(lev * 72 + cell, HEADS, stride=12), :] = flat[
                        lev * 8 : lev * 8 + HEADS, start + half * 128 : start + half * 128 + 128
                    ]
    for step in range(12):
        total = None
        for other in range(2):
            value = jnp.concatenate([parts[2 * other], parts[2 * other + 1]], axis=1)
            if step:
                value = pltpu.roll(value, 256 - step, 1)
            matrix = spread_ref[other * 256 : (other + 1) * 256, :]
            for _ in range(3):
                part = value.astype(BF16)
                value = value - part.astype(F32)
                term = mm(part, matrix)
                total = term if total is None else total + term
        for lev in range(2):
            for half in range(2):
                stage[lev, half, pl.ds(step, 72, stride=12), :] = total[
                    lev * 72 : (lev + 1) * 72, half * 128 : half * 128 + 128
                ]
    for lev in range(2):
        closed = masks_ref[1] * last
        if lev == 1:
            closed = closed + masks_ref[0]
        for h in range(HEADS):
            rows = slice(h * TOK, (h + 1) * TOK)
            value = jnp.concatenate([stage[lev, 0, rows, :], stage[lev, 1, rows, 0:16]], axis=1)
            bias[lev, rows, :] = jnp.where(closed > 0.5, -1000000000.0, value)


def reduce_table(d_bias, spread_ref, parts, flat, table):
    sums = [None, None]
    for step in range(12):
        value = jnp.concatenate(
            [
                jnp.concatenate(
                    [d_bias[lev, half, pl.ds(step, 72, stride=12), :] for half in range(2)], axis=1
                )
                for lev in range(2)
            ],
            axis=0,
        )
        high = value.astype(BF16)
        low = (value - high.astype(F32)).astype(BF16)
        for other in range(2):
            matrix = spread_ref[other * 256 : (other + 1) * 256, :]
            term = mm_nt(high, matrix) + mm_nt(low, matrix)
            if step:
                sums[other] = sums[other] + pltpu.roll(term, step, 1)
            else:
                sums[other] = term
    for other in range(2):
        for half in range(2):
            parts[2 * other + half] = sums[other][:, half * 128 : half * 128 + 128]
    flat[...] = jnp.zeros_like(flat)
    for lev in range(2):
        for cell in range(12):
            for other in range(2):
                start = segment(cell, other)
                rows = pl.ds(lev * 72 + cell, HEADS, stride=12)
                flat[lev * 8 : lev * 8 + HEADS, start : start + 128] = parts[2 * other, rows, :]
                flat[lev * 8 : lev * 8 + HEADS, start + 128 : start + SEG] = parts[
                    2 * other + 1, rows, :
                ][:, 0 : SEG - 128]
    for part in range(16):
        table[part * 16 : (part + 1) * 16, :] = flat[:, part * 256 : (part + 1) * 256]


def gather_level(own, below, east, corner, matrix, lev):
    source = (lev + 1) % 4
    parts = [
        own[source, 3:6].astype(F32).reshape(72, C),
        below[source].astype(F32).reshape(72, C),
        east[source].astype(F32).reshape(48, C),
        corner[source].astype(F32).reshape(48, C),
    ]
    return mm(matrix, jnp.concatenate(parts, axis=0).astype(BF16))


def gather_all(own, halos, matrix, out):
    below, east, corner = halos
    for lev in range(4):
        rows = gather_level(own, below, east, corner, matrix, lev)
        for half in range(2):
            start = ((lev // 2) * 2 + half) * TOK + (lev % 2) * 72
            out[start : start + 72, :] = rows[half * 72 : (half + 1) * 72, :].astype(out.dtype)


def scatter_all(value, matrix, full, side):
    for lev in range(4):
        parts = []
        for half in range(2):
            start = ((lev // 2) * 2 + half) * TOK + (lev % 2) * 72
            parts.append(value[start : start + 72, :].astype(F32))
        rows = mm(matrix, jnp.concatenate(parts, axis=0).astype(BF16))
        full[lev] = rows[0:144].reshape(6, 24, C).astype(BF16)
        side[lev] = rows[144:240].reshape(6, 16, C).astype(BF16)


def block_kernel(
    n_k,
    n_l,
    fields,
    cotangent,
    bias_ref,
    gain_one,
    w_qkv,
    w_proj,
    gain_two,
    w_in,
    w_out,
    place_in,
    place_out,
    spread_ref,
    masks_ref,
    heads_ref,
    gathered,
    full_out,
    below_out,
    east_out,
    corner_out,
    below,
    east,
    corner,
    side,
    x_ref,
    cot_ref,
    n1_ref,
    q_ref,
    k_ref,
    v_ref,
    bias,
    probs,
    att_ref,
    act_ref,
    dpre_ref,
    n2_ref,
    dbb_ref,
    dbranch_ref,
    datt_ref,
    out_ref,
    dq_ref,
    dk_ref,
    dv_ref,
    d_bias,
    pack,
    parts,
    stage,
    flat,
    table,
    send_pair,
    recv_pair,
    send_lon,
    recv_lon,
    send_lat,
    recv_lat,
    total,
    in_send,
    in_recv,
    out_send,
    out_recv,
    pair_send,
    pair_recv,
    lon_send,
    lon_recv,
    lat_send,
    lat_recv,
    glat_send,
    glat_recv,
    glon_send,
    glon_recv,
    gpair_send,
    gpair_recv,
):
    n_lon = 2 * n_k
    chunk = PACK // n_lon
    rest = TABLE // n_lon
    piece = chunk // n_l
    lon, lat = lax.axis_index("lon"), lax.axis_index("lat")
    core, k = lax.rem(lon, 2), lon // 2
    other = 1 - core

    def at(d_lon, d_lat):
        return (lax.rem(lon + d_lon + n_lon, n_lon), lax.rem(lat + d_lat + n_l, n_l))

    def in_lon8(d):
        return (2 * lax.rem(k + d, n_k) + core, lat)

    partner = (2 * k + other, lat)
    far_lon = lax.rem(lon + 2 * core - 1 + n_lon, n_lon)

    friends = [partner, (far_lon, lat), at(1, 1), at(-1, -1)]
    friends += [in_lon8(d) for d in range(1, n_k)]
    friends += [at(0, d) for d in range(1, n_l)]
    barrier = pltpu.get_barrier_semaphore()
    for friend in friends:
        pl.semaphore_signal(barrier, inc=1, device_id=friend, device_id_type=MESH)
    pl.semaphore_wait(barrier, len(friends))

    def copy(source, target, send, recv, device):
        return pltpu.make_async_remote_copy(
            src_ref=source,
            dst_ref=target,
            send_sem=send,
            recv_sem=recv,
            device_id=device,
            device_id_type=MESH,
        )

    in_copies = []
    for i, source in enumerate((fields, cotangent)):
        in_copies.append(
            [
                copy(source.at[:, 0:3], below.at[i], in_send.at[i, 0], in_recv.at[i, 0], at(0, -1)),
                copy(
                    source.at[:, 3:6, 0:16],
                    east.at[i],
                    in_send.at[i, 1],
                    in_recv.at[i, 1],
                    at(-1, 0),
                ),
                copy(
                    source.at[:, 0:3, 0:16],
                    corner.at[i],
                    in_send.at[i, 2],
                    in_recv.at[i, 2],
                    at(-1, -1),
                ),
            ]
        )
        for c in in_copies[i]:
            c.start()

    def send_out(i):
        copies = [
            copy(
                full_out.at[i, :, 3:6],
                below_out.at[i],
                out_send.at[i, 0],
                out_recv.at[i, 0],
                at(0, 1),
            ),
            copy(side.at[i, :, 0:3], east_out.at[i], out_send.at[i, 1], out_recv.at[i, 1], at(1, 0)),
            copy(
                side.at[i, :, 3:6],
                corner_out.at[i],
                out_send.at[i, 2],
                out_recv.at[i, 2],
                at(1, 1),
            ),
        ]
        for c in copies:
            c.start()
        return copies

    last = (lat == n_l - 1).astype(F32)
    expand_bias(bias_ref, spread_ref, masks_ref, parts, flat, stage, bias, last)

    heads = heads_ref[...]
    heads32 = heads.astype(F32)
    scale = 32**-0.5
    gain1 = gain_one[...]
    gain2 = gain_two[...]

    for c in in_copies[0]:
        c.wait_recv()
    gather_all(fields, (below.at[0], east.at[0], corner.at[0]), place_in[...], x_ref)
    unit, _ = norm(x_ref[...])
    n1 = (unit * gain1).astype(BF16)
    n1_ref[...] = n1
    for i, ref in enumerate((q_ref, k_ref, v_ref)):
        ref[...] = mm(n1, w_qkv[:, i * C : (i + 1) * C]).astype(BF16)

    def attend(w, carry):
        rows = pl.ds(pl.multiple_of(w * TOK, TOK), TOK)
        stacked = split_heads(q_ref[rows, :], heads)
        scores = mm_nt(stacked, k_ref[rows, :]) * scale + bias[w // 2]
        top = jnp.max(scores, axis=-1, keepdims=True)
        exps = jnp.exp(scores - top)
        prob = exps * (1.0 / jnp.sum(exps, axis=-1, keepdims=True))
        probs[w] = prob
        mixed = mm(prob.astype(BF16), v_ref[rows, :])
        att_ref[rows, :] = join_heads(mixed, heads32).astype(BF16)
        return carry

    lax.fori_loop(0, WIN, attend, 0)

    for c in in_copies[1]:
        c.wait_recv()
    gather_all(cotangent, (below.at[1], east.at[1], corner.at[1]), place_in[...], cot_ref)

    half = ROWS // 2

    def feed(i, gain_sum):
        rows = pl.ds(pl.multiple_of(i * half, half), half)
        branch = x_ref[rows, :] + mm(att_ref[rows, :], w_proj[...])
        unit, inverse = norm(branch)
        n2 = (unit * gain2).astype(BF16)
        n2_ref[rows, :] = n2
        pre = mm(n2, w_in[...])
        cdf = 0.5 + 0.5 * lax.erf(pre * (0.5**0.5))
        slope = cdf + pre * (jnp.exp(-0.5 * pre * pre) * ((2.0 * np.pi) ** -0.5))
        act = (pre * cdf).astype(BF16)
        act_ref[rows, :] = act
        out_ref[rows, :] = branch + mm(act, w_out[...])
        cot = cot_ref[rows, :]
        d_pre = (slope * mm_nt(cot, w_out[...])).astype(BF16)
        dpre_ref[rows, :] = d_pre
        d_normed = mm_nt(d_pre, w_in[...])
        d_branch = cot.astype(F32) + norm_grad(d_normed, gain2, unit, inverse)
        dbranch_ref[rows, :] = d_branch
        dbb = d_branch.astype(BF16)
        dbb_ref[rows, :] = dbb
        datt_ref[rows, :] = mm_nt(dbb, w_proj[...]).astype(BF16)
        return gain_sum + jnp.sum(d_normed * unit, axis=0, keepdims=True)

    gain_sum2 = lax.fori_loop(0, 2, feed, jnp.zeros((1, C), F32))
    scatter_all(out_ref, place_out[...], full_out.at[0], side.at[0])
    out_copies = send_out(0)

    pack[1152:PACK, 128:256] = jnp.zeros((PACK - 1152, 128), F32)
    pack[1920:PACK, 0:128] = jnp.zeros((PACK - 1920, 128), F32)
    pack[1928:1929, 0:C] = gain_sum2
    for i in range(3):
        cols = slice(i * 256, (i + 1) * 256)
        pack[i * C : (i + 1) * C, :] = mm_tn(cot_ref[...], act_ref[:, cols])
        pack[576 + i * C : 576 + (i + 1) * C, :] = mm_tn(n2_ref[...], dpre_ref[:, cols])
    pack[1152 : 1152 + C, 0:C] = mm_tn(att_ref[...], dbb_ref[...])

    d_bias[...] = jnp.zeros_like(d_bias)

    def attend_back(w, carry):
        rows = pl.ds(pl.multiple_of(w * TOK, TOK), TOK)
        prob = probs[w]
        d_stacked = split_heads(datt_ref[rows, :], heads)
        d_prob = mm_nt(d_stacked, v_ref[rows, :])
        d_score = prob * (d_prob - jnp.sum(d_prob * prob, axis=-1, keepdims=True))
        d_bias[w // 2, 0] += d_score[:, 0:128]
        d_bias[w // 2, 1, :, 0:16] += d_score[:, 128:144]
        d_score_b = d_score.astype(BF16)
        dv_ref[rows, :] = mm_tn(prob.astype(BF16), d_stacked).astype(BF16)
        dq_ref[rows, :] = (join_heads(mm(d_score_b, k_ref[rows, :]), heads32) * scale).astype(BF16)
        stacked = split_heads(q_ref[rows, :], heads)
        dk_ref[rows, :] = (mm_tn(d_score_b, stacked) * scale).astype(BF16)
        return carry

    lax.fori_loop(0, WIN, attend_back, 0)

    d_normed = None
    for i, ref in enumerate((dq_ref, dk_ref, dv_ref)):
        pack[1344 + i * C : 1344 + (i + 1) * C, 0:C] = mm_tn(n1_ref[...], ref[...])
        term = mm_nt(ref[...], w_qkv[:, i * C : (i + 1) * C])
        d_normed = term if d_normed is None else d_normed + term
    unit, inverse = norm(x_ref[...])
    pack[1920:1921, 0:C] = jnp.sum(d_normed * unit, axis=0, keepdims=True)
    out_ref[...] = dbranch_ref[...] + norm_grad(d_normed, gain1, unit, inverse)
    scatter_all(out_ref, place_out[...], full_out.at[1], side.at[1])
    out_copies += send_out(1)
    reduce_table(d_bias, spread_ref, parts, flat, table)

    def pack_rows(c, kk):
        start = pl.multiple_of((2 * kk + c) * chunk, chunk)
        return pack[pl.ds(start, chunk), :]

    def table_rows(c, kk):
        start = pl.multiple_of((2 * kk + c) * rest, rest)
        return table[pl.ds(start, rest), :]

    sends = []

    def start(c):
        c.start()
        sends.append(c)
        return c

    pair = []
    for d in range(1, n_k + 1):
        kk = lax.rem(k + d, n_k)
        send_pair[d - 1, 0:chunk, :] = pack_rows(other, kk).astype(BF16)
        send_pair[d - 1, chunk : chunk + rest, :] = table_rows(other, kk).astype(BF16)
        pair.append(
            start(
                copy(
                    send_pair.at[d - 1],
                    recv_pair.at[d - 1],
                    pair_send.at[d - 1],
                    pair_recv.at[d - 1],
                    partner,
                )
            )
        )
    along_lon = []
    for d in range(1, n_k + 1):
        kk = lax.rem(k + d, n_k)
        pair[d - 1].wait_recv()
        top = pack_rows(core, kk) + recv_pair[d - 1, 0:chunk, :].astype(F32)
        end = table_rows(core, kk) + recv_pair[d - 1, chunk : chunk + rest, :].astype(F32)
        if d < n_k:
            send_lon[d - 1, 0:chunk, :] = top.astype(BF16)
            send_lon[d - 1, chunk : chunk + rest, :] = end.astype(BF16)
            along_lon.append(
                start(
                    copy(
                        send_lon.at[d - 1],
                        recv_lon.at[d - 1],
                        lon_send.at[d - 1],
                        lon_recv.at[d - 1],
                        in_lon8(d),
                    )
                )
            )
        else:
            total[0:chunk, :] = top
            total[chunk : chunk + rest, :] = end
    for d in range(1, n_k):
        along_lon[d - 1].wait_recv()
        total[...] += recv_lon[d - 1].astype(F32)

    def piece_at(d):
        return pl.ds(pl.multiple_of(lax.rem(lat + d + n_l, n_l) * piece, piece), piece)

    along_lat = []
    for d in range(1, n_l):
        send_lat[d - 1] = total[piece_at(d), :].astype(BF16)
        along_lat.append(
            start(
                copy(
                    send_lat.at[d - 1],
                    recv_lat.at[d - 1],
                    lat_send.at[d - 1],
                    lat_recv.at[d - 1],
                    at(0, d),
                )
            )
        )
    final = total[piece_at(0), :]
    for d in range(1, n_l):
        along_lat[d - 1].wait_recv()
        final = final + recv_lat[d - 1].astype(F32)
    gathered[core, k, piece_at(0), :] = final.astype(BF16)
    gathered[core, k, chunk : chunk + rest, :] = total[chunk : chunk + rest, :].astype(BF16)

    for d in range(1, n_l):
        mine = gathered.at[core, k, piece_at(0), :]
        start(copy(mine, mine, glat_send.at[d - 1], glat_recv.at[d - 1], at(0, d)))
    for d in range(1, n_l):
        theirs = gathered.at[core, k, piece_at(-d), :]
        copy(theirs, theirs, glat_send.at[d - 1], glat_recv.at[d - 1], partner).wait_recv()
    mine = gathered.at[core, k]
    for d in range(1, n_k):
        start(copy(mine, mine, glon_send.at[d - 1], glon_recv.at[d - 1], in_lon8(d)))
    start(copy(mine, mine, gpair_send.at[0], gpair_recv.at[0], partner))
    for d in range(1, n_k):
        theirs = gathered.at[core, lax.rem(k - d + n_k, n_k)]
        copy(theirs, theirs, glon_send.at[d - 1], glon_recv.at[d - 1], partner).wait_recv()
        start(copy(theirs, theirs, gpair_send.at[d], gpair_recv.at[d], partner))
    for d in range(n_k):
        theirs = gathered.at[other, lax.rem(k - d + n_k, n_k)]
        copy(theirs, theirs, gpair_send.at[d], gpair_recv.at[d], partner).wait_recv()

    for c in out_copies:
        c.wait_recv()
    for c in in_copies[0] + in_copies[1] + out_copies + sends:
        c.wait_send()


def finish_kernel(
    n_k,
    gathered,
    full_out,
    below_out,
    east_out,
    corner_out,
    place_end,
    block_out,
    grad_fields,
    g_gain_one,
    g_w_qkv,
    g_table,
    g_w_proj,
    g_gain_two,
    g_w_in,
    g_w_out,
    weights,
):
    n_lon = 2 * n_k
    chunk = PACK // n_lon
    rest = TABLE // n_lon
    for i, ref in enumerate((block_out, grad_fields)):
        for lev in range(4):
            parts = [
                below_out[i, lev].astype(F32).reshape(72, C),
                full_out[i, lev, 0:3].astype(F32).reshape(72, C),
                corner_out[i, lev].astype(F32).reshape(48, C),
                east_out[i, lev].astype(F32).reshape(48, C),
            ]
            rows = mm(place_end[...], jnp.concatenate(parts, axis=0).astype(BF16))
            ref[(lev + 1) % 4] = rows.reshape(6, 24, C).astype(BF16)
    for part in range(n_lon):
        weights[part * chunk : (part + 1) * chunk, :] = gathered[
            part % 2, part // 2, 0:chunk, :
        ].astype(F32)
    for i in range(3):
        cols = slice(i * 256, (i + 1) * 256)
        g_w_out[cols, :] = weights[i * C : (i + 1) * C, :].T
        g_w_in[:, cols] = weights[576 + i * C : 576 + (i + 1) * C, :]
        g_w_qkv[:, i * C : (i + 1) * C] = weights[1344 + i * C : 1344 + (i + 1) * C, 0:C]
    g_w_proj[...] = weights[1152 : 1152 + C, 0:C]
    g_gain_one[...] = weights[1920:1921, 0:C]
    g_gain_two[...] = weights[1928:1929, 0:C]
    for part in range(13):
        width = min(256, POS - part * 256)
        place, offset = divmod(part * 16, rest)
        value = gathered[place % 2, place // 2, chunk + offset : chunk + offset + 16, :].astype(F32)
        for lev in range(2):
            g_table[0, lev, :, part * 256 : part * 256 + width] = value[
                lev * 8 : lev * 8 + HEADS, 0:width
            ]


def local(n_k, n_l, fields, cotangent, bias_table, gain_one, w_qkv, w_proj, gain_two, w_in, w_out):
    n_lon = 2 * n_k
    chunk = PACK // n_lon
    rest = TABLE // n_lon
    piece = chunk // n_l
    sds = jax.ShapeDtypeStruct
    vmem = pltpu.VMEM
    dma = pltpu.SemaphoreType.DMA
    whole = pl.BlockSpec(memory_space=pltpu.VMEM)
    moved = (
        sds((2, n_k, chunk + rest, 256), BF16),
        sds((2, 4, 6, 24, C), BF16),
        sds((2, 4, 3, 24, C), BF16),
        sds((2, 4, 3, 16, C), BF16),
        sds((2, 4, 3, 16, C), BF16),
    )
    results = pl.pallas_call(
        functools.partial(block_kernel, n_k, n_l),
        out_shape=moved,
        in_specs=[whole] * 14,
        out_specs=[whole] * 5,
        scratch_shapes=[
            vmem((2, 4, 3, 24, C), BF16),
            vmem((2, 4, 3, 16, C), BF16),
            vmem((2, 4, 3, 16, C), BF16),
            vmem((2, 4, 6, 16, C), BF16),
            vmem((ROWS, C), F32),
            vmem((ROWS, C), BF16),
            vmem((ROWS, C), BF16),
            vmem((ROWS, C), BF16),
            vmem((ROWS, C), BF16),
            vmem((ROWS, C), BF16),
            vmem((2, STACK, TOK), F32),
            vmem((WIN, STACK, TOK), F32),
            vmem((ROWS, C), BF16),
            vmem((ROWS, FFH), BF16),
            vmem((ROWS, FFH), BF16),
            vmem((ROWS, C), BF16),
            vmem((ROWS, C), BF16),
            vmem((ROWS, C), F32),
            vmem((ROWS, C), BF16),
            vmem((ROWS, C), F32),
            vmem((ROWS, C), BF16),
            vmem((ROWS, C), BF16),
            vmem((ROWS, C), BF16),
            vmem((2, 2, STACK, 128), F32),
            vmem((PACK, 256), F32),
            vmem((4, TOK, 128), F32),
            vmem((2, 2, STACK, 128), F32),
            vmem((16, 4096), F32),
            vmem((TABLE, 256), F32),
            vmem((n_k, chunk + rest, 256), BF16),
            vmem((n_k, chunk + rest, 256), BF16),
            vmem((n_k - 1, chunk + rest, 256), BF16),
            vmem((n_k - 1, chunk + rest, 256), BF16),
            vmem((n_l - 1, piece, 256), BF16),
            vmem((n_l - 1, piece, 256), BF16),
            vmem((chunk + rest, 256), F32),
            dma((2, 3)),
            dma((2, 3)),
            dma((2, 3)),
            dma((2, 3)),
            dma((n_k,)),
            dma((n_k,)),
            dma((n_k - 1,)),
            dma((n_k - 1,)),
            dma((n_l - 1,)),
            dma((n_l - 1,)),
            dma((n_l - 1,)),
            dma((n_l - 1,)),
            dma((n_k - 1,)),
            dma((n_k - 1,)),
            dma((n_k,)),
            dma((n_k,)),
        ],
        compiler_params=pltpu.CompilerParams(
            collective_id=0, has_side_effects=True, vmem_limit_bytes=56 * 1024 * 1024
        ),
        name="block",
    )(
        fields,
        cotangent,
        bias_table,
        gain_one.reshape(1, C),
        w_qkv,
        w_proj,
        gain_two.reshape(1, C),
        w_in,
        w_out,
        jnp.asarray(placement_in(), BF16),
        jnp.asarray(placement_out(), BF16),
        jnp.asarray(spread_matrix(), BF16),
        jnp.asarray(region_masks(), F32),
        jnp.asarray(head_masks(), BF16),
    )
    outs = pl.pallas_call(
        functools.partial(finish_kernel, n_k),
        out_shape=(
            sds((4, 6, 24, C), BF16),
            sds((4, 6, 24, C), BF16),
            sds((1, C), F32),
            sds((C, 3 * C), F32),
            sds((1, 2, HEADS, POS), F32),
            sds((C, C), F32),
            sds((1, C), F32),
            sds((C, FFH), F32),
            sds((FFH, C), F32),
        ),
        in_specs=[whole] * 6,
        out_specs=[whole] * 9,
        scratch_shapes=[vmem((PACK, 256), F32)],
        compiler_params=pltpu.CompilerParams(vmem_limit_bytes=48 * 1024 * 1024),
        name="finish",
    )(*results, jnp.asarray(placement_end(), BF16))
    outs = list(outs)
    outs[2] = outs[2].reshape(C)
    outs[6] = outs[6].reshape(C)
    return tuple(outs)


def solution(mesh):
    n_k, n_l = mesh.shape["lon"] // 2, mesh.shape["lat"]
    placed = (
        P(None, "lat", "lon", None),
        P(None, "lat", "lon", None),
        P("lat", None, None, None),
    ) + (P(),) * 6
    return jax.shard_map(
        functools.partial(local, n_k, n_l),
        mesh=mesh,
        in_specs=placed,
        out_specs=(
            P(None, "lat", "lon", None),
            P(None, "lat", "lon", None),
            P(),
            P(),
            P("lat", None, None, None),
            P(),
            P(),
            P(),
            P(),
        ),
        check_vma=False,
    )
```

```python
import functools

import jax
import jax.numpy as jnp
import numpy as np
from jax import lax
from jax.experimental import pallas as pl
from jax.experimental.pallas import tpu as pltpu
from jax.sharding import PartitionSpec as P

HEADS = 6
C = 192
FFH = 768
TOK = 144
WIN = 4
ROWS = WIN * TOK
STACK = HEADS * TOK
POS = 3312
SEG = 138
EARLY = 1536
LATE = 768
TABLE = 256
EDGE = 80
MESH = pl.DeviceIdType.MESH
F32 = jnp.float32
BF16 = jnp.bfloat16


def window_row(lev, lat, col):
    return ((lev // 2) * 2 + col // 12) * TOK + (lev % 2) * 72 + lat * 12 + col % 12


def place_level_in():
    out = np.zeros((TOK, TOK), np.float32)
    for lat in range(6):
        for col in range(18):
            out[col // 12 * 72 + lat * 12 + col % 12, lat * 24 + col + 6] = 1
    return out


def edge_row(lev, lat, col):
    return (0 if lat < 3 else EDGE) + lev * 18 + lat % 3 * 6 + col


def place_edge_in():
    out = np.zeros((4, TOK, 2 * EDGE), np.float32)
    for lev in range(4):
        for lat in range(6):
            for col in range(6):
                out[lev, 72 + lat * 12 + 6 + col, edge_row((lev + 1) % 4, lat, col)] = 1
    return out


def pick_edge_in():
    out = np.zeros((2 * EDGE, ROWS), np.float32)
    for lev in range(4):
        for lat in range(6):
            for col in range(6):
                out[edge_row(lev, (lat + 3) % 6, col), (lev * 6 + lat) * 24 + col] = 1
    return out


def place_level_out():
    out = np.zeros((TOK, TOK), np.float32)
    for lat in range(6):
        for col in range(24):
            out[lat * 24 + col, col // 12 * 72 + lat * 12 + col % 12] = 1
    return out


def pick_edge_out():
    out = np.zeros((2 * EDGE, ROWS), np.float32)
    for lev in range(4):
        for lat in range(6):
            for col in range(6):
                out[edge_row(lev, lat, col), window_row(lev, lat, 18 + col)] = 1
    return out


def place_level_end():
    out = np.zeros((TOK, TOK), np.float32)
    for lat in range(6):
        for lon in range(6, 24):
            out[lat * 24 + lon, lat * 24 + lon - 6] = 1
    return out


def place_edge_end():
    out = np.zeros((4, TOK, 2 * EDGE), np.float32)
    for lev in range(4):
        for lat in range(6):
            for lon in range(6):
                out[lev, lat * 24 + lon, edge_row(lev, (lat + 3) % 6, lon)] = 1
    return out


def spread_matrix():
    out = np.zeros((512, 256), np.float32)
    for level in range(2):
        for lat in range(6):
            for col in range(12):
                out[level * 256 + lat * 23 + 11 - col, level * 72 + lat * 12 + col] = 1
    return out


def region_masks():
    ids = np.arange(TOK)
    level, lat = ids // 72, ids // 12 % 6 >= 3
    out = np.zeros((2, TOK, TOK), np.float32)
    out[0] = level[:, None] != level[None, :]
    out[1] = lat[:, None] != lat[None, :]
    return out


def head_masks():
    out = np.zeros((8, C), np.float32)
    for head in range(HEADS):
        out[head, head * 32 : head * 32 + 32] = 1
    return out


def mm(left, right):
    return lax.dot_general(left, right, (((1,), (0,)), ((), ())), preferred_element_type=F32)


def mm_nt(left, right):
    return lax.dot_general(left, right, (((1,), (1,)), ((), ())), preferred_element_type=F32)


def mm_tn(left, right):
    return lax.dot_general(left, right, (((0,), (0,)), ((), ())), preferred_element_type=F32)


def norm(values):
    center = values - jnp.mean(values, axis=-1, keepdims=True)
    spread = jnp.mean(center * center, axis=-1, keepdims=True)
    inverse = lax.rsqrt(spread + 1e-05)
    return center * inverse, inverse


def norm_grad(d_normed, gain, unit, inverse):
    d_unit = d_normed * gain
    mean_one = jnp.mean(d_unit, axis=-1, keepdims=True)
    mean_two = jnp.mean(d_unit * unit, axis=-1, keepdims=True)
    return inverse * (d_unit - mean_one - unit * mean_two)


def split_heads(value, heads):
    return jnp.concatenate([value * heads[h : h + 1, :] for h in range(HEADS)], axis=0)


def join_heads(stacked, heads):
    total = stacked[0:TOK, :] * heads[0:1, :]
    for h in range(1, HEADS):
        total = total + stacked[h * TOK : (h + 1) * TOK, :] * heads[h : h + 1, :]
    return total


def segment(cell, other):
    return ((2 * (cell // 6) + other) * 36 + 6 * (cell % 6)) * 23


def segment(cell, other):
    return ((2 * (cell // 6) + other) * 36 + 6 * (cell % 6)) * 23


def expand_bias(bias_ref, spread_ref, masks_ref, parts, flat, stage, bias, last):
    flat[...] = jnp.zeros_like(flat)
    for h in range(HEADS):
        flat[2 * h : 2 * h + 2, 0:POS] = bias_ref[0, h]
    for cell in range(12):
        for other in range(2):
            start = segment(cell, other)
            for half in range(2):
                parts[2 * other + half, pl.ds(cell, 12, stride=12), :] = flat[
                    0:12, start + half * 128 : start + half * 128 + 128
                ]
    for step in range(12):
        total = None
        for other in range(2):
            value = jnp.concatenate([parts[2 * other], parts[2 * other + 1]], axis=1)
            if step:
                value = pltpu.roll(value, 256 - step, 1)
            matrix = spread_ref[other * 256 : (other + 1) * 256, :].astype(BF16)
            for _ in range(3):
                part = value.astype(BF16)
                value = value - part.astype(F32)
                term = mm(part, matrix)
                total = term if total is None else total + term
        for half in range(2):
            stage[half, pl.ds(step, TOK, stride=12), :] = total[:, half * 128 : half * 128 + 128]
    for lev in range(2):
        closed = masks_ref[1] * last
        if lev == 1:
            closed = closed + masks_ref[0]
        for h in range(HEADS):
            rows = slice((2 * h + lev) * TOK, (2 * h + lev + 1) * TOK)
            value = jnp.concatenate([stage[0, rows, :], stage[1, rows, 0:16]], axis=1)
            bias[lev, h * TOK : (h + 1) * TOK, :] = jnp.where(closed > 0.5, -1000000000.0, value)


def reduce_table(d_bias, spread_ref, parts, flat, table):
    sums = [None, None]
    for step in range(12):
        value = jnp.concatenate(
            [d_bias[half, pl.ds(step, TOK, stride=12), :] for half in range(2)], axis=1
        )
        high = value.astype(BF16)
        low = (value - high.astype(F32)).astype(BF16)
        for other in range(2):
            matrix = spread_ref[other * 256 : (other + 1) * 256, :].astype(BF16)
            term = mm_nt(high, matrix) + mm_nt(low, matrix)
            if step:
                sums[other] = sums[other] + pltpu.roll(term, step, 1)
            else:
                sums[other] = term
    for other in range(2):
        for half in range(2):
            parts[2 * other + half] = sums[other][:, half * 128 : half * 128 + 128]
    flat[...] = jnp.zeros_like(flat)
    for cell in range(12):
        for other in range(2):
            start = segment(cell, other)
            rows = pl.ds(cell, 12, stride=12)
            flat[0:12, start : start + 128] = parts[2 * other, rows, :]
            flat[0:12, start + 128 : start + SEG] = parts[2 * other + 1, rows, :][:, 0 : SEG - 128]
    for part in range(16):
        table[part * 16 : (part + 1) * 16, :] = flat[:, part * 256 : (part + 1) * 256]


def gather_all(own, below, edges, place, place_edge, out):
    place = place[...].astype(BF16)
    for lev in range(4):
        source = (lev + 1) % 4
        parts = [
            own[source, 3:6].astype(F32).reshape(72, C),
            below[source].astype(F32).reshape(72, C),
        ]
        rows = mm(place, jnp.concatenate(parts, axis=0).astype(BF16))
        rows = rows + mm(place_edge[lev].astype(BF16), edges[...])
        for half in range(2):
            start = ((lev // 2) * 2 + half) * TOK + (lev % 2) * 72
            out[start : start + 72, :] = rows[half * 72 : (half + 1) * 72, :].astype(out.dtype)


def scatter_all(value, place, pick, own, full, edges):
    place = place[...].astype(BF16)
    for lev in range(4):
        parts = []
        for half in range(2):
            start = ((lev // 2) * 2 + half) * TOK + (lev % 2) * 72
            parts.append(value[start : start + 72, :])
        rows = mm(place, jnp.concatenate(parts, axis=0).astype(BF16))
        own[lev] = rows[0:72].reshape(3, 24, C).astype(BF16)
        full[lev] = rows[72:144].reshape(3, 24, C).astype(BF16)
    edges[...] = mm(pick[...].astype(BF16), value[...].astype(BF16)).astype(BF16)


INPUTS = (
    "fields",
    "cotangent",
    "bias_table",
    "gain_one",
    "w_qkv",
    "w_proj",
    "gain_two",
    "w_in",
    "w_out",
    "place_in",
    "edge_in",
    "pick_in",
    "place_out",
    "pick_out",
    "spread",
    "masks",
    "heads",
)


class Section:
    def __init__(self, net, chunk, rest, refs):
        self.net, self.chunk, self.rest = net, chunk, rest
        (
            self.pack,
            self.table,
            self.send_pair,
            self.recv_pair,
            self.send_lon,
            self.recv_lon,
            self.total,
            self.by_lat,
            self.gathered,
            self.sems,
        ) = refs
        self.pair, self.along_lon, self.along_lat = [], [], []

    def rows(self, ref, size, core, k):
        start = pl.multiple_of((2 * k + core) * size, size)
        return ref[pl.ds(start, size), :]

    def sem(self, stage, slot):
        return (self.sems.at[stage, slot], self.sems.at[stage + 1, slot])

    def to_pair(self):
        net = self.net
        for d in range(1, net.n_k + 1):
            k = lax.rem(net.k + d, net.n_k)
            self.send_pair[d - 1, 0 : self.chunk, :] = self.rows(
                self.pack, self.chunk, net.other, k
            ).astype(BF16)
            if self.rest:
                self.send_pair[d - 1, self.chunk : self.chunk + self.rest, :] = self.rows(
                    self.table, self.rest, net.other, k
                ).astype(BF16)
            self.pair.append(
                net.start(
                    self.send_pair.at[d - 1],
                    self.recv_pair.at[d - 1],
                    self.sem(0, d - 1),
                    net.partner,
                )
            )

    def to_lon(self):
        net = self.net
        for d in range(1, net.n_k + 1):
            k = lax.rem(net.k + d, net.n_k)
            self.pair[d - 1].wait_recv()
            value = self.rows(self.pack, self.chunk, net.core, k)
            if self.rest:
                value = jnp.concatenate(
                    [value, self.rows(self.table, self.rest, net.core, k)], axis=0
                )
            value = value + self.recv_pair[d - 1].astype(F32)
            if d == net.n_k:
                self.total[...] = value
                continue
            self.send_lon[d - 1] = value.astype(BF16)
            self.along_lon.append(
                net.start(
                    self.send_lon.at[d - 1],
                    self.recv_lon.at[d - 1],
                    self.sem(2, d - 1),
                    net.along_lon(d),
                )
            )

    def to_lat(self):
        net = self.net
        value = self.total[...]
        for d in range(1, net.n_k):
            self.along_lon[d - 1].wait_recv()
            value = value + self.recv_lon[d - 1].astype(F32)
        value = value.astype(BF16)
        mine = self.by_lat.at[net.lat]
        mine[...] = value[0 : self.chunk, :]
        if self.rest:
            self.gathered[net.core, net.k, self.chunk : self.chunk + self.rest, :] = value[
                self.chunk : self.chunk + self.rest, :
            ]
        for d in range(1, net.n_l):
            self.along_lat.append(net.start(mine, mine, self.sem(4, d - 1), net.along_lat(d)))

    def spread_lon(self):
        net = self.net
        for d in range(1, net.n_l):
            theirs = self.by_lat.at[lax.rem(net.lat - d + net.n_l, net.n_l)]
            net.copy(theirs, theirs, self.sem(4, d - 1), net.partner).wait_recv()
        value = self.by_lat[0].astype(F32)
        for i in range(1, net.n_l):
            value = value + self.by_lat[i].astype(F32)
        self.gathered[net.core, net.k, 0 : self.chunk, :] = value.astype(BF16)
        mine = self.gathered.at[net.core, net.k]
        for d in range(1, net.n_k):
            net.start(mine, mine, self.sem(6, d - 1), net.along_lon(d))
        net.start(mine, mine, self.sem(8, 0), net.partner)

    def spread_pair(self):
        net = self.net
        for d in range(1, net.n_k):
            theirs = self.gathered.at[net.core, lax.rem(net.k - d + net.n_k, net.n_k)]
            net.copy(theirs, theirs, self.sem(6, d - 1), net.partner).wait_recv()
            net.start(theirs, theirs, self.sem(8, d), net.partner)

    def close(self):
        net = self.net
        for d in range(net.n_k):
            theirs = self.gathered.at[net.other, lax.rem(net.k - d + net.n_k, net.n_k)]
            net.copy(theirs, theirs, self.sem(8, d), net.partner).wait_recv()


class Net:
    def __init__(self, n_k, n_l):
        self.n_k, self.n_l = n_k, n_l
        self.n_lon = 2 * n_k
        self.lon, self.lat = lax.axis_index("lon"), lax.axis_index("lat")
        self.core, self.k = lax.rem(self.lon, 2), self.lon // 2
        self.other = 1 - self.core
        self.partner = (2 * self.k + self.other, self.lat)
        self.started = []

    def at(self, d_lon, d_lat):
        return (
            lax.rem(self.lon + d_lon + self.n_lon, self.n_lon),
            lax.rem(self.lat + d_lat + self.n_l, self.n_l),
        )

    def along_lon(self, d):
        return (2 * lax.rem(self.k + d, self.n_k) + self.core, self.lat)

    def along_lat(self, d):
        return self.at(0, d)

    def greet(self):
        far = lax.rem(self.lon + 2 * self.core - 1 + self.n_lon, self.n_lon)
        friends = [self.partner, (far, self.lat), self.at(1, 1), self.at(-1, -1)]
        friends += [self.along_lon(d) for d in range(1, self.n_k)]
        friends += [self.along_lat(d) for d in range(1, self.n_l)]
        barrier = pltpu.get_barrier_semaphore()
        for friend in friends:
            pl.semaphore_signal(barrier, inc=1, device_id=friend, device_id_type=MESH)
        return barrier, len(friends)

    def copy(self, source, target, sems, device):
        return pltpu.make_async_remote_copy(
            src_ref=source,
            dst_ref=target,
            send_sem=sems[0],
            recv_sem=sems[1],
            device_id=device,
            device_id_type=MESH,
        )

    def start(self, source, target, sems, device):
        c = self.copy(source, target, sems, device)
        c.start()
        self.started.append(c)
        return c


def block_kernel(n_k, n_l, *refs):
    refs = list(refs)

    def take(count):
        out = refs[:count]
        del refs[:count]
        return out

    hbm = dict(zip(INPUTS, take(len(INPUTS)), strict=True))
    early_out, late_out, own_out, below_out, edge_out = take(5)
    here = dict(zip(INPUTS, take(len(INPUTS)), strict=True))
    below, edges, edges_send, full, edges_back = take(5)
    x_ref, cot_ref, n1_ref, q_ref, k_ref, v_ref, bias, probs, att_ref = take(9)
    act_ref, dpre_ref, n2_ref, dbb_ref, dbranch_ref, datt_ref, out_ref = take(7)
    dq_ref, dk_ref, dv_ref, d_bias, parts, stage, flat = take(7)
    early_pack, late_pack, table = take(3)
    early_bufs, late_bufs = take(6), take(6)
    load_sem, in_sem, out_sem, early_sem, late_sem = take(5)

    net = Net(n_k, n_l)
    barrier, count = net.greet()
    loads = {
        name: pltpu.make_async_copy(hbm[name], here[name], load_sem.at[i])
        for i, name in enumerate(INPUTS)
    }
    for name in INPUTS:
        loads[name].start()

    early = Section(net, EARLY // net.n_lon, 0, [early_pack, None, *early_bufs, early_out, early_sem])
    late = Section(
        net,
        LATE // net.n_lon,
        TABLE // net.n_lon,
        [late_pack, table, *late_bufs, late_out, late_sem],
    )

    def send_in(i, name):
        south = net.start(
            hbm[name].at[:, 0:3], below.at[i], (in_sem.at[0, i, 0], in_sem.at[1, i, 0]), net.at(0, -1)
        )
        flat_rows = here[name][...].astype(F32).reshape(ROWS, C).astype(BF16)
        edges_send[i] = mm(here["pick_in"][...].astype(BF16), flat_rows).astype(BF16)
        east = net.start(
            edges_send.at[i, 0:EDGE],
            edges.at[i, 0:EDGE],
            (in_sem.at[0, i, 1], in_sem.at[1, i, 1]),
            net.at(-1, 0),
        )
        corner = net.start(
            edges_send.at[i, EDGE : 2 * EDGE],
            edges.at[i, EDGE : 2 * EDGE],
            (in_sem.at[0, i, 2], in_sem.at[1, i, 2]),
            net.at(-1, -1),
        )
        return [south, east, corner]

    def send_out(i):
        return [
            net.start(
                full.at[i], below_out.at[i], (out_sem.at[0, i, 0], out_sem.at[1, i, 0]), net.at(0, 1)
            ),
            net.start(
                edges_back.at[i, 0:EDGE],
                edge_out.at[i, 0:EDGE],
                (out_sem.at[0, i, 1], out_sem.at[1, i, 1]),
                net.at(1, 0),
            ),
            net.start(
                edges_back.at[i, EDGE : 2 * EDGE],
                edge_out.at[i, EDGE : 2 * EDGE],
                (out_sem.at[0, i, 2], out_sem.at[1, i, 2]),
                net.at(1, 1),
            ),
        ]

    for name in INPUTS:
        loads[name].wait()
    pl.semaphore_wait(barrier, count)
    in_copies = [send_in(0, "fields")]

    last = (net.lat == n_l - 1).astype(F32)
    expand_bias(here["bias_table"], here["spread"], here["masks"], parts, flat, stage, bias, last)

    heads32 = here["heads"][...]
    heads = heads32.astype(BF16)
    scale = 32**-0.5
    gain1 = here["gain_one"][...]
    gain2 = here["gain_two"][...]
    w_qkv, w_proj, w_in, w_out = here["w_qkv"], here["w_proj"], here["w_in"], here["w_out"]

    for c in in_copies[0]:
        c.wait_recv()
    in_copies.append(send_in(1, "cotangent"))
    gather_all(here["fields"], below.at[0], edges.at[0], here["place_in"], here["edge_in"], x_ref)
    unit, _ = norm(x_ref[...])
    n1 = (unit * gain1).astype(BF16)
    n1_ref[...] = n1
    for i, ref in enumerate((q_ref, k_ref, v_ref)):
        ref[...] = mm(n1, w_qkv[:, i * C : (i + 1) * C]).astype(BF16)

    def attend(w, carry):
        rows = pl.ds(pl.multiple_of(w * TOK, TOK), TOK)
        stacked = split_heads(q_ref[rows, :], heads)
        scores = mm_nt(stacked, k_ref[rows, :]) * scale + bias[w // 2]
        top = jnp.max(scores, axis=-1, keepdims=True)
        exps = jnp.exp(scores - top)
        prob = exps * (1.0 / jnp.sum(exps, axis=-1, keepdims=True))
        probs[w] = prob
        mixed = mm(prob.astype(BF16), v_ref[rows, :])
        att_ref[rows, :] = join_heads(mixed, heads32).astype(BF16)
        return carry

    lax.fori_loop(0, WIN, attend, 0)

    for c in in_copies[1]:
        c.wait_recv()
    gather_all(
        here["cotangent"], below.at[1], edges.at[1], here["place_in"], here["edge_in"], cot_ref
    )
    half = ROWS // 2

    def feed(i, gain_sum):
        rows = pl.ds(pl.multiple_of(i * half, half), half)
        branch = x_ref[rows, :] + mm(att_ref[rows, :], w_proj[...])
        unit, inverse = norm(branch)
        n2 = (unit * gain2).astype(BF16)
        n2_ref[rows, :] = n2
        pre = mm(n2, w_in[...])
        cdf = 0.5 + 0.5 * lax.erf(pre * (0.5**0.5))
        slope = cdf + pre * (jnp.exp(-0.5 * pre * pre) * ((2.0 * np.pi) ** -0.5))
        act = (pre * cdf).astype(BF16)
        act_ref[rows, :] = act
        out_ref[rows, :] = branch + mm_nt(act, w_out[...])
        cot = cot_ref[rows, :]
        d_pre = (slope * mm(cot, w_out[...])).astype(BF16)
        dpre_ref[rows, :] = d_pre
        d_normed = mm_nt(d_pre, w_in[...])
        d_branch = cot.astype(F32) + norm_grad(d_normed, gain2, unit, inverse)
        dbranch_ref[rows, :] = d_branch
        dbb = d_branch.astype(BF16)
        dbb_ref[rows, :] = dbb
        datt_ref[rows, :] = mm_nt(dbb, w_proj[...]).astype(BF16)
        return gain_sum + jnp.sum(d_normed * unit, axis=0, keepdims=True)

    gain_sum2 = lax.fori_loop(0, 2, feed, jnp.zeros((1, C), F32))

    early_pack[1152:EARLY, 128:256] = jnp.zeros((EARLY - 1152, 128), F32)
    early_pack[1344:EARLY, 0:128] = jnp.zeros((EARLY - 1344, 128), F32)
    early_pack[1344:1345, 0:C] = gain_sum2
    for i in range(3):
        cols = slice(i * 256, (i + 1) * 256)
        early_pack[i * C : (i + 1) * C, :] = mm_tn(cot_ref[...], act_ref[:, cols])
        early_pack[576 + i * C : 576 + (i + 1) * C, :] = mm_tn(n2_ref[...], dpre_ref[:, cols])
    early_pack[1152 : 1152 + C, 0:C] = mm_tn(att_ref[...], dbb_ref[...])
    early.to_pair()
    scatter_all(
        out_ref, here["place_out"], here["pick_out"], own_out.at[0], full.at[0], edges_back.at[0]
    )
    out_copies = send_out(0)

    d_bias[...] = jnp.zeros_like(d_bias)

    def attend_back(w, carry):
        rows = pl.ds(pl.multiple_of(w * TOK, TOK), TOK)
        prob = probs[w]
        d_stacked = split_heads(datt_ref[rows, :], heads)
        d_prob = mm_nt(d_stacked, v_ref[rows, :])
        d_score = prob * (d_prob - jnp.sum(d_prob * prob, axis=-1, keepdims=True))
        for h in range(HEADS):
            group = pl.ds(pl.multiple_of((2 * h + w // 2) * TOK, TOK), TOK)
            part = d_score[h * TOK : (h + 1) * TOK, :]
            d_bias[0, group, :] += part[:, 0:128]
            d_bias[1, group, 0:16] += part[:, 128:144]
        d_score_b = d_score.astype(BF16)
        dv_ref[rows, :] = mm_tn(prob.astype(BF16), d_stacked).astype(BF16)
        dq_ref[rows, :] = (join_heads(mm(d_score_b, k_ref[rows, :]), heads32) * scale).astype(BF16)
        stacked = split_heads(q_ref[rows, :], heads)
        dk_ref[rows, :] = (mm_tn(d_score_b, stacked) * scale).astype(BF16)
        return carry

    lax.fori_loop(0, WIN // 2, attend_back, 0)
    early.to_lon()
    lax.fori_loop(WIN // 2, WIN, attend_back, 0)

    d_normed = None
    late_pack[:, 128:256] = jnp.zeros((LATE, 128), F32)
    late_pack[576:LATE, 0:128] = jnp.zeros((LATE - 576, 128), F32)
    for i, ref in enumerate((dq_ref, dk_ref, dv_ref)):
        late_pack[i * C : (i + 1) * C, 0:C] = mm_tn(n1_ref[...], ref[...])
        term = mm_nt(ref[...], w_qkv[:, i * C : (i + 1) * C])
        d_normed = term if d_normed is None else d_normed + term
    unit, inverse = norm(x_ref[...])
    late_pack[576:577, 0:C] = jnp.sum(d_normed * unit, axis=0, keepdims=True)
    out_ref[...] = dbranch_ref[...] + norm_grad(d_normed, gain1, unit, inverse)
    reduce_table(d_bias, here["spread"], parts, flat, table)
    late.to_pair()
    early.to_lat()
    late.to_lon()
    scatter_all(
        out_ref, here["place_out"], here["pick_out"], own_out.at[1], full.at[1], edges_back.at[1]
    )
    out_copies += send_out(1)
    early.spread_lon()
    late.to_lat()
    late.spread_lon()
    early.spread_pair()
    late.spread_pair()
    early.close()
    late.close()
    for c in out_copies:
        c.wait_recv()
    for c in net.started:
        c.wait_send()


def finish_kernel(
    n_k,
    early,
    late,
    own_out,
    below_out,
    edge_out,
    place_end,
    edge_end,
    block_out,
    grad_fields,
    g_gain_one,
    g_w_qkv,
    g_table,
    g_w_proj,
    g_gain_two,
    g_w_in,
    g_w_out,
    early_rows,
    late_rows,
):
    n_lon = 2 * n_k
    place = place_end[...].astype(BF16)
    for i, ref in enumerate((block_out, grad_fields)):
        for lev in range(4):
            parts = [
                below_out[i, lev].astype(F32).reshape(72, C),
                own_out[i, lev].astype(F32).reshape(72, C),
            ]
            rows = mm(place, jnp.concatenate(parts, axis=0).astype(BF16))
            rows = rows + mm(edge_end[lev].astype(BF16), edge_out[i])
            ref[(lev + 1) % 4] = rows.reshape(6, 24, C).astype(BF16)
    for source, target, size in ((early, early_rows, EARLY), (late, late_rows, LATE)):
        chunk = size // n_lon
        for part in range(n_lon):
            target[part * chunk : (part + 1) * chunk, :] = source[
                part % 2, part // 2, 0:chunk, :
            ].astype(F32)
    for i in range(3):
        cols = slice(i * 256, (i + 1) * 256)
        g_w_out[:, cols] = early_rows[i * C : (i + 1) * C, :]
        g_w_in[:, cols] = early_rows[576 + i * C : 576 + (i + 1) * C, :]
        g_w_qkv[:, i * C : (i + 1) * C] = late_rows[i * C : (i + 1) * C, 0:C]
    g_w_proj[...] = early_rows[1152 : 1152 + C, 0:C]
    g_gain_two[...] = early_rows[1344:1345, 0:C]
    g_gain_one[...] = late_rows[576:577, 0:C]
    rest, chunk = TABLE // n_lon, LATE // n_lon
    for part in range(13):
        width = min(256, POS - part * 256)
        place, offset = divmod(part * 16, rest)
        value = late[place % 2, place // 2, chunk + offset : chunk + offset + 16, :].astype(F32)
        for h in range(HEADS):
            g_table[0, h, :, part * 256 : part * 256 + width] = value[2 * h : 2 * h + 2, 0:width]


def local(n_k, n_l, fields, cotangent, bias_table, gain_one, w_qkv, w_proj, gain_two, w_in, w_out):
    n_lon = 2 * n_k
    sds = jax.ShapeDtypeStruct
    vmem = pltpu.VMEM
    dma = pltpu.SemaphoreType.DMA
    whole = pl.BlockSpec(memory_space=pltpu.VMEM)
    apart = pl.BlockSpec(memory_space=pl.ANY)
    early, late = EARLY // n_lon, LATE // n_lon
    both = late + TABLE // n_lon
    inputs = (
        fields,
        cotangent,
        bias_table.transpose(0, 2, 1, 3),
        gain_one.reshape(1, C),
        w_qkv,
        w_proj,
        gain_two.reshape(1, C),
        w_in,
        w_out.T,
        jnp.asarray(place_level_in()),
        jnp.asarray(place_edge_in()),
        jnp.asarray(pick_edge_in()),
        jnp.asarray(place_level_out()),
        jnp.asarray(pick_edge_out()),
        jnp.asarray(spread_matrix()),
        jnp.asarray(region_masks()),
        jnp.asarray(head_masks()),
    )

    def buffers(chunk, kept):
        return [
            vmem((n_k, chunk, 256), BF16),
            vmem((n_k, chunk, 256), BF16),
            vmem((n_k - 1, chunk, 256), BF16),
            vmem((n_k - 1, chunk, 256), BF16),
            vmem((chunk, 256), F32),
            vmem((n_l, kept, 256), BF16),
        ]

    slots = max(n_k, n_l)
    results = pl.pallas_call(
        functools.partial(block_kernel, n_k, n_l),
        out_shape=(
            sds((2, n_k, early, 256), BF16),
            sds((2, n_k, both, 256), BF16),
            sds((2, 4, 3, 24, C), BF16),
            sds((2, 4, 3, 24, C), BF16),
            sds((2, 2 * EDGE, C), BF16),
        ),
        in_specs=[apart] * len(INPUTS),
        out_specs=[whole] * 5,
        scratch_shapes=[vmem(value.shape, value.dtype) for value in inputs]
        + [
            vmem((2, 4, 3, 24, C), BF16),
            vmem((2, 2 * EDGE, C), BF16),
            vmem((2, 2 * EDGE, C), BF16),
            vmem((2, 4, 3, 24, C), BF16),
            vmem((2, 2 * EDGE, C), BF16),
            vmem((ROWS, C), F32),
            vmem((ROWS, C), BF16),
            vmem((ROWS, C), BF16),
            vmem((ROWS, C), BF16),
            vmem((ROWS, C), BF16),
            vmem((ROWS, C), BF16),
            vmem((2, STACK, TOK), F32),
            vmem((WIN, STACK, TOK), F32),
            vmem((ROWS, C), BF16),
            vmem((ROWS, FFH), BF16),
            vmem((ROWS, FFH), BF16),
            vmem((ROWS, C), BF16),
            vmem((ROWS, C), BF16),
            vmem((ROWS, C), F32),
            vmem((ROWS, C), BF16),
            vmem((ROWS, C), F32),
            vmem((ROWS, C), BF16),
            vmem((ROWS, C), BF16),
            vmem((ROWS, C), BF16),
            vmem((2, 2 * STACK, 128), F32),
            vmem((4, TOK, 128), F32),
            vmem((2, 2 * STACK, 128), F32),
            vmem((16, 4096), F32),
            vmem((EARLY, 256), F32),
            vmem((LATE, 256), F32),
            vmem((TABLE, 256), F32),
        ]
        + buffers(early, early)
        + buffers(both, late)
        + [
            dma((len(INPUTS),)),
            dma((2, 2, 3)),
            dma((2, 2, 3)),
            dma((10, slots)),
            dma((10, slots)),
        ],
        compiler_params=pltpu.CompilerParams(
            collective_id=0, has_side_effects=True, vmem_limit_bytes=60 * 1024 * 1024
        ),
        name="block",
    )(*inputs)
    outs = pl.pallas_call(
        functools.partial(finish_kernel, n_k),
        out_shape=(
            sds((4, 6, 24, C), BF16),
            sds((4, 6, 24, C), BF16),
            sds((1, C), F32),
            sds((C, 3 * C), F32),
            sds((1, HEADS, 2, POS), F32),
            sds((C, C), F32),
            sds((1, C), F32),
            sds((C, FFH), F32),
            sds((C, FFH), F32),
        ),
        in_specs=[whole] * 7,
        out_specs=[whole] * 9,
        scratch_shapes=[vmem((EARLY, 256), F32), vmem((LATE, 256), F32)],
        compiler_params=pltpu.CompilerParams(vmem_limit_bytes=60 * 1024 * 1024),
        name="finish",
    )(*results, jnp.asarray(place_level_end()), jnp.asarray(place_edge_end()))
    outs = list(outs)
    outs[2] = outs[2].reshape(C)
    outs[4] = outs[4].transpose(0, 2, 1, 3)
    outs[6] = outs[6].reshape(C)
    outs[8] = outs[8].T
    return tuple(outs)


def solution(mesh):
    n_k, n_l = mesh.shape["lon"] // 2, mesh.shape["lat"]
    placed = (
        P(None, "lat", "lon", None),
        P(None, "lat", "lon", None),
        P("lat", None, None, None),
    ) + (P(),) * 6
    return jax.shard_map(
        functools.partial(local, n_k, n_l),
        mesh=mesh,
        in_specs=placed,
        out_specs=(
            P(None, "lat", "lon", None),
            P(None, "lat", "lon", None),
            P(),
            P(),
            P("lat", None, None, None),
            P(),
            P(),
            P(),
            P(),
        ),
        check_vma=False,
    )
```

```python
import functools

import jax
import jax.numpy as jnp
import numpy as np
from jax import lax
from jax.experimental import pallas as pl
from jax.experimental.pallas import tpu as pltpu
from jax.sharding import PartitionSpec as P

HEADS = 6
C = 192
FFH = 768
TOK = 144
WIN = 4
ROWS = WIN * TOK
STACK = HEADS * TOK
POS = 3312
SEG = 138
EARLY = 1536
LATE = 512
TABLE = 256
EDGE = 80
MESH = pl.DeviceIdType.MESH
F32 = jnp.float32
BF16 = jnp.bfloat16


def window_row(lev, lat, col):
    return ((lev // 2) * 2 + col // 12) * TOK + (lev % 2) * 72 + lat * 12 + col % 12


def place_level_in():
    out = np.zeros((TOK, TOK), np.float32)
    for lat in range(6):
        for col in range(18):
            out[col // 12 * 72 + lat * 12 + col % 12, lat * 24 + col + 6] = 1
    return out


def edge_row(lev, lat, col):
    return (0 if lat < 3 else EDGE) + lev * 18 + lat % 3 * 6 + col


def place_edge_in():
    out = np.zeros((4, TOK, 2 * EDGE), np.float32)
    for lev in range(4):
        for lat in range(6):
            for col in range(6):
                out[lev, 72 + lat * 12 + 6 + col, edge_row((lev + 1) % 4, lat, col)] = 1
    return out


def pick_edge_in():
    out = np.zeros((2 * EDGE, ROWS), np.float32)
    for lev in range(4):
        for lat in range(6):
            for col in range(6):
                out[edge_row(lev, (lat + 3) % 6, col), (lev * 6 + lat) * 24 + col] = 1
    return out


def place_level_out():
    out = np.zeros((TOK, TOK), np.float32)
    for lat in range(6):
        for col in range(24):
            out[lat * 24 + col, col // 12 * 72 + lat * 12 + col % 12] = 1
    return out


def pick_edge_out():
    out = np.zeros((2 * EDGE, ROWS), np.float32)
    for lev in range(4):
        for lat in range(6):
            for col in range(6):
                out[edge_row(lev, lat, col), window_row(lev, lat, 18 + col)] = 1
    return out


def place_level_end():
    out = np.zeros((TOK, TOK), np.float32)
    for lat in range(6):
        for lon in range(6, 24):
            out[lat * 24 + lon, lat * 24 + lon - 6] = 1
    return out


def place_edge_end():
    out = np.zeros((4, TOK, 2 * EDGE), np.float32)
    for lev in range(4):
        for lat in range(6):
            for lon in range(6):
                out[lev, lat * 24 + lon, edge_row(lev, (lat + 3) % 6, lon)] = 1
    return out


def spread_matrix():
    out = np.zeros((512, 256), np.float32)
    for level in range(2):
        for lat in range(6):
            for col in range(12):
                out[level * 256 + lat * 23 + 11 - col, level * 72 + lat * 12 + col] = 1
    return out


def region_masks():
    ids = np.arange(TOK)
    level, lat = ids // 72, ids // 12 % 6 >= 3
    out = np.zeros((2, TOK, TOK), np.float32)
    out[0] = level[:, None] != level[None, :]
    out[1] = lat[:, None] != lat[None, :]
    return out


def head_masks():
    out = np.zeros((8, C), np.float32)
    for head in range(HEADS):
        out[head, head * 32 : head * 32 + 32] = 1
    return out


def mm(left, right):
    return lax.dot_general(left, right, (((1,), (0,)), ((), ())), preferred_element_type=F32)


def mm_nt(left, right):
    return lax.dot_general(left, right, (((1,), (1,)), ((), ())), preferred_element_type=F32)


def mm_tn(left, right):
    return lax.dot_general(left, right, (((0,), (0,)), ((), ())), preferred_element_type=F32)


def norm(values):
    center = values - jnp.mean(values, axis=-1, keepdims=True)
    spread = jnp.mean(center * center, axis=-1, keepdims=True)
    inverse = lax.rsqrt(spread + 1e-05)
    return center * inverse, inverse


def norm_grad(d_normed, gain, unit, inverse):
    d_unit = d_normed * gain
    mean_one = jnp.mean(d_unit, axis=-1, keepdims=True)
    mean_two = jnp.mean(d_unit * unit, axis=-1, keepdims=True)
    return inverse * (d_unit - mean_one - unit * mean_two)


def split_heads(value, heads):
    return jnp.concatenate([value * heads[h : h + 1, :] for h in range(HEADS)], axis=0)


def join_heads(stacked, heads):
    total = stacked[0:TOK, :] * heads[0:1, :]
    for h in range(1, HEADS):
        total = total + stacked[h * TOK : (h + 1) * TOK, :] * heads[h : h + 1, :]
    return total


def segment(cell, other):
    return ((2 * (cell // 6) + other) * 36 + 6 * (cell % 6)) * 23


def segment(cell, other):
    return ((2 * (cell // 6) + other) * 36 + 6 * (cell % 6)) * 23


def expand_bias(bias_ref, spread_ref, masks_ref, parts, flat, stage, bias, last):
    flat[...] = jnp.zeros_like(flat)
    for h in range(HEADS):
        flat[2 * h : 2 * h + 2, 0:POS] = bias_ref[0, h]
    for cell in range(12):
        for other in range(2):
            start = segment(cell, other)
            for half in range(2):
                parts[2 * other + half, pl.ds(cell, 12, stride=12), :] = flat[
                    0:12, start + half * 128 : start + half * 128 + 128
                ]
    for step in range(12):
        total = None
        for other in range(2):
            value = jnp.concatenate([parts[2 * other], parts[2 * other + 1]], axis=1)
            if step:
                value = pltpu.roll(value, 256 - step, 1)
            matrix = spread_ref[other * 256 : (other + 1) * 256, :].astype(BF16)
            for _ in range(3):
                part = value.astype(BF16)
                value = value - part.astype(F32)
                term = mm(part, matrix)
                total = term if total is None else total + term
        for half in range(2):
            stage[half, pl.ds(step, TOK, stride=12), :] = total[:, half * 128 : half * 128 + 128]
    for lev in range(2):
        closed = masks_ref[1] * last
        if lev == 1:
            closed = closed + masks_ref[0]
        for h in range(HEADS):
            rows = slice((2 * h + lev) * TOK, (2 * h + lev + 1) * TOK)
            value = jnp.concatenate([stage[0, rows, :], stage[1, rows, 0:16]], axis=1)
            bias[lev, h * TOK : (h + 1) * TOK, :] = jnp.where(closed > 0.5, -1000000000.0, value)


def reduce_table(d_bias, spread_ref, parts, flat, table):
    value = jnp.concatenate(
        [
            jnp.concatenate(
                [d_bias[half, pl.ds(step, TOK, stride=12), :] for half in range(2)], axis=1
            )
            for step in range(12)
        ],
        axis=0,
    ).astype(BF16)
    sums = []
    for other in range(2):
        terms = mm_nt(value, spread_ref[other * 256 : (other + 1) * 256, :].astype(BF16))
        total = terms[0:TOK, :]
        for step in range(1, 12):
            total = total + pltpu.roll(terms[step * TOK : (step + 1) * TOK, :], step, 1)
        sums.append(total)
    for other in range(2):
        for half in range(2):
            parts[2 * other + half] = sums[other][:, half * 128 : half * 128 + 128]
    flat[...] = jnp.zeros_like(flat)
    for cell in range(12):
        for other in range(2):
            start = segment(cell, other)
            rows = pl.ds(cell, 12, stride=12)
            flat[0:12, start : start + 128] = parts[2 * other, rows, :]
            flat[0:12, start + 128 : start + SEG] = parts[2 * other + 1, rows, :][:, 0 : SEG - 128]
    for part in range(16):
        table[part * 16 : (part + 1) * 16, :] = flat[:, part * 256 : (part + 1) * 256]


def gather_all(own, below, edges, place, place_edge, out):
    place = place[...].astype(BF16)
    for lev in range(4):
        source = (lev + 1) % 4
        parts = [
            own[source, 3:6].astype(F32).reshape(72, C),
            below[source].astype(F32).reshape(72, C),
        ]
        rows = mm(place, jnp.concatenate(parts, axis=0).astype(BF16))
        rows = rows + mm(place_edge[lev].astype(BF16), edges[...])
        for half in range(2):
            start = ((lev // 2) * 2 + half) * TOK + (lev % 2) * 72
            out[start : start + 72, :] = rows[half * 72 : (half + 1) * 72, :].astype(out.dtype)


def scatter_all(value, place, pick, own, full, edges):
    place = place[...].astype(BF16)
    for lev in range(4):
        parts = []
        for half in range(2):
            start = ((lev // 2) * 2 + half) * TOK + (lev % 2) * 72
            parts.append(value[start : start + 72, :])
        rows = mm(place, jnp.concatenate(parts, axis=0).astype(BF16))
        own[lev] = rows[0:72].reshape(3, 24, C).astype(BF16)
        full[lev] = rows[72:144].reshape(3, 24, C).astype(BF16)
    edges[...] = mm(pick[...].astype(BF16), value[...].astype(BF16)).astype(BF16)


INPUTS = (
    "fields",
    "cotangent",
    "bias_table",
    "gain_one",
    "w_qkv",
    "w_proj",
    "gain_two",
    "w_in",
    "w_out",
    "place_in",
    "edge_in",
    "pick_in",
    "place_out",
    "pick_out",
    "spread",
    "masks",
    "heads",
)


class Section:
    def __init__(self, net, chunk, rest, refs):
        self.net, self.chunk, self.rest = net, chunk, rest
        (
            self.pack,
            self.table,
            self.send_pair,
            self.recv_pair,
            self.send_lon,
            self.recv_lon,
            self.total,
            self.by_lat,
            self.send_lat,
            self.gathered,
            self.sems,
        ) = refs
        self.pair, self.along_lon = [], []

    def rows(self, ref, size, core, k):
        start = pl.multiple_of((2 * k + core) * size, size)
        return ref[pl.ds(start, size), :]

    def sem(self, stage, slot):
        return (self.sems.at[stage, slot], self.sems.at[stage + 1, slot])

    def to_pair(self):
        net = self.net
        for d in range(1, net.n_k + 1):
            k = lax.rem(net.k + d, net.n_k)
            self.send_pair[d - 1, 0 : self.chunk, :] = self.rows(
                self.pack, self.chunk, net.other, k
            ).astype(BF16)
            if self.rest:
                self.send_pair[d - 1, self.chunk : self.chunk + self.rest, :] = self.rows(
                    self.table, self.rest, net.other, k
                ).astype(BF16)
            self.pair.append(
                net.start(
                    self.send_pair.at[d - 1],
                    self.recv_pair.at[d - 1],
                    self.sem(0, d - 1),
                    net.partner,
                )
            )

    def to_lon(self):
        net = self.net
        for d in range(1, net.n_k + 1):
            k = lax.rem(net.k + d, net.n_k)
            self.pair[d - 1].wait_recv()
            value = self.rows(self.pack, self.chunk, net.core, k)
            if self.rest:
                value = jnp.concatenate(
                    [value, self.rows(self.table, self.rest, net.core, k)], axis=0
                )
            value = value + self.recv_pair[d - 1].astype(F32)
            if d == net.n_k:
                self.total[...] = value
                continue
            self.send_lon[d - 1] = value.astype(BF16)
            self.along_lon.append(
                net.start(
                    self.send_lon.at[d - 1],
                    self.recv_lon.at[d - 1],
                    self.sem(2, d - 1),
                    net.along_lon(d),
                )
            )

    def sum_lon(self):
        value = self.total[...]
        for d in range(1, self.net.n_k):
            self.along_lon[d - 1].wait_recv()
            value = value + self.recv_lon[d - 1].astype(F32)
        return value.astype(BF16)

    def sum_lat(self):
        value = self.by_lat[0].astype(F32)
        for i in range(1, self.net.n_l):
            value = value + self.by_lat[i].astype(F32)
        return value.astype(BF16)

    def spread_lon(self):
        net = self.net
        mine = self.gathered.at[net.core, net.k]
        for d in range(1, net.n_k):
            net.start(mine, mine, self.sem(8, d - 1), net.along_lon(d))
        net.start(mine, mine, self.sem(10, 0), net.partner)

    def to_lat(self):
        net = self.net
        value = self.sum_lon()
        mine = self.by_lat.at[net.lat]
        mine[...] = value[0 : self.chunk, :]
        self.gathered[net.core, net.k, self.chunk : self.chunk + self.rest, :] = value[
            self.chunk : self.chunk + self.rest, :
        ]
        for d in range(1, net.n_l):
            net.start(mine, mine, self.sem(4, d - 1), net.along_lat(d))

    def from_lat(self):
        net = self.net
        for d in range(1, net.n_l):
            theirs = self.by_lat.at[lax.rem(net.lat - d + net.n_l, net.n_l)]
            net.copy(theirs, theirs, self.sem(4, d - 1), net.partner).wait_recv()
        self.gathered[net.core, net.k, 0 : self.chunk, :] = self.sum_lat()
        self.spread_lon()

    def to_owner(self, pieces):
        net = self.net
        value = self.sum_lon()
        for p in range(pieces):
            pieces_ref = self.send_lat.at[p]
            pieces_ref[...] = value[p * 16 : (p + 1) * 16, :]

            @pl.when(net.lat != p)
            def _(p=p):
                self.owner_copy(p).start()

    def owner_copy(self, p):
        net = self.net
        sems = (self.sems.at[4, p], self.sems.at[5, net.lat])
        return net.copy(self.send_lat.at[p], self.by_lat.at[net.lat], sems, (net.lon, p))

    def own_piece(self):
        net = self.net
        return self.gathered.at[net.core, net.k, pl.ds(pl.multiple_of(net.lat * 16, 16), 16), :]

    def back_copy(self, d):
        net = self.net
        sems = (self.sems.at[6, d - 1], self.sems.at[7, net.lat])
        return net.copy(self.own_piece(), self.own_piece(), sems, net.along_lat(d))

    def from_owner(self, pieces):
        net = self.net

        @pl.when(net.lat < pieces)
        def _():
            self.by_lat[net.lat] = self.send_lat[net.lat]
            for d in range(1, net.n_l):
                source = lax.rem(net.lat + d, net.n_l)
                theirs = self.by_lat.at[source]
                sems = (self.sems.at[4, 0], self.sems.at[5, source])
                net.copy(theirs, theirs, sems, net.partner).wait_recv()
            self.own_piece()[...] = self.sum_lat()
            for d in range(1, net.n_l):
                self.back_copy(d).start()

    def after_owner(self, pieces):
        net = self.net
        for p in range(pieces):

            @pl.when(net.lat != p)
            def _(p=p):
                theirs = self.gathered.at[net.core, net.k, p * 16 : (p + 1) * 16, :]
                sems = (self.sems.at[6, 0], self.sems.at[7, p])
                net.copy(theirs, theirs, sems, net.partner).wait_recv()

        self.spread_lon()

    def close_owner(self, pieces):
        net = self.net
        for p in range(pieces):

            @pl.when(net.lat != p)
            def _(p=p):
                self.owner_copy(p).wait_send()

        @pl.when(net.lat < pieces)
        def _():
            for d in range(1, net.n_l):
                self.back_copy(d).wait_send()

    def spread_pair(self):
        net = self.net
        for d in range(1, net.n_k):
            theirs = self.gathered.at[net.core, lax.rem(net.k - d + net.n_k, net.n_k)]
            net.copy(theirs, theirs, self.sem(8, d - 1), net.partner).wait_recv()
            net.start(theirs, theirs, self.sem(10, d), net.partner)

    def close(self):
        net = self.net
        for d in range(net.n_k):
            theirs = self.gathered.at[net.other, lax.rem(net.k - d + net.n_k, net.n_k)]
            net.copy(theirs, theirs, self.sem(10, d), net.partner).wait_recv()


class Net:
    def __init__(self, n_k, n_l):
        self.n_k, self.n_l = n_k, n_l
        self.n_lon = 2 * n_k
        self.lon, self.lat = lax.axis_index("lon"), lax.axis_index("lat")
        self.core, self.k = lax.rem(self.lon, 2), self.lon // 2
        self.other = 1 - self.core
        self.partner = (2 * self.k + self.other, self.lat)
        self.started = []

    def at(self, d_lon, d_lat):
        return (
            lax.rem(self.lon + d_lon + self.n_lon, self.n_lon),
            lax.rem(self.lat + d_lat + self.n_l, self.n_l),
        )

    def along_lon(self, d):
        return (2 * lax.rem(self.k + d, self.n_k) + self.core, self.lat)

    def along_lat(self, d):
        return self.at(0, d)

    def greet(self):
        far = lax.rem(self.lon + 2 * self.core - 1 + self.n_lon, self.n_lon)
        friends = [self.partner, (far, self.lat), self.at(1, 1), self.at(-1, -1)]
        friends += [self.along_lon(d) for d in range(1, self.n_k)]
        friends += [self.along_lat(d) for d in range(1, self.n_l)]
        barrier = pltpu.get_barrier_semaphore()
        for friend in friends:
            pl.semaphore_signal(barrier, inc=1, device_id=friend, device_id_type=MESH)
        return barrier, len(friends)

    def copy(self, source, target, sems, device):
        return pltpu.make_async_remote_copy(
            src_ref=source,
            dst_ref=target,
            send_sem=sems[0],
            recv_sem=sems[1],
            device_id=device,
            device_id_type=MESH,
        )

    def start(self, source, target, sems, device):
        c = self.copy(source, target, sems, device)
        c.start()
        self.started.append(c)
        return c


def block_kernel(n_k, n_l, *refs):
    refs = list(refs)

    def take(count):
        out = refs[:count]
        del refs[:count]
        return out

    hbm = dict(zip(INPUTS, take(len(INPUTS)), strict=True))
    early_out, late_out, own_out, below_out, edge_out = take(5)
    here = dict(zip(INPUTS, take(len(INPUTS)), strict=True))
    below, edges, edges_send, full, edges_back = take(5)
    x_ref, cot_ref, n1_ref, q_ref, k_ref, v_ref, bias, probs, att_ref = take(9)
    act_ref, dpre_ref, n2_ref, dbb_ref, dbranch_ref, datt_ref, out_ref = take(7)
    dq_ref, dk_ref, dv_ref, d_bias, parts, stage, flat = take(7)
    early_pack, late_pack, table = take(3)
    early_bufs, late_bufs = take(7), take(7)
    load_sem, in_sem, out_sem, early_sem, late_sem = take(5)

    net = Net(n_k, n_l)
    barrier, count = net.greet()
    loads = {
        name: pltpu.make_async_copy(hbm[name], here[name], load_sem.at[i])
        for i, name in enumerate(INPUTS)
    }
    for name in INPUTS:
        loads[name].start()

    early = Section(net, EARLY // net.n_lon, 0, [early_pack, None, *early_bufs, early_out, early_sem])
    late = Section(
        net,
        LATE // net.n_lon,
        TABLE // net.n_lon,
        [late_pack, table, *late_bufs, late_out, late_sem],
    )

    def send_in(i, name):
        south = net.start(
            hbm[name].at[:, 0:3], below.at[i], (in_sem.at[0, i, 0], in_sem.at[1, i, 0]), net.at(0, -1)
        )
        if i == 0:
            loads["fields"].wait()
            loads["pick_in"].wait()
        flat_rows = here[name][...].astype(F32).reshape(ROWS, C).astype(BF16)
        edges_send[i] = mm(here["pick_in"][...].astype(BF16), flat_rows).astype(BF16)
        east = net.start(
            edges_send.at[i, 0:EDGE],
            edges.at[i, 0:EDGE],
            (in_sem.at[0, i, 1], in_sem.at[1, i, 1]),
            net.at(-1, 0),
        )
        corner = net.start(
            edges_send.at[i, EDGE : 2 * EDGE],
            edges.at[i, EDGE : 2 * EDGE],
            (in_sem.at[0, i, 2], in_sem.at[1, i, 2]),
            net.at(-1, -1),
        )
        return [south, east, corner]

    def send_out(i):
        return [
            net.start(
                full.at[i], below_out.at[i], (out_sem.at[0, i, 0], out_sem.at[1, i, 0]), net.at(0, 1)
            ),
            net.start(
                edges_back.at[i, 0:EDGE],
                edge_out.at[i, 0:EDGE],
                (out_sem.at[0, i, 1], out_sem.at[1, i, 1]),
                net.at(1, 0),
            ),
            net.start(
                edges_back.at[i, EDGE : 2 * EDGE],
                edge_out.at[i, EDGE : 2 * EDGE],
                (out_sem.at[0, i, 2], out_sem.at[1, i, 2]),
                net.at(1, 1),
            ),
        ]

    pl.semaphore_wait(barrier, count)
    in_copies = [send_in(0, "fields")]
    for name in INPUTS:
        if name not in ("fields", "pick_in"):
            loads[name].wait()

    last = (net.lat == n_l - 1).astype(F32)
    expand_bias(here["bias_table"], here["spread"], here["masks"], parts, flat, stage, bias, last)

    heads32 = here["heads"][...]
    heads = heads32.astype(BF16)
    scale = 32**-0.5
    gain1 = here["gain_one"][...]
    gain2 = here["gain_two"][...]
    w_qkv, w_proj, w_in, w_out = here["w_qkv"], here["w_proj"], here["w_in"], here["w_out"]

    for c in in_copies[0]:
        c.wait_recv()
    in_copies.append(send_in(1, "cotangent"))
    gather_all(here["fields"], below.at[0], edges.at[0], here["place_in"], here["edge_in"], x_ref)
    unit, _ = norm(x_ref[...])
    n1 = (unit * gain1).astype(BF16)
    n1_ref[...] = n1
    for i, ref in enumerate((q_ref, k_ref, v_ref)):
        ref[...] = mm(n1, w_qkv[:, i * C : (i + 1) * C]).astype(BF16)

    def attend(w, carry):
        rows = pl.ds(pl.multiple_of(w * TOK, TOK), TOK)
        stacked = split_heads(q_ref[rows, :], heads)
        scores = mm_nt(stacked, k_ref[rows, :]) * scale + bias[w // 2]
        top = jnp.max(scores, axis=-1, keepdims=True)
        exps = jnp.exp(scores - top)
        prob = exps * (1.0 / jnp.sum(exps, axis=-1, keepdims=True))
        probs[w] = prob
        mixed = mm(prob.astype(BF16), v_ref[rows, :])
        att_ref[rows, :] = join_heads(mixed, heads32).astype(BF16)
        return carry

    lax.fori_loop(0, WIN, attend, 0, unroll=True)

    for c in in_copies[1]:
        c.wait_recv()
    gather_all(
        here["cotangent"], below.at[1], edges.at[1], here["place_in"], here["edge_in"], cot_ref
    )
    half = ROWS // 2

    def feed(i, gain_sum):
        rows = pl.ds(pl.multiple_of(i * half, half), half)
        branch = x_ref[rows, :] + mm(att_ref[rows, :], w_proj[...])
        unit, inverse = norm(branch)
        n2 = (unit * gain2).astype(BF16)
        n2_ref[rows, :] = n2
        pre = mm(n2, w_in[...])
        cdf = 0.5 + 0.5 * lax.erf(pre * (0.5**0.5))
        slope = cdf + pre * (jnp.exp(-0.5 * pre * pre) * ((2.0 * np.pi) ** -0.5))
        act = (pre * cdf).astype(BF16)
        act_ref[rows, :] = act
        out_ref[rows, :] = branch + mm_nt(act, w_out[...])
        cot = cot_ref[rows, :]
        d_pre = (slope * mm(cot, w_out[...])).astype(BF16)
        dpre_ref[rows, :] = d_pre
        d_normed = mm_nt(d_pre, w_in[...])
        d_branch = cot.astype(F32) + norm_grad(d_normed, gain2, unit, inverse)
        dbranch_ref[rows, :] = d_branch
        dbb = d_branch.astype(BF16)
        dbb_ref[rows, :] = dbb
        datt_ref[rows, :] = mm_nt(dbb, w_proj[...]).astype(BF16)
        return gain_sum + jnp.sum(d_normed * unit, axis=0, keepdims=True)

    gain_sum2 = lax.fori_loop(0, 2, feed, jnp.zeros((1, C), F32), unroll=True)

    early_pack[1152:EARLY, 128:256] = jnp.zeros((EARLY - 1152, 128), F32)
    early_pack[1344:EARLY, 0:128] = jnp.zeros((EARLY - 1344, 128), F32)
    early_pack[1344:1345, 0:C] = gain_sum2
    for i in range(3):
        cols = slice(i * 256, (i + 1) * 256)
        early_pack[i * C : (i + 1) * C, :] = mm_tn(cot_ref[...], act_ref[:, cols])
        early_pack[576 + i * C : 576 + (i + 1) * C, :] = mm_tn(n2_ref[...], dpre_ref[:, cols])
    early_pack[1152 : 1152 + C, 0:C] = mm_tn(att_ref[...], dbb_ref[...])
    early.to_pair()
    scatter_all(
        out_ref, here["place_out"], here["pick_out"], own_out.at[0], full.at[0], edges_back.at[0]
    )
    out_copies = send_out(0)

    early.to_lon()
    d_bias[...] = jnp.zeros_like(d_bias)

    def attend_back(w, carry):
        rows = pl.ds(pl.multiple_of(w * TOK, TOK), TOK)
        prob = probs[w]
        d_stacked = split_heads(datt_ref[rows, :], heads)
        d_prob = mm_nt(d_stacked, v_ref[rows, :])
        d_score = prob * (d_prob - jnp.sum(d_prob * prob, axis=-1, keepdims=True))
        for h in range(HEADS):
            group = pl.ds(pl.multiple_of((2 * h + w // 2) * TOK, TOK), TOK)
            part = d_score[h * TOK : (h + 1) * TOK, :]
            d_bias[0, group, :] += part[:, 0:128]
            d_bias[1, group, 0:16] += part[:, 128:144]
        d_score_b = d_score.astype(BF16)
        dv_ref[rows, :] = mm_tn(prob.astype(BF16), d_stacked).astype(BF16)
        dq_ref[rows, :] = (join_heads(mm(d_score_b, k_ref[rows, :]), heads32) * scale).astype(BF16)
        stacked = split_heads(q_ref[rows, :], heads)
        dk_ref[rows, :] = (mm_tn(d_score_b, stacked) * scale).astype(BF16)
        return carry

    lax.fori_loop(0, WIN, attend_back, 0, unroll=2)
    pieces = EARLY // net.n_lon // 16
    early.to_owner(pieces)

    d_normed = None
    late_pack[432:LATE, :] = jnp.zeros((LATE - 432, 256), F32)
    for i, ref in enumerate((dq_ref, dk_ref, dv_ref)):
        grad = mm_tn(n1_ref[...], ref[...])
        late_pack[i * TOK : (i + 1) * TOK, 0:C] = grad[0:TOK, :]
        for j in range(3):
            rows = slice(i * TOK + j * 48, i * TOK + (j + 1) * 48)
            late_pack[rows, C:256] = grad[TOK:C, j * 64 : (j + 1) * 64]
        term = mm_nt(ref[...], w_qkv[:, i * C : (i + 1) * C])
        d_normed = term if d_normed is None else d_normed + term
    unit, inverse = norm(x_ref[...])
    late_pack[432:433, 0:C] = jnp.sum(d_normed * unit, axis=0, keepdims=True)
    out_ref[...] = dbranch_ref[...] + norm_grad(d_normed, gain1, unit, inverse)
    reduce_table(d_bias, here["spread"], parts, flat, table)
    late.to_pair()
    early.from_owner(pieces)
    late.to_lon()
    scatter_all(
        out_ref, here["place_out"], here["pick_out"], own_out.at[1], full.at[1], edges_back.at[1]
    )
    out_copies += send_out(1)
    early.after_owner(pieces)
    late.to_lat()
    late.from_lat()
    early.spread_pair()
    late.spread_pair()
    early.close()
    late.close()
    early.close_owner(pieces)
    for c in out_copies:
        c.wait_recv()
    for c in net.started:
        c.wait_send()


def finish_kernel(n_k, *refs):
    hbm, outs, here = refs[0:7], refs[7:16], refs[16:23]
    early_rows, late_rows = refs[23:25]
    results = refs[25:34]
    load_sem, store_sem = refs[34:36]
    loads = [pltpu.make_async_copy(hbm[i], here[i], load_sem.at[i]) for i in range(7)]
    for c in loads:
        c.start()
    early, late, own_out, below_out, edge_out, place_end, edge_end = here
    block_out, grad_fields, g_gain_one, g_w_qkv, g_table, g_w_proj, g_gain_two, _, _ = results
    out_w_in, out_w_out = outs[7], outs[8]
    stores = []

    def store(source, target):
        c = pltpu.make_async_copy(source, target, store_sem.at[len(stores)])
        c.start()
        stores.append(c)

    n_lon = 2 * n_k
    chunk = EARLY // n_lon
    loads[0].wait()
    for part in range(n_lon):
        early_rows[part * chunk : (part + 1) * chunk, :] = early[part % 2, part // 2].astype(F32)
    for i in range(3):
        cols = slice(i * 256, (i + 1) * 256)
        store(early_rows.at[i * C : (i + 1) * C, :], out_w_out.at[:, cols])
        store(early_rows.at[576 + i * C : 576 + (i + 1) * C, :], out_w_in.at[:, cols])
    g_w_proj[...] = early_rows[1152 : 1152 + C, 0:C]
    store(g_w_proj, outs[5])
    g_gain_two[...] = early_rows[1344:1345, 0:C]
    store(g_gain_two, outs[6])
    for c in loads[2:]:
        c.wait()
    place = place_end[...].astype(BF16)
    for i, ref in enumerate((block_out, grad_fields)):
        for lev in range(4):
            parts = [
                below_out[i, lev].astype(F32).reshape(72, C),
                own_out[i, lev].astype(F32).reshape(72, C),
            ]
            rows = mm(place, jnp.concatenate(parts, axis=0).astype(BF16))
            rows = rows + mm(edge_end[lev].astype(BF16), edge_out[i])
            ref[(lev + 1) % 4] = rows.reshape(6, 24, C).astype(BF16)
        store(ref, outs[i])
    loads[1].wait()
    rest, chunk = TABLE // n_lon, LATE // n_lon
    for part in range(n_lon):
        late_rows[part * chunk : (part + 1) * chunk, :] = late[
            part % 2, part // 2, 0:chunk, :
        ].astype(F32)
    for i in range(3):
        g_w_qkv[0:TOK, i * C : (i + 1) * C] = late_rows[i * TOK : (i + 1) * TOK, 0:C]
        for j in range(3):
            cols = slice(i * C + j * 64, i * C + (j + 1) * 64)
            g_w_qkv[TOK:C, cols] = late_rows[i * TOK + j * 48 : i * TOK + (j + 1) * 48, C:256]
    store(g_w_qkv, outs[3])
    g_gain_one[...] = late_rows[432:433, 0:C]
    store(g_gain_one, outs[2])
    for part in range(13):
        width = min(256, POS - part * 256)
        place, offset = divmod(part * 16, rest)
        value = late[place % 2, place // 2, chunk + offset : chunk + offset + 16, :].astype(F32)
        for h in range(HEADS):
            g_table[0, h, :, part * 256 : part * 256 + width] = value[2 * h : 2 * h + 2, 0:width]
    store(g_table, outs[4])
    for c in stores:
        c.wait()


def local(n_k, n_l, fields, cotangent, bias_table, gain_one, w_qkv, w_proj, gain_two, w_in, w_out):
    n_lon = 2 * n_k
    sds = jax.ShapeDtypeStruct
    vmem = pltpu.VMEM
    dma = pltpu.SemaphoreType.DMA
    whole = pl.BlockSpec(memory_space=pltpu.VMEM)
    apart = pl.BlockSpec(memory_space=pl.ANY)
    early, late = EARLY // n_lon, LATE // n_lon
    both = late + TABLE // n_lon
    inputs = (
        fields,
        cotangent,
        bias_table.transpose(0, 2, 1, 3),
        gain_one.reshape(1, C),
        w_qkv,
        w_proj,
        gain_two.reshape(1, C),
        w_in,
        w_out.T,
        jnp.asarray(place_level_in()),
        jnp.asarray(place_edge_in()),
        jnp.asarray(pick_edge_in()),
        jnp.asarray(place_level_out()),
        jnp.asarray(pick_edge_out()),
        jnp.asarray(spread_matrix()),
        jnp.asarray(region_masks()),
        jnp.asarray(head_masks()),
    )

    def buffers(chunk, kept):
        return [
            vmem((n_k, chunk, 256), BF16),
            vmem((n_k, chunk, 256), BF16),
            vmem((n_k - 1, chunk, 256), BF16),
            vmem((n_k - 1, chunk, 256), BF16),
            vmem((chunk, 256), F32),
            vmem((n_l, kept, 256), BF16),
            vmem((n_l, 16, 256), BF16),
        ]

    slots = max(n_k, n_l)
    results = pl.pallas_call(
        functools.partial(block_kernel, n_k, n_l),
        out_shape=(
            sds((2, n_k, early, 256), BF16),
            sds((2, n_k, both, 256), BF16),
            sds((2, 4, 3, 24, C), BF16),
            sds((2, 4, 3, 24, C), BF16),
            sds((2, 2 * EDGE, C), BF16),
        ),
        in_specs=[apart] * len(INPUTS),
        out_specs=[whole] * 5,
        scratch_shapes=[vmem(value.shape, value.dtype) for value in inputs]
        + [
            vmem((2, 4, 3, 24, C), BF16),
            vmem((2, 2 * EDGE, C), BF16),
            vmem((2, 2 * EDGE, C), BF16),
            vmem((2, 4, 3, 24, C), BF16),
            vmem((2, 2 * EDGE, C), BF16),
            vmem((ROWS, C), F32),
            vmem((ROWS, C), BF16),
            vmem((ROWS, C), BF16),
            vmem((ROWS, C), BF16),
            vmem((ROWS, C), BF16),
            vmem((ROWS, C), BF16),
            vmem((2, STACK, TOK), F32),
            vmem((WIN, STACK, TOK), F32),
            vmem((ROWS, C), BF16),
            vmem((ROWS, FFH), BF16),
            vmem((ROWS, FFH), BF16),
            vmem((ROWS, C), BF16),
            vmem((ROWS, C), BF16),
            vmem((ROWS, C), F32),
            vmem((ROWS, C), BF16),
            vmem((ROWS, C), F32),
            vmem((ROWS, C), BF16),
            vmem((ROWS, C), BF16),
            vmem((ROWS, C), BF16),
            vmem((2, 2 * STACK, 128), F32),
            vmem((4, TOK, 128), F32),
            vmem((2, 2 * STACK, 128), F32),
            vmem((16, 4096), F32),
            vmem((EARLY, 256), F32),
            vmem((LATE, 256), F32),
            vmem((TABLE, 256), F32),
        ]
        + buffers(early, 16)
        + buffers(both, late)
        + [
            dma((len(INPUTS),)),
            dma((2, 2, 3)),
            dma((2, 2, 3)),
            dma((12, slots)),
            dma((12, slots)),
        ],
        compiler_params=pltpu.CompilerParams(
            collective_id=0, has_side_effects=True, vmem_limit_bytes=60 * 1024 * 1024
        ),
        name="block",
    )(*inputs)
    given = (*results, jnp.asarray(place_level_end()), jnp.asarray(place_edge_end()))
    shapes = (
        sds((4, 6, 24, C), BF16),
        sds((4, 6, 24, C), BF16),
        sds((1, C), F32),
        sds((C, 3 * C), F32),
        sds((1, HEADS, 2, POS), F32),
        sds((C, C), F32),
        sds((1, C), F32),
        sds((C, FFH), F32),
        sds((C, FFH), F32),
    )
    outs = pl.pallas_call(
        functools.partial(finish_kernel, n_k),
        out_shape=shapes,
        in_specs=[apart] * 7,
        out_specs=[apart] * 9,
        scratch_shapes=[vmem(value.shape, value.dtype) for value in given]
        + [vmem((EARLY, 256), F32), vmem((LATE, 256), F32)]
        + [vmem(value.shape, value.dtype) for value in shapes]
        + [dma((7,)), dma((13,))],
        compiler_params=pltpu.CompilerParams(vmem_limit_bytes=60 * 1024 * 1024),
        name="finish",
    )(*given)
    outs = list(outs)
    outs[2] = outs[2].reshape(C)
    outs[4] = outs[4].transpose(0, 2, 1, 3)
    outs[6] = outs[6].reshape(C)
    outs[8] = outs[8].T
    return tuple(outs)


def solution(mesh):
    n_k, n_l = mesh.shape["lon"] // 2, mesh.shape["lat"]
    placed = (
        P(None, "lat", "lon", None),
        P(None, "lat", "lon", None),
        P("lat", None, None, None),
    ) + (P(),) * 6
    return jax.shard_map(
        functools.partial(local, n_k, n_l),
        mesh=mesh,
        in_specs=placed,
        out_specs=(
            P(None, "lat", "lon", None),
            P(None, "lat", "lon", None),
            P(),
            P(),
            P("lat", None, None, None),
            P(),
            P(),
            P(),
            P(),
        ),
        check_vma=False,
    )
```

```python
import functools

import jax
import jax.numpy as jnp
import numpy as np
from jax import lax
from jax.experimental import pallas as pl
from jax.experimental.pallas import tpu as pltpu
from jax.sharding import PartitionSpec as P

HEADS = 6
C = 192
FFH = 768
TOK = 144
WIN = 4
ROWS = WIN * TOK
STACK = HEADS * TOK
POS = 3312
SEG = 138
EARLY = 1280
LATE = 512
TABLE = 256
EDGE = 80
MESH = pl.DeviceIdType.MESH
F32 = jnp.float32
BF16 = jnp.bfloat16


def window_row(lev, lat, col):
    return ((lev // 2) * 2 + col // 12) * TOK + (lev % 2) * 72 + lat * 12 + col % 12


def place_level_in():
    out = np.zeros((TOK, TOK), np.float32)
    for lat in range(6):
        for col in range(18):
            out[col // 12 * 72 + lat * 12 + col % 12, lat * 24 + col + 6] = 1
    return out


def edge_row(lev, lat, col):
    return (0 if lat < 3 else EDGE) + lev * 18 + lat % 3 * 6 + col


def place_edge_in():
    out = np.zeros((4, TOK, 2 * EDGE), np.float32)
    for lev in range(4):
        for lat in range(6):
            for col in range(6):
                out[lev, 72 + lat * 12 + 6 + col, edge_row((lev + 1) % 4, lat, col)] = 1
    return out


def pick_edge_in():
    out = np.zeros((2 * EDGE, ROWS), np.float32)
    for lev in range(4):
        for lat in range(6):
            for col in range(6):
                out[edge_row(lev, (lat + 3) % 6, col), (lev * 6 + lat) * 24 + col] = 1
    return out


def place_level_out():
    out = np.zeros((TOK, TOK), np.float32)
    for lat in range(6):
        for col in range(24):
            out[lat * 24 + col, col // 12 * 72 + lat * 12 + col % 12] = 1
    return out


def pick_edge_out():
    out = np.zeros((2 * EDGE, ROWS), np.float32)
    for lev in range(4):
        for lat in range(6):
            for col in range(6):
                out[edge_row(lev, lat, col), window_row(lev, lat, 18 + col)] = 1
    return out


def place_level_end():
    out = np.zeros((TOK, TOK), np.float32)
    for lat in range(6):
        for lon in range(6, 24):
            out[lat * 24 + lon, lat * 24 + lon - 6] = 1
    return out


def place_edge_end():
    out = np.zeros((4, TOK, 2 * EDGE), np.float32)
    for lev in range(4):
        for lat in range(6):
            for lon in range(6):
                out[lev, lat * 24 + lon, edge_row(lev, (lat + 3) % 6, lon)] = 1
    return out


def spread_matrix():
    out = np.zeros((512, 256), np.float32)
    for level in range(2):
        for lat in range(6):
            for col in range(12):
                out[level * 256 + lat * 23 + 11 - col, level * 72 + lat * 12 + col] = 1
    return out


def region_masks():
    ids = np.arange(TOK)
    level, lat = ids // 72, ids // 12 % 6 >= 3
    out = np.zeros((2, TOK, TOK), np.float32)
    out[0] = level[:, None] != level[None, :]
    out[1] = lat[:, None] != lat[None, :]
    return out


def head_masks():
    out = np.zeros((8, C), np.float32)
    for head in range(HEADS):
        out[head, head * 32 : head * 32 + 32] = 1
    return out


def mm(left, right):
    return lax.dot_general(left, right, (((1,), (0,)), ((), ())), preferred_element_type=F32)


def mm_nt(left, right):
    return lax.dot_general(left, right, (((1,), (1,)), ((), ())), preferred_element_type=F32)


def mm_tn(left, right):
    return lax.dot_general(left, right, (((0,), (0,)), ((), ())), preferred_element_type=F32)


def norm(values):
    center = values - jnp.mean(values, axis=-1, keepdims=True)
    spread = jnp.mean(center * center, axis=-1, keepdims=True)
    inverse = lax.rsqrt(spread + 1e-05)
    return center * inverse, inverse


def norm_grad(d_normed, gain, unit, inverse):
    d_unit = d_normed * gain
    mean_one = jnp.mean(d_unit, axis=-1, keepdims=True)
    mean_two = jnp.mean(d_unit * unit, axis=-1, keepdims=True)
    return inverse * (d_unit - mean_one - unit * mean_two)


def split_heads(value, heads):
    return jnp.concatenate([value * heads[h : h + 1, :] for h in range(HEADS)], axis=0)


def join_heads(stacked, heads):
    total = stacked[0:TOK, :] * heads[0:1, :]
    for h in range(1, HEADS):
        total = total + stacked[h * TOK : (h + 1) * TOK, :] * heads[h : h + 1, :]
    return total


def segment(cell, other):
    return ((2 * (cell // 6) + other) * 36 + 6 * (cell % 6)) * 23


def segment(cell, other):
    return ((2 * (cell // 6) + other) * 36 + 6 * (cell % 6)) * 23


def expand_bias(bias_ref, spread_ref, masks_ref, parts, flat, stage, bias, last):
    flat[...] = jnp.zeros_like(flat)
    for h in range(HEADS):
        flat[2 * h : 2 * h + 2, 0:POS] = bias_ref[0, h]
    for cell in range(12):
        for other in range(2):
            start = segment(cell, other)
            for half in range(2):
                parts[2 * other + half, pl.ds(cell, 12, stride=12), :] = flat[
                    0:12, start + half * 128 : start + half * 128 + 128
                ]
    for step in range(12):
        total = None
        for other in range(2):
            value = jnp.concatenate([parts[2 * other], parts[2 * other + 1]], axis=1)
            if step:
                value = pltpu.roll(value, 256 - step, 1)
            matrix = spread_ref[other * 256 : (other + 1) * 256, :].astype(BF16)
            for _ in range(3):
                part = value.astype(BF16)
                value = value - part.astype(F32)
                term = mm(part, matrix)
                total = term if total is None else total + term
        for half in range(2):
            stage[half, pl.ds(step, TOK, stride=12), :] = total[:, half * 128 : half * 128 + 128]
    for lev in range(2):
        closed = masks_ref[1] * last
        if lev == 1:
            closed = closed + masks_ref[0]
        for h in range(HEADS):
            rows = slice((2 * h + lev) * TOK, (2 * h + lev + 1) * TOK)
            value = jnp.concatenate([stage[0, rows, :], stage[1, rows, 0:16]], axis=1)
            bias[lev, h * TOK : (h + 1) * TOK, :] = jnp.where(closed > 0.5, -1000000000.0, value)


def reduce_table(d_bias, spread_ref, parts, flat, table):
    value = jnp.concatenate(
        [
            jnp.concatenate(
                [d_bias[half, pl.ds(step, TOK, stride=12), :] for half in range(2)], axis=1
            )
            for step in range(12)
        ],
        axis=0,
    ).astype(BF16)
    sums = []
    for other in range(2):
        terms = mm_nt(value, spread_ref[other * 256 : (other + 1) * 256, :].astype(BF16))
        total = terms[0:TOK, :]
        for step in range(1, 12):
            total = total + pltpu.roll(terms[step * TOK : (step + 1) * TOK, :], step, 1)
        sums.append(total)
    for other in range(2):
        for half in range(2):
            parts[2 * other + half] = sums[other][:, half * 128 : half * 128 + 128]
    flat[...] = jnp.zeros_like(flat)
    for cell in range(12):
        for other in range(2):
            start = segment(cell, other)
            rows = pl.ds(cell, 12, stride=12)
            flat[0:12, start : start + 128] = parts[2 * other, rows, :]
            flat[0:12, start + 128 : start + SEG] = parts[2 * other + 1, rows, :][:, 0 : SEG - 128]
    for part in range(16):
        table[part * 16 : (part + 1) * 16, :] = flat[:, part * 256 : (part + 1) * 256]


def gather_all(own, below, edges, place, place_edge, out):
    place = place[...].astype(BF16)
    for lev in range(4):
        source = (lev + 1) % 4
        parts = [
            own[source, 3:6].astype(F32).reshape(72, C),
            below[source].astype(F32).reshape(72, C),
        ]
        rows = mm(place, jnp.concatenate(parts, axis=0).astype(BF16))
        rows = rows + mm(place_edge[lev].astype(BF16), edges[...])
        for half in range(2):
            start = ((lev // 2) * 2 + half) * TOK + (lev % 2) * 72
            out[start : start + 72, :] = rows[half * 72 : (half + 1) * 72, :].astype(out.dtype)


def scatter_all(value, place, pick, own, full, edges):
    place = place[...].astype(BF16)
    for lev in range(4):
        parts = []
        for half in range(2):
            start = ((lev // 2) * 2 + half) * TOK + (lev % 2) * 72
            parts.append(value[start : start + 72, :])
        rows = mm(place, jnp.concatenate(parts, axis=0).astype(BF16))
        own[lev] = rows[0:72].reshape(3, 24, C).astype(BF16)
        full[lev] = rows[72:144].reshape(3, 24, C).astype(BF16)
    edges[...] = mm(pick[...].astype(BF16), value[...].astype(BF16)).astype(BF16)


INPUTS = (
    "fields",
    "cotangent",
    "bias_table",
    "gain_one",
    "w_qkv",
    "w_proj",
    "gain_two",
    "w_in",
    "w_out",
    "place_in",
    "edge_in",
    "pick_in",
    "place_out",
    "pick_out",
    "spread",
    "masks",
    "heads",
    "place_end",
    "edge_end",
)


class Section:
    def __init__(self, net, chunk, rest, refs):
        self.net, self.chunk, self.rest = net, chunk, rest
        (
            self.pack,
            self.table,
            self.send_pair,
            self.recv_pair,
            self.send_lon,
            self.recv_lon,
            self.total,
            self.by_lat,
            self.send_lat,
            self.gathered,
            self.sems,
        ) = refs
        self.pair, self.along_lon = [], []

    def rows(self, ref, size, core, k):
        start = pl.multiple_of((2 * k + core) * size, size)
        return ref[pl.ds(start, size), :]

    def sem(self, stage, slot):
        return (self.sems.at[stage, slot], self.sems.at[stage + 1, slot])

    def to_pair(self):
        net = self.net
        for d in range(1, net.n_k + 1):
            k = lax.rem(net.k + d, net.n_k)
            self.send_pair[d - 1, 0 : self.chunk, :] = self.rows(
                self.pack, self.chunk, net.other, k
            ).astype(BF16)
            if self.rest:
                self.send_pair[d - 1, self.chunk : self.chunk + self.rest, :] = self.rows(
                    self.table, self.rest, net.other, k
                ).astype(BF16)
            self.pair.append(
                net.start(
                    self.send_pair.at[d - 1],
                    self.recv_pair.at[d - 1],
                    self.sem(0, d - 1),
                    net.partner,
                )
            )

    def to_lon(self):
        net = self.net
        for d in range(1, net.n_k + 1):
            k = lax.rem(net.k + d, net.n_k)
            self.pair[d - 1].wait_recv()
            value = self.rows(self.pack, self.chunk, net.core, k)
            if self.rest:
                value = jnp.concatenate(
                    [value, self.rows(self.table, self.rest, net.core, k)], axis=0
                )
            value = value + self.recv_pair[d - 1].astype(F32)
            if d == net.n_k:
                self.total[...] = value
                continue
            self.send_lon[d - 1] = value.astype(BF16)
            self.along_lon.append(
                net.start(
                    self.send_lon.at[d - 1],
                    self.recv_lon.at[d - 1],
                    self.sem(2, d - 1),
                    net.along_lon(d),
                )
            )

    def sum_lon(self):
        value = self.total[...]
        for d in range(1, self.net.n_k):
            self.along_lon[d - 1].wait_recv()
            value = value + self.recv_lon[d - 1].astype(F32)
        return value.astype(BF16)

    def sum_lat(self):
        value = self.by_lat[0].astype(F32)
        for i in range(1, self.net.n_l):
            value = value + self.by_lat[i].astype(F32)
        return value.astype(BF16)

    def spread_lon(self):
        net = self.net
        mine = self.gathered.at[net.core, net.k]
        for d in range(1, net.n_k):
            net.start(mine, mine, self.sem(8, d - 1), net.along_lon(d))
        net.start(mine, mine, self.sem(10, 0), net.partner)

    def to_lat(self):
        net = self.net
        value = self.sum_lon()
        mine = self.by_lat.at[net.lat]
        mine[...] = value[0 : self.chunk, :]
        self.gathered[net.core, net.k, self.chunk : self.chunk + self.rest, :] = value[
            self.chunk : self.chunk + self.rest, :
        ]
        for d in range(1, net.n_l):
            net.start(mine, mine, self.sem(4, d - 1), net.along_lat(d))

    def from_lat(self):
        net = self.net
        for d in range(1, net.n_l):
            theirs = self.by_lat.at[lax.rem(net.lat - d + net.n_l, net.n_l)]
            net.copy(theirs, theirs, self.sem(4, d - 1), net.partner).wait_recv()
        self.gathered[net.core, net.k, 0 : self.chunk, :] = self.sum_lat()
        self.spread_lon()

    def to_owner(self, pieces):
        net = self.net
        value = self.sum_lon()
        for p in range(pieces):
            pieces_ref = self.send_lat.at[p]
            pieces_ref[...] = value[p * 16 : (p + 1) * 16, :]

            @pl.when(net.lat != p)
            def _(p=p):
                self.owner_copy(p).start()

    def owner_copy(self, p):
        net = self.net
        sems = (self.sems.at[4, p], self.sems.at[5, net.lat])
        return net.copy(self.send_lat.at[p], self.by_lat.at[net.lat], sems, (net.lon, p))

    def own_piece(self):
        net = self.net
        return self.gathered.at[net.core, net.k, pl.ds(pl.multiple_of(net.lat * 16, 16), 16), :]

    def back_copy(self, d):
        net = self.net
        sems = (self.sems.at[6, d - 1], self.sems.at[7, net.lat])
        return net.copy(self.own_piece(), self.own_piece(), sems, net.along_lat(d))

    def from_owner(self, pieces):
        net = self.net

        @pl.when(net.lat < pieces)
        def _():
            self.by_lat[net.lat] = self.send_lat[net.lat]
            for d in range(1, net.n_l):
                source = lax.rem(net.lat + d, net.n_l)
                theirs = self.by_lat.at[source]
                sems = (self.sems.at[4, 0], self.sems.at[5, source])
                net.copy(theirs, theirs, sems, net.partner).wait_recv()
            self.own_piece()[...] = self.sum_lat()
            for d in range(1, net.n_l):
                self.back_copy(d).start()

    def after_owner(self, pieces):
        net = self.net
        for p in range(pieces):

            @pl.when(net.lat != p)
            def _(p=p):
                theirs = self.gathered.at[net.core, net.k, p * 16 : (p + 1) * 16, :]
                sems = (self.sems.at[6, 0], self.sems.at[7, p])
                net.copy(theirs, theirs, sems, net.partner).wait_recv()

        self.spread_lon()

    def close_owner(self, pieces):
        net = self.net
        for p in range(pieces):

            @pl.when(net.lat != p)
            def _(p=p):
                self.owner_copy(p).wait_send()

        @pl.when(net.lat < pieces)
        def _():
            for d in range(1, net.n_l):
                self.back_copy(d).wait_send()

    def spread_pair(self):
        net = self.net
        for d in range(1, net.n_k):
            theirs = self.gathered.at[net.core, lax.rem(net.k - d + net.n_k, net.n_k)]
            net.copy(theirs, theirs, self.sem(8, d - 1), net.partner).wait_recv()
            net.start(theirs, theirs, self.sem(10, d), net.partner)

    def close(self):
        net = self.net
        for d in range(net.n_k):
            theirs = self.gathered.at[net.other, lax.rem(net.k - d + net.n_k, net.n_k)]
            net.copy(theirs, theirs, self.sem(10, d), net.partner).wait_recv()


class Net:
    def __init__(self, n_k, n_l):
        self.n_k, self.n_l = n_k, n_l
        self.n_lon = 2 * n_k
        self.lon, self.lat = lax.axis_index("lon"), lax.axis_index("lat")
        self.core, self.k = lax.rem(self.lon, 2), self.lon // 2
        self.other = 1 - self.core
        self.partner = (2 * self.k + self.other, self.lat)
        self.started = []

    def at(self, d_lon, d_lat):
        return (
            lax.rem(self.lon + d_lon + self.n_lon, self.n_lon),
            lax.rem(self.lat + d_lat + self.n_l, self.n_l),
        )

    def along_lon(self, d):
        return (2 * lax.rem(self.k + d, self.n_k) + self.core, self.lat)

    def along_lat(self, d):
        return self.at(0, d)

    def greet(self):
        far = lax.rem(self.lon + 2 * self.core - 1 + self.n_lon, self.n_lon)
        friends = [self.partner, (far, self.lat), self.at(1, 1), self.at(-1, -1)]
        friends += [self.along_lon(d) for d in range(1, self.n_k)]
        friends += [self.along_lat(d) for d in range(1, self.n_l)]
        barrier = pltpu.get_barrier_semaphore()
        for friend in friends:
            pl.semaphore_signal(barrier, inc=1, device_id=friend, device_id_type=MESH)
        return barrier, len(friends)

    def copy(self, source, target, sems, device):
        return pltpu.make_async_remote_copy(
            src_ref=source,
            dst_ref=target,
            send_sem=sems[0],
            recv_sem=sems[1],
            device_id=device,
            device_id_type=MESH,
        )

    def start(self, source, target, sems, device):
        c = self.copy(source, target, sems, device)
        c.start()
        self.started.append(c)
        return c


def block_kernel(n_k, n_l, *refs):
    refs = list(refs)

    def take(count):
        out = refs[:count]
        del refs[:count]
        return out

    hbm = dict(zip(INPUTS, take(len(INPUTS)), strict=True))
    early_out, late_out, block_out, grad_fields = take(4)
    here = dict(zip(INPUTS, take(len(INPUTS)), strict=True))
    below, edges, edges_send, full, edges_back = take(5)
    own_out, below_out, edge_out = take(3)
    x_ref, cot_ref, n1_ref, q_ref, k_ref, v_ref, bias, probs, att_ref = take(9)
    act_ref, dpre_ref, n2_ref, dbb_ref, dbranch_ref, datt_ref, out_ref = take(7)
    dq_ref, dk_ref, dv_ref, d_bias, parts, stage, flat = take(7)
    early_pack, late_pack, table = take(3)
    early_bufs, late_bufs = take(7), take(7)
    load_sem, in_sem, out_sem, early_sem, late_sem = take(5)

    net = Net(n_k, n_l)
    barrier, count = net.greet()
    loads = {
        name: pltpu.make_async_copy(hbm[name], here[name], load_sem.at[i])
        for i, name in enumerate(INPUTS)
    }
    for name in INPUTS:
        loads[name].start()

    early = Section(net, EARLY // net.n_lon, 0, [early_pack, None, *early_bufs, early_out, early_sem])
    late = Section(
        net,
        LATE // net.n_lon,
        TABLE // net.n_lon,
        [late_pack, table, *late_bufs, late_out, late_sem],
    )

    def send_in(i, name):
        south = net.start(
            hbm[name].at[:, 0:3], below.at[i], (in_sem.at[0, i, 0], in_sem.at[1, i, 0]), net.at(0, -1)
        )
        if i == 0:
            loads["fields"].wait()
            loads["pick_in"].wait()
        flat_rows = here[name][...].astype(F32).reshape(ROWS, C).astype(BF16)
        edges_send[i] = mm(here["pick_in"][...].astype(BF16), flat_rows).astype(BF16)
        east = net.start(
            edges_send.at[i, 0:EDGE],
            edges.at[i, 0:EDGE],
            (in_sem.at[0, i, 1], in_sem.at[1, i, 1]),
            net.at(-1, 0),
        )
        corner = net.start(
            edges_send.at[i, EDGE : 2 * EDGE],
            edges.at[i, EDGE : 2 * EDGE],
            (in_sem.at[0, i, 2], in_sem.at[1, i, 2]),
            net.at(-1, -1),
        )
        return [south, east, corner]

    def send_out(i):
        return [
            net.start(
                full.at[i], below_out.at[i], (out_sem.at[0, i, 0], out_sem.at[1, i, 0]), net.at(0, 1)
            ),
            net.start(
                edges_back.at[i, 0:EDGE],
                edge_out.at[i, 0:EDGE],
                (out_sem.at[0, i, 1], out_sem.at[1, i, 1]),
                net.at(1, 0),
            ),
            net.start(
                edges_back.at[i, EDGE : 2 * EDGE],
                edge_out.at[i, EDGE : 2 * EDGE],
                (out_sem.at[0, i, 2], out_sem.at[1, i, 2]),
                net.at(1, 1),
            ),
        ]

    pl.semaphore_wait(barrier, count)
    in_copies = [send_in(0, "fields")]
    for name in INPUTS:
        if name not in ("fields", "pick_in"):
            loads[name].wait()

    last = (net.lat == n_l - 1).astype(F32)
    expand_bias(here["bias_table"], here["spread"], here["masks"], parts, flat, stage, bias, last)

    heads32 = here["heads"][...]
    heads = heads32.astype(BF16)
    scale = 32**-0.5
    gain1 = here["gain_one"][...]
    gain2 = here["gain_two"][...]
    w_qkv, w_proj, w_in, w_out = here["w_qkv"], here["w_proj"], here["w_in"], here["w_out"]

    for c in in_copies[0]:
        c.wait_recv()
    in_copies.append(send_in(1, "cotangent"))
    gather_all(here["fields"], below.at[0], edges.at[0], here["place_in"], here["edge_in"], x_ref)
    unit, _ = norm(x_ref[...])
    n1 = (unit * gain1).astype(BF16)
    n1_ref[...] = n1
    for i, ref in enumerate((q_ref, k_ref, v_ref)):
        ref[...] = mm(n1, w_qkv[:, i * C : (i + 1) * C]).astype(BF16)

    def attend(w, carry):
        rows = pl.ds(pl.multiple_of(w * TOK, TOK), TOK)
        stacked = split_heads(q_ref[rows, :], heads)
        scores = mm_nt(stacked, k_ref[rows, :]) * scale + bias[w // 2]
        top = jnp.max(scores, axis=-1, keepdims=True)
        exps = jnp.exp(scores - top)
        prob = exps * (1.0 / jnp.sum(exps, axis=-1, keepdims=True))
        probs[w] = prob
        mixed = mm(prob.astype(BF16), v_ref[rows, :])
        att_ref[rows, :] = join_heads(mixed, heads32).astype(BF16)
        return carry

    lax.fori_loop(0, WIN, attend, 0, unroll=True)

    for c in in_copies[1]:
        c.wait_recv()
    gather_all(
        here["cotangent"], below.at[1], edges.at[1], here["place_in"], here["edge_in"], cot_ref
    )
    half = ROWS // 2

    def feed(i, gain_sum):
        rows = pl.ds(pl.multiple_of(i * half, half), half)
        branch = x_ref[rows, :] + mm(att_ref[rows, :], w_proj[...])
        unit, inverse = norm(branch)
        n2 = (unit * gain2).astype(BF16)
        n2_ref[rows, :] = n2
        pre = mm(n2, w_in[...])
        cdf = 0.5 + 0.5 * lax.erf(pre * (0.5**0.5))
        slope = cdf + pre * (jnp.exp(-0.5 * pre * pre) * ((2.0 * np.pi) ** -0.5))
        act = (pre * cdf).astype(BF16)
        act_ref[rows, :] = act
        out_ref[rows, :] = branch + mm_nt(act, w_out[...])
        cot = cot_ref[rows, :]
        d_pre = (slope * mm(cot, w_out[...])).astype(BF16)
        dpre_ref[rows, :] = d_pre
        d_normed = mm_nt(d_pre, w_in[...])
        d_branch = cot.astype(F32) + norm_grad(d_normed, gain2, unit, inverse)
        dbranch_ref[rows, :] = d_branch
        dbb = d_branch.astype(BF16)
        dbb_ref[rows, :] = dbb
        datt_ref[rows, :] = mm_nt(dbb, w_proj[...]).astype(BF16)
        return gain_sum + jnp.sum(d_normed * unit, axis=0, keepdims=True)

    gain_sum2 = lax.fori_loop(0, 2, feed, jnp.zeros((1, C), F32), unroll=True)

    late_pack[448:LATE, :] = jnp.zeros((LATE - 448, 256), F32)
    late_pack[456:457, 0:C] = gain_sum2
    for i in range(3):
        cols = slice(i * 256, (i + 1) * 256)
        early_pack[i * C : (i + 1) * C, :] = mm_tn(cot_ref[...], act_ref[:, cols])
        early_pack[576 + i * C : 576 + (i + 1) * C, :] = mm_tn(n2_ref[...], dpre_ref[:, cols])
    grad = mm_tn(att_ref[...], dbb_ref[...])
    early_pack[1152:EARLY, 0:C] = grad[0:128, :]
    late_pack[432:448, 0:C] = grad[128:TOK, :]
    early_pack[1152:1200, C:256] = grad[TOK:C, 0:64]
    early_pack[1200:1248, C:256] = grad[TOK:C, 64:128]
    early_pack[1248:EARLY, C:256] = grad[TOK:176, 128:C]
    late_pack[432:448, C:256] = grad[176:C, 128:C]
    early.to_pair()
    scatter_all(
        out_ref, here["place_out"], here["pick_out"], own_out.at[0], full.at[0], edges_back.at[0]
    )
    out_copies = send_out(0)

    early.to_lon()
    d_bias[...] = jnp.zeros_like(d_bias)

    def attend_back(w, carry):
        rows = pl.ds(pl.multiple_of(w * TOK, TOK), TOK)
        prob = probs[w]
        d_stacked = split_heads(datt_ref[rows, :], heads)
        d_prob = mm_nt(d_stacked, v_ref[rows, :])
        d_score = prob * (d_prob - jnp.sum(d_prob * prob, axis=-1, keepdims=True))
        for h in range(HEADS):
            group = pl.ds(pl.multiple_of((2 * h + w // 2) * TOK, TOK), TOK)
            part = d_score[h * TOK : (h + 1) * TOK, :]
            d_bias[0, group, :] += part[:, 0:128]
            d_bias[1, group, 0:16] += part[:, 128:144]
        d_score_b = d_score.astype(BF16)
        dv_ref[rows, :] = mm_tn(prob.astype(BF16), d_stacked).astype(BF16)
        dq_ref[rows, :] = (join_heads(mm(d_score_b, k_ref[rows, :]), heads32) * scale).astype(BF16)
        stacked = split_heads(q_ref[rows, :], heads)
        dk_ref[rows, :] = (mm_tn(d_score_b, stacked) * scale).astype(BF16)
        return carry

    lax.fori_loop(0, WIN, attend_back, 0, unroll=2)
    pieces = EARLY // net.n_lon // 16

    d_normed = None
    for i, ref in enumerate((dq_ref, dk_ref, dv_ref)):
        grad = mm_tn(n1_ref[...], ref[...])
        late_pack[i * TOK : (i + 1) * TOK, 0:C] = grad[0:TOK, :]
        for j in range(3):
            rows = slice(i * TOK + j * 48, i * TOK + (j + 1) * 48)
            late_pack[rows, C:256] = grad[TOK:C, j * 64 : (j + 1) * 64]
        term = mm_nt(ref[...], w_qkv[:, i * C : (i + 1) * C])
        d_normed = term if d_normed is None else d_normed + term
    unit, inverse = norm(x_ref[...])
    late_pack[448:449, 0:C] = jnp.sum(d_normed * unit, axis=0, keepdims=True)
    out_ref[...] = dbranch_ref[...] + norm_grad(d_normed, gain1, unit, inverse)
    reduce_table(d_bias, here["spread"], parts, flat, table)
    late.to_pair()
    scatter_all(
        out_ref, here["place_out"], here["pick_out"], own_out.at[1], full.at[1], edges_back.at[1]
    )
    late.to_lon()
    early.to_owner(pieces)

    def merge(i, target):
        for c in out_copies[3 * i : 3 * i + 3]:
            c.wait_recv()
        place = here["place_end"][...].astype(BF16)
        for lev in range(4):
            rows = [
                below_out[i, lev].astype(F32).reshape(72, C),
                own_out[i, lev].astype(F32).reshape(72, C),
            ]
            value = mm(place, jnp.concatenate(rows, axis=0).astype(BF16))
            value = value + mm(here["edge_end"][lev].astype(BF16), edge_out[i])
            target[(lev + 1) % 4] = value.reshape(6, 24, C).astype(BF16)

    merge(0, block_out)
    early.from_owner(pieces)
    late.to_lat()
    early.after_owner(pieces)
    out_copies += send_out(1)
    late.from_lat()
    early.spread_pair()
    late.spread_pair()
    merge(1, grad_fields)
    early.close()
    late.close()
    early.close_owner(pieces)
    for c in net.started:
        c.wait_send()


def finish_kernel(n_k, *refs):
    hbm, outs, here = refs[0:4], refs[4:13], refs[13:17]
    early_rows, late_rows = refs[17:19]
    g_gain_one, g_w_qkv, g_table, g_w_proj, g_gain_two = refs[19:24]
    load_sem, store_sem = refs[24:26]
    loads = [pltpu.make_async_copy(hbm[i], here[i], load_sem.at[i]) for i in range(4)]
    for c in loads:
        c.start()
    early, late = here[0:2]
    out_w_in, out_w_out = outs[7], outs[8]
    stores = []

    def store(source, target):
        c = pltpu.make_async_copy(source, target, store_sem.at[len(stores)])
        c.start()
        stores.append(c)

    n_lon = 2 * n_k
    chunk = EARLY // n_lon
    loads[0].wait()
    for part in range(n_lon):
        early_rows[part * chunk : (part + 1) * chunk, :] = early[part % 2, part // 2].astype(F32)
    for i in range(3):
        cols = slice(i * 256, (i + 1) * 256)
        store(early_rows.at[i * C : (i + 1) * C, :], out_w_out.at[:, cols])
        store(early_rows.at[576 + i * C : 576 + (i + 1) * C, :], out_w_in.at[:, cols])
    for i in range(2):
        loads[2 + i].wait()
        store(here[2 + i], outs[i])
    loads[1].wait()
    rest, chunk = TABLE // n_lon, LATE // n_lon
    for part in range(n_lon):
        late_rows[part * chunk : (part + 1) * chunk, :] = late[
            part % 2, part // 2, 0:chunk, :
        ].astype(F32)
    for i in range(3):
        g_w_qkv[0:TOK, i * C : (i + 1) * C] = late_rows[i * TOK : (i + 1) * TOK, 0:C]
        for j in range(3):
            cols = slice(i * C + j * 64, i * C + (j + 1) * 64)
            g_w_qkv[TOK:C, cols] = late_rows[i * TOK + j * 48 : i * TOK + (j + 1) * 48, C:256]
    store(g_w_qkv, outs[3])
    g_w_proj[0:128, :] = early_rows[1152:EARLY, 0:C]
    g_w_proj[128:TOK, :] = late_rows[432:448, 0:C]
    g_w_proj[TOK:C, 0:64] = early_rows[1152:1200, C:256]
    g_w_proj[TOK:C, 64:128] = early_rows[1200:1248, C:256]
    g_w_proj[TOK:176, 128:C] = early_rows[1248:EARLY, C:256]
    g_w_proj[176:C, 128:C] = late_rows[432:448, C:256]
    store(g_w_proj, outs[5])
    g_gain_one[...] = late_rows[448:449, 0:C]
    store(g_gain_one, outs[2])
    g_gain_two[...] = late_rows[456:457, 0:C]
    store(g_gain_two, outs[6])
    for part in range(13):
        width = min(256, POS - part * 256)
        place, offset = divmod(part * 16, rest)
        value = late[place % 2, place // 2, chunk + offset : chunk + offset + 16, :].astype(F32)
        for h in range(HEADS):
            g_table[0, h, :, part * 256 : part * 256 + width] = value[2 * h : 2 * h + 2, 0:width]
    store(g_table, outs[4])
    for c in stores:
        c.wait()


def local(n_k, n_l, fields, cotangent, bias_table, gain_one, w_qkv, w_proj, gain_two, w_in, w_out):
    n_lon = 2 * n_k
    sds = jax.ShapeDtypeStruct
    vmem = pltpu.VMEM
    dma = pltpu.SemaphoreType.DMA
    whole = pl.BlockSpec(memory_space=pltpu.VMEM)
    apart = pl.BlockSpec(memory_space=pl.ANY)
    early, late = EARLY // n_lon, LATE // n_lon
    both = late + TABLE // n_lon
    inputs = (
        fields,
        cotangent,
        bias_table.transpose(0, 2, 1, 3),
        gain_one.reshape(1, C),
        w_qkv,
        w_proj,
        gain_two.reshape(1, C),
        w_in,
        w_out.T,
        jnp.asarray(place_level_in()),
        jnp.asarray(place_edge_in()),
        jnp.asarray(pick_edge_in()),
        jnp.asarray(place_level_out()),
        jnp.asarray(pick_edge_out()),
        jnp.asarray(spread_matrix()),
        jnp.asarray(region_masks()),
        jnp.asarray(head_masks()),
        jnp.asarray(place_level_end()),
        jnp.asarray(place_edge_end()),
    )

    def buffers(chunk, kept):
        return [
            vmem((n_k, chunk, 256), BF16),
            vmem((n_k, chunk, 256), BF16),
            vmem((n_k - 1, chunk, 256), BF16),
            vmem((n_k - 1, chunk, 256), BF16),
            vmem((chunk, 256), F32),
            vmem((n_l, kept, 256), BF16),
            vmem((n_l, 16, 256), BF16),
        ]

    slots = max(n_k, n_l)
    results = pl.pallas_call(
        functools.partial(block_kernel, n_k, n_l),
        out_shape=(
            sds((2, n_k, early, 256), BF16),
            sds((2, n_k, both, 256), BF16),
            sds((4, 6, 24, C), BF16),
            sds((4, 6, 24, C), BF16),
        ),
        in_specs=[apart] * len(INPUTS),
        out_specs=[whole] * 4,
        scratch_shapes=[vmem(value.shape, value.dtype) for value in inputs]
        + [
            vmem((2, 4, 3, 24, C), BF16),
            vmem((2, 2 * EDGE, C), BF16),
            vmem((2, 2 * EDGE, C), BF16),
            vmem((2, 4, 3, 24, C), BF16),
            vmem((2, 2 * EDGE, C), BF16),
            vmem((2, 4, 3, 24, C), BF16),
            vmem((2, 4, 3, 24, C), BF16),
            vmem((2, 2 * EDGE, C), BF16),
            vmem((ROWS, C), F32),
            vmem((ROWS, C), BF16),
            vmem((ROWS, C), BF16),
            vmem((ROWS, C), BF16),
            vmem((ROWS, C), BF16),
            vmem((ROWS, C), BF16),
            vmem((2, STACK, TOK), F32),
            vmem((WIN, STACK, TOK), F32),
            vmem((ROWS, C), BF16),
            vmem((ROWS, FFH), BF16),
            vmem((ROWS, FFH), BF16),
            vmem((ROWS, C), BF16),
            vmem((ROWS, C), BF16),
            vmem((ROWS, C), F32),
            vmem((ROWS, C), BF16),
            vmem((ROWS, C), F32),
            vmem((ROWS, C), BF16),
            vmem((ROWS, C), BF16),
            vmem((ROWS, C), BF16),
            vmem((2, 2 * STACK, 128), F32),
            vmem((4, TOK, 128), F32),
            vmem((2, 2 * STACK, 128), F32),
            vmem((16, 4096), F32),
            vmem((EARLY, 256), F32),
            vmem((LATE, 256), F32),
            vmem((TABLE, 256), F32),
        ]
        + buffers(early, 16)
        + buffers(both, late)
        + [
            dma((len(INPUTS),)),
            dma((2, 2, 3)),
            dma((2, 2, 3)),
            dma((12, slots)),
            dma((12, slots)),
        ],
        compiler_params=pltpu.CompilerParams(
            collective_id=0, has_side_effects=True, vmem_limit_bytes=60 * 1024 * 1024
        ),
        name="block",
    )(*inputs)
    shapes = (
        sds((4, 6, 24, C), BF16),
        sds((4, 6, 24, C), BF16),
        sds((1, C), F32),
        sds((C, 3 * C), F32),
        sds((1, HEADS, 2, POS), F32),
        sds((C, C), F32),
        sds((1, C), F32),
        sds((C, FFH), F32),
        sds((C, FFH), F32),
    )
    outs = pl.pallas_call(
        functools.partial(finish_kernel, n_k),
        out_shape=shapes,
        in_specs=[apart] * 4,
        out_specs=[apart] * 9,
        scratch_shapes=[vmem(value.shape, value.dtype) for value in results]
        + [vmem((EARLY, 256), F32), vmem((LATE, 256), F32)]
        + [vmem(value.shape, value.dtype) for value in shapes[2:7]]
        + [dma((4,)), dma((13,))],
        compiler_params=pltpu.CompilerParams(vmem_limit_bytes=60 * 1024 * 1024),
        name="finish",
    )(*results)
    outs = list(outs)
    outs[2] = outs[2].reshape(C)
    outs[4] = outs[4].transpose(0, 2, 1, 3)
    outs[6] = outs[6].reshape(C)
    outs[8] = outs[8].T
    return tuple(outs)


def solution(mesh):
    n_k, n_l = mesh.shape["lon"] // 2, mesh.shape["lat"]
    placed = (
        P(None, "lat", "lon", None),
        P(None, "lat", "lon", None),
        P("lat", None, None, None),
    ) + (P(),) * 6
    return jax.shard_map(
        functools.partial(local, n_k, n_l),
        mesh=mesh,
        in_specs=placed,
        out_specs=(
            P(None, "lat", "lon", None),
            P(None, "lat", "lon", None),
            P(),
            P(),
            P("lat", None, None, None),
            P(),
            P(),
            P(),
            P(),
        ),
        check_vma=False,
    )
```

```python
import functools

import jax
import jax.numpy as jnp
import numpy as np
from jax import lax
from jax.experimental import pallas as pl
from jax.experimental.pallas import tpu as pltpu
from jax.sharding import PartitionSpec as P

HEADS = 6
C = 192
FFH = 768
TOK = 144
WIN = 4
ROWS = WIN * TOK
STACK = HEADS * TOK
POS = 3312
SEG = 138
EARLY = 1280
LATE = 512
TABLE = 256
EDGE = 80
MESH = pl.DeviceIdType.MESH
F32 = jnp.float32
BF16 = jnp.bfloat16


def window_row(lev, lat, col):
    return ((lev // 2) * 2 + col // 12) * TOK + (lev % 2) * 72 + lat * 12 + col % 12


def place_level_in():
    out = np.zeros((TOK, TOK), np.float32)
    for lat in range(6):
        for col in range(18):
            out[col // 12 * 72 + lat * 12 + col % 12, lat * 24 + col + 6] = 1
    return out


def edge_row(lev, lat, col):
    return (0 if lat < 3 else EDGE) + lev * 18 + lat % 3 * 6 + col


def place_edge_in():
    out = np.zeros((4, TOK, 2 * EDGE), np.float32)
    for lev in range(4):
        for lat in range(6):
            for col in range(6):
                out[lev, 72 + lat * 12 + 6 + col, edge_row((lev + 1) % 4, lat, col)] = 1
    return out


def pick_edge_in():
    out = np.zeros((2 * EDGE, ROWS), np.float32)
    for lev in range(4):
        for lat in range(6):
            for col in range(6):
                out[edge_row(lev, (lat + 3) % 6, col), (lev * 6 + lat) * 24 + col] = 1
    return out


def place_level_out():
    out = np.zeros((TOK, TOK), np.float32)
    for lat in range(6):
        for col in range(24):
            out[lat * 24 + col, col // 12 * 72 + lat * 12 + col % 12] = 1
    return out


def pick_edge_out():
    out = np.zeros((2 * EDGE, ROWS), np.float32)
    for lev in range(4):
        for lat in range(6):
            for col in range(6):
                out[edge_row(lev, lat, col), window_row(lev, lat, 18 + col)] = 1
    return out


def place_level_end():
    out = np.zeros((TOK, TOK), np.float32)
    for lat in range(6):
        for lon in range(6, 24):
            out[lat * 24 + lon, lat * 24 + lon - 6] = 1
    return out


def place_edge_end():
    out = np.zeros((4, TOK, 2 * EDGE), np.float32)
    for lev in range(4):
        for lat in range(6):
            for lon in range(6):
                out[lev, lat * 24 + lon, edge_row(lev, (lat + 3) % 6, lon)] = 1
    return out


def spread_matrix():
    out = np.zeros((512, 256), np.float32)
    for level in range(2):
        for lat in range(6):
            for col in range(12):
                out[level * 256 + lat * 23 + 11 - col, level * 72 + lat * 12 + col] = 1
    return out


def region_masks():
    ids = np.arange(TOK)
    level, lat = ids // 72, ids // 12 % 6 >= 3
    out = np.zeros((2, TOK, TOK), np.float32)
    out[0] = level[:, None] != level[None, :]
    out[1] = lat[:, None] != lat[None, :]
    return out


def head_masks():
    out = np.zeros((8, C), np.float32)
    for head in range(HEADS):
        out[head, head * 32 : head * 32 + 32] = 1
    return out


def mm(left, right):
    return lax.dot_general(left, right, (((1,), (0,)), ((), ())), preferred_element_type=F32)


def mm_nt(left, right):
    return lax.dot_general(left, right, (((1,), (1,)), ((), ())), preferred_element_type=F32)


def mm_tn(left, right):
    return lax.dot_general(left, right, (((0,), (0,)), ((), ())), preferred_element_type=F32)


def norm(values):
    center = values - jnp.mean(values, axis=-1, keepdims=True)
    spread = jnp.mean(center * center, axis=-1, keepdims=True)
    inverse = lax.rsqrt(spread + 1e-05)
    return center * inverse, inverse


def norm_grad(d_normed, gain, unit, inverse):
    d_unit = d_normed * gain
    mean_one = jnp.mean(d_unit, axis=-1, keepdims=True)
    mean_two = jnp.mean(d_unit * unit, axis=-1, keepdims=True)
    return inverse * (d_unit - mean_one - unit * mean_two)


def split_heads(value, heads):
    return jnp.concatenate([value * heads[h : h + 1, :] for h in range(HEADS)], axis=0)


def join_heads(stacked, heads):
    total = stacked[0:TOK, :] * heads[0:1, :]
    for h in range(1, HEADS):
        total = total + stacked[h * TOK : (h + 1) * TOK, :] * heads[h : h + 1, :]
    return total


def segment(cell, other):
    return ((2 * (cell // 6) + other) * 36 + 6 * (cell % 6)) * 23


def segment(cell, other):
    return ((2 * (cell // 6) + other) * 36 + 6 * (cell % 6)) * 23


def expand_bias(bias_ref, spread_ref, masks_ref, parts, flat, stage, bias, last):
    flat[...] = jnp.zeros_like(flat)
    for h in range(HEADS):
        flat[2 * h : 2 * h + 2, 0:POS] = bias_ref[0, h]
    for cell in range(12):
        for other in range(2):
            start = segment(cell, other)
            for half in range(2):
                parts[2 * other + half, pl.ds(cell, 12, stride=12), :] = flat[
                    0:12, start + half * 128 : start + half * 128 + 128
                ]
    for step in range(12):
        total = None
        for other in range(2):
            value = jnp.concatenate([parts[2 * other], parts[2 * other + 1]], axis=1)
            if step:
                value = pltpu.roll(value, 256 - step, 1)
            matrix = spread_ref[other * 256 : (other + 1) * 256, :].astype(BF16)
            for _ in range(3):
                part = value.astype(BF16)
                value = value - part.astype(F32)
                term = mm(part, matrix)
                total = term if total is None else total + term
        for half in range(2):
            stage[half, pl.ds(step, TOK, stride=12), :] = total[:, half * 128 : half * 128 + 128]
    for lev in range(2):
        closed = masks_ref[1] * last
        if lev == 1:
            closed = closed + masks_ref[0]
        for h in range(HEADS):
            rows = slice((2 * h + lev) * TOK, (2 * h + lev + 1) * TOK)
            value = jnp.concatenate([stage[0, rows, :], stage[1, rows, 0:16]], axis=1)
            bias[lev, h * TOK : (h + 1) * TOK, :] = jnp.where(closed > 0.5, -1000000000.0, value)


def reduce_table(d_bias, spread_ref, parts, flat, table):
    value = jnp.concatenate(
        [
            jnp.concatenate(
                [d_bias[half, pl.ds(step, TOK, stride=12), :] for half in range(2)], axis=1
            )
            for step in range(12)
        ],
        axis=0,
    ).astype(BF16)
    sums = []
    for other in range(2):
        terms = mm_nt(value, spread_ref[other * 256 : (other + 1) * 256, :].astype(BF16))
        total = terms[0:TOK, :]
        for step in range(1, 12):
            total = total + pltpu.roll(terms[step * TOK : (step + 1) * TOK, :], step, 1)
        sums.append(total)
    for other in range(2):
        for half in range(2):
            parts[2 * other + half] = sums[other][:, half * 128 : half * 128 + 128]
    flat[...] = jnp.zeros_like(flat)
    for cell in range(12):
        for other in range(2):
            start = segment(cell, other)
            rows = pl.ds(cell, 12, stride=12)
            flat[0:12, start : start + 128] = parts[2 * other, rows, :]
            flat[0:12, start + 128 : start + SEG] = parts[2 * other + 1, rows, :][:, 0 : SEG - 128]
    for part in range(16):
        table[part * 16 : (part + 1) * 16, :] = flat[:, part * 256 : (part + 1) * 256]


def gather_all(own, below, edges, place, place_edge, out):
    place = place[...].astype(BF16)
    for lev in range(4):
        source = (lev + 1) % 4
        parts = [
            own[source, 3:6].astype(F32).reshape(72, C),
            below[source].astype(F32).reshape(72, C),
        ]
        rows = mm(place, jnp.concatenate(parts, axis=0).astype(BF16))
        rows = rows + mm(place_edge[lev].astype(BF16), edges[...])
        for half in range(2):
            start = ((lev // 2) * 2 + half) * TOK + (lev % 2) * 72
            out[start : start + 72, :] = rows[half * 72 : (half + 1) * 72, :].astype(out.dtype)


def scatter_all(value, place, pick, own, full, edges):
    place = place[...].astype(BF16)
    for lev in range(4):
        parts = []
        for half in range(2):
            start = ((lev // 2) * 2 + half) * TOK + (lev % 2) * 72
            parts.append(value[start : start + 72, :])
        rows = mm(place, jnp.concatenate(parts, axis=0).astype(BF16))
        own[lev] = rows[0:72].reshape(3, 24, C).astype(BF16)
        full[lev] = rows[72:144].reshape(3, 24, C).astype(BF16)
    edges[...] = mm(pick[...].astype(BF16), value[...].astype(BF16)).astype(BF16)


INPUTS = (
    "fields",
    "cotangent",
    "bias_table",
    "gain_one",
    "w_qkv",
    "w_proj",
    "gain_two",
    "w_in",
    "w_out",
    "place_in",
    "edge_in",
    "pick_in",
    "place_out",
    "pick_out",
    "spread",
    "masks",
    "heads",
    "place_end",
    "edge_end",
)


class Section:
    def __init__(self, net, chunk, rest, refs):
        self.net, self.chunk, self.rest = net, chunk, rest
        (
            self.pack,
            self.table,
            self.send_pair,
            self.recv_pair,
            self.send_lon,
            self.recv_lon,
            self.total,
            self.by_lat,
            self.send_lat,
            self.gathered,
            self.sems,
        ) = refs
        self.pair, self.along_lon = [], []

    def rows(self, ref, size, core, k):
        start = pl.multiple_of((2 * k + core) * size, size)
        return ref[pl.ds(start, size), :]

    def sem(self, stage, slot):
        return (self.sems.at[stage, slot], self.sems.at[stage + 1, slot])

    def to_pair(self):
        net = self.net
        for d in range(1, net.n_k + 1):
            k = lax.rem(net.k + d, net.n_k)
            self.send_pair[d - 1, 0 : self.chunk, :] = self.rows(
                self.pack, self.chunk, net.other, k
            ).astype(BF16)
            if self.rest:
                self.send_pair[d - 1, self.chunk : self.chunk + self.rest, :] = self.rows(
                    self.table, self.rest, net.other, k
                ).astype(BF16)
            self.pair.append(
                net.start(
                    self.send_pair.at[d - 1],
                    self.recv_pair.at[d - 1],
                    self.sem(0, d - 1),
                    net.partner,
                )
            )

    def to_lon(self):
        net = self.net
        for d in range(1, net.n_k + 1):
            k = lax.rem(net.k + d, net.n_k)
            self.pair[d - 1].wait_recv()
            value = self.rows(self.pack, self.chunk, net.core, k)
            if self.rest:
                value = jnp.concatenate(
                    [value, self.rows(self.table, self.rest, net.core, k)], axis=0
                )
            value = value + self.recv_pair[d - 1].astype(F32)
            if d == net.n_k:
                self.total[...] = value
                continue
            self.send_lon[d - 1] = value.astype(BF16)
            self.along_lon.append(
                net.start(
                    self.send_lon.at[d - 1],
                    self.recv_lon.at[d - 1],
                    self.sem(2, d - 1),
                    net.along_lon(d),
                )
            )

    def sum_lon(self):
        value = self.total[...]
        for d in range(1, self.net.n_k):
            self.along_lon[d - 1].wait_recv()
            value = value + self.recv_lon[d - 1].astype(F32)
        return value.astype(BF16)

    def sum_lat(self):
        value = self.by_lat[0].astype(F32)
        for i in range(1, self.net.n_l):
            value = value + self.by_lat[i].astype(F32)
        return value.astype(BF16)

    def spread_lon(self):
        net = self.net
        mine = self.gathered.at[net.core, net.k]
        for d in range(1, net.n_k):
            net.start(mine, mine, self.sem(8, d - 1), net.along_lon(d))
        net.start(mine, mine, self.sem(10, 0), net.partner)

    def to_lat(self):
        net = self.net
        value = self.sum_lon()
        mine = self.by_lat.at[net.lat]
        mine[...] = value[0 : self.chunk, :]
        self.gathered[net.core, net.k, self.chunk : self.chunk + self.rest, :] = value[
            self.chunk : self.chunk + self.rest, :
        ]
        for d in range(1, net.n_l):
            net.start(mine, mine, self.sem(4, d - 1), net.along_lat(d))

    def from_lat(self):
        net = self.net
        for d in range(1, net.n_l):
            theirs = self.by_lat.at[lax.rem(net.lat - d + net.n_l, net.n_l)]
            net.copy(theirs, theirs, self.sem(4, d - 1), net.partner).wait_recv()
        self.gathered[net.core, net.k, 0 : self.chunk, :] = self.sum_lat()
        self.spread_lon()

    def to_owner(self, pieces):
        net = self.net
        value = self.sum_lon()
        for p in range(pieces):
            pieces_ref = self.send_lat.at[p]
            pieces_ref[...] = value[p * 16 : (p + 1) * 16, :]

            @pl.when(net.lat != p)
            def _(p=p):
                self.owner_copy(p).start()

    def owner_copy(self, p):
        net = self.net
        sems = (self.sems.at[4, p], self.sems.at[5, net.lat])
        return net.copy(self.send_lat.at[p], self.by_lat.at[net.lat], sems, (net.lon, p))

    def own_piece(self):
        net = self.net
        return self.gathered.at[net.core, net.k, pl.ds(pl.multiple_of(net.lat * 16, 16), 16), :]

    def back_copy(self, d):
        net = self.net
        sems = (self.sems.at[6, d - 1], self.sems.at[7, net.lat])
        return net.copy(self.own_piece(), self.own_piece(), sems, net.along_lat(d))

    def from_owner(self, pieces):
        net = self.net

        @pl.when(net.lat < pieces)
        def _():
            self.by_lat[net.lat] = self.send_lat[net.lat]
            for d in range(1, net.n_l):
                source = lax.rem(net.lat + d, net.n_l)
                theirs = self.by_lat.at[source]
                sems = (self.sems.at[4, 0], self.sems.at[5, source])
                net.copy(theirs, theirs, sems, net.partner).wait_recv()
            self.own_piece()[...] = self.sum_lat()
            for d in range(1, net.n_l):
                self.back_copy(d).start()

    def after_owner(self, pieces):
        net = self.net
        for p in range(pieces):

            @pl.when(net.lat != p)
            def _(p=p):
                theirs = self.gathered.at[net.core, net.k, p * 16 : (p + 1) * 16, :]
                sems = (self.sems.at[6, 0], self.sems.at[7, p])
                net.copy(theirs, theirs, sems, net.partner).wait_recv()

        self.spread_lon()

    def close_owner(self, pieces):
        net = self.net
        for p in range(pieces):

            @pl.when(net.lat != p)
            def _(p=p):
                self.owner_copy(p).wait_send()

        @pl.when(net.lat < pieces)
        def _():
            for d in range(1, net.n_l):
                self.back_copy(d).wait_send()

    def spread_pair(self):
        net = self.net
        for d in range(1, net.n_k):
            theirs = self.gathered.at[net.core, lax.rem(net.k - d + net.n_k, net.n_k)]
            net.copy(theirs, theirs, self.sem(8, d - 1), net.partner).wait_recv()
            net.start(theirs, theirs, self.sem(10, d), net.partner)

    def close(self):
        net = self.net
        for d in range(net.n_k):
            theirs = self.gathered.at[net.other, lax.rem(net.k - d + net.n_k, net.n_k)]
            net.copy(theirs, theirs, self.sem(10, d), net.partner).wait_recv()


class Net:
    def __init__(self, n_k, n_l):
        self.n_k, self.n_l = n_k, n_l
        self.n_lon = 2 * n_k
        self.lon, self.lat = lax.axis_index("lon"), lax.axis_index("lat")
        self.core, self.k = lax.rem(self.lon, 2), self.lon // 2
        self.other = 1 - self.core
        self.partner = (2 * self.k + self.other, self.lat)
        self.started = []

    def at(self, d_lon, d_lat):
        return (
            lax.rem(self.lon + d_lon + self.n_lon, self.n_lon),
            lax.rem(self.lat + d_lat + self.n_l, self.n_l),
        )

    def along_lon(self, d):
        return (2 * lax.rem(self.k + d, self.n_k) + self.core, self.lat)

    def along_lat(self, d):
        return self.at(0, d)

    def greet(self):
        far = lax.rem(self.lon + 2 * self.core - 1 + self.n_lon, self.n_lon)
        friends = [self.partner, (far, self.lat), self.at(1, 1), self.at(-1, -1)]
        friends += [self.along_lon(d) for d in range(1, self.n_k)]
        friends += [self.along_lat(d) for d in range(1, self.n_l)]
        barrier = pltpu.get_barrier_semaphore()
        for friend in friends:
            pl.semaphore_signal(barrier, inc=1, device_id=friend, device_id_type=MESH)
        return barrier, len(friends)

    def copy(self, source, target, sems, device):
        return pltpu.make_async_remote_copy(
            src_ref=source,
            dst_ref=target,
            send_sem=sems[0],
            recv_sem=sems[1],
            device_id=device,
            device_id_type=MESH,
        )

    def start(self, source, target, sems, device):
        c = self.copy(source, target, sems, device)
        c.start()
        self.started.append(c)
        return c


def block_kernel(n_k, n_l, *refs):
    refs = list(refs)

    def take(count):
        out = refs[:count]
        del refs[:count]
        return out

    hbm = dict(zip(INPUTS, take(len(INPUTS)), strict=True))
    early_out, late_out, block_out, grad_fields = take(4)
    here = dict(zip(INPUTS, take(len(INPUTS)), strict=True))
    below, edges, edges_send, full, edges_back = take(5)
    own_out, below_out, edge_out = take(3)
    x_ref, cot_ref, n1_ref, q_ref, k_ref, v_ref, bias, probs, att_ref = take(9)
    act_ref, dpre_ref, n2_ref, dbb_ref, dbranch_ref, datt_ref, out_ref = take(7)
    dq_ref, dk_ref, dv_ref, d_bias, parts, stage, flat = take(7)
    early_pack, late_pack, table = take(3)
    early_bufs, late_bufs = take(7), take(7)
    load_sem, in_sem, out_sem, early_sem, late_sem = take(5)

    net = Net(n_k, n_l)
    barrier, count = net.greet()
    loads = {
        name: pltpu.make_async_copy(hbm[name], here[name], load_sem.at[i])
        for i, name in enumerate(INPUTS)
    }
    for name in INPUTS:
        loads[name].start()

    early = Section(net, EARLY // net.n_lon, 0, [early_pack, None, *early_bufs, early_out, early_sem])
    late = Section(
        net,
        LATE // net.n_lon,
        TABLE // net.n_lon,
        [late_pack, table, *late_bufs, late_out, late_sem],
    )

    def send_in(i, name):
        south = net.start(
            hbm[name].at[:, 0:3], below.at[i], (in_sem.at[0, i, 0], in_sem.at[1, i, 0]), net.at(0, -1)
        )
        if i == 0:
            loads["fields"].wait()
            loads["pick_in"].wait()
        flat_rows = here[name][...].astype(F32).reshape(ROWS, C).astype(BF16)
        edges_send[i] = mm(here["pick_in"][...].astype(BF16), flat_rows).astype(BF16)
        east = net.start(
            edges_send.at[i, 0:EDGE],
            edges.at[i, 0:EDGE],
            (in_sem.at[0, i, 1], in_sem.at[1, i, 1]),
            net.at(-1, 0),
        )
        corner = net.start(
            edges_send.at[i, EDGE : 2 * EDGE],
            edges.at[i, EDGE : 2 * EDGE],
            (in_sem.at[0, i, 2], in_sem.at[1, i, 2]),
            net.at(-1, -1),
        )
        return [south, east, corner]

    def send_out(i):
        return [
            net.start(
                full.at[i], below_out.at[i], (out_sem.at[0, i, 0], out_sem.at[1, i, 0]), net.at(0, 1)
            ),
            net.start(
                edges_back.at[i, 0:EDGE],
                edge_out.at[i, 0:EDGE],
                (out_sem.at[0, i, 1], out_sem.at[1, i, 1]),
                net.at(1, 0),
            ),
            net.start(
                edges_back.at[i, EDGE : 2 * EDGE],
                edge_out.at[i, EDGE : 2 * EDGE],
                (out_sem.at[0, i, 2], out_sem.at[1, i, 2]),
                net.at(1, 1),
            ),
        ]

    pl.semaphore_wait(barrier, count)
    in_copies = [send_in(0, "fields")]
    for name in INPUTS:
        if name not in ("fields", "pick_in"):
            loads[name].wait()

    last = (net.lat == n_l - 1).astype(F32)
    expand_bias(here["bias_table"], here["spread"], here["masks"], parts, flat, stage, bias, last)

    heads32 = here["heads"][...]
    heads = heads32.astype(BF16)
    scale = 32**-0.5
    gain1 = here["gain_one"][...]
    gain2 = here["gain_two"][...]
    w_qkv, w_proj, w_in, w_out = here["w_qkv"], here["w_proj"], here["w_in"], here["w_out"]

    for c in in_copies[0]:
        c.wait_recv()
    in_copies.append(send_in(1, "cotangent"))
    gather_all(here["fields"], below.at[0], edges.at[0], here["place_in"], here["edge_in"], x_ref)
    unit, _ = norm(x_ref[...])
    n1 = (unit * gain1).astype(BF16)
    n1_ref[...] = n1
    for i, ref in enumerate((q_ref, k_ref, v_ref)):
        ref[...] = mm(n1, w_qkv[:, i * C : (i + 1) * C]).astype(BF16)

    def attend(w, carry):
        rows = pl.ds(pl.multiple_of(w * TOK, TOK), TOK)
        stacked = split_heads(q_ref[rows, :], heads)
        scores = mm_nt(stacked, k_ref[rows, :]) * scale + bias[w // 2]
        top = jnp.max(scores, axis=-1, keepdims=True)
        exps = jnp.exp(scores - top)
        prob = exps * (1.0 / jnp.sum(exps, axis=-1, keepdims=True))
        probs[w] = prob
        mixed = mm(prob.astype(BF16), v_ref[rows, :])
        att_ref[rows, :] = join_heads(mixed, heads32).astype(BF16)
        return carry

    lax.fori_loop(0, WIN, attend, 0, unroll=True)

    for c in in_copies[1]:
        c.wait_recv()
    gather_all(
        here["cotangent"], below.at[1], edges.at[1], here["place_in"], here["edge_in"], cot_ref
    )
    half = ROWS // 2

    def feed(i, gain_sum):
        rows = pl.ds(pl.multiple_of(i * half, half), half)
        branch = x_ref[rows, :] + mm(att_ref[rows, :], w_proj[...])
        unit, inverse = norm(branch)
        n2 = (unit * gain2).astype(BF16)
        n2_ref[rows, :] = n2
        pre = mm(n2, w_in[...])
        cdf = 0.5 + 0.5 * lax.erf(pre * (0.5**0.5))
        slope = cdf + pre * (jnp.exp(-0.5 * pre * pre) * ((2.0 * np.pi) ** -0.5))
        act = (pre * cdf).astype(BF16)
        act_ref[rows, :] = act
        out_ref[rows, :] = branch + mm_nt(act, w_out[...])
        cot = cot_ref[rows, :]
        d_pre = (slope * mm(cot, w_out[...])).astype(BF16)
        dpre_ref[rows, :] = d_pre
        d_normed = mm_nt(d_pre, w_in[...])
        d_branch = cot.astype(F32) + norm_grad(d_normed, gain2, unit, inverse)
        dbranch_ref[rows, :] = d_branch
        dbb = d_branch.astype(BF16)
        dbb_ref[rows, :] = dbb
        datt_ref[rows, :] = mm_nt(dbb, w_proj[...]).astype(BF16)
        return gain_sum + jnp.sum(d_normed * unit, axis=0, keepdims=True)

    gain_sum2 = lax.fori_loop(0, 2, feed, jnp.zeros((1, C), F32), unroll=True)

    late_pack[448:LATE, :] = jnp.zeros((LATE - 448, 256), F32)
    late_pack[456:457, 0:C] = gain_sum2
    for i in range(3):
        cols = slice(i * 256, (i + 1) * 256)
        early_pack[i * C : (i + 1) * C, :] = mm_tn(cot_ref[...], act_ref[:, cols])
        early_pack[576 + i * C : 576 + (i + 1) * C, :] = mm_tn(n2_ref[...], dpre_ref[:, cols])
    grad = mm_tn(att_ref[...], dbb_ref[...])
    early_pack[1152:EARLY, 0:C] = grad[0:128, :]
    late_pack[432:448, 0:C] = grad[128:TOK, :]
    early_pack[1152:1200, C:256] = grad[TOK:C, 0:64]
    early_pack[1200:1248, C:256] = grad[TOK:C, 64:128]
    early_pack[1248:EARLY, C:256] = grad[TOK:176, 128:C]
    late_pack[432:448, C:256] = grad[176:C, 128:C]
    early.to_pair()
    scatter_all(
        out_ref, here["place_out"], here["pick_out"], own_out.at[0], full.at[0], edges_back.at[0]
    )
    out_copies = send_out(0)

    early.to_lon()
    d_bias[...] = jnp.zeros_like(d_bias)

    def attend_back(w, carry):
        rows = pl.ds(pl.multiple_of(w * TOK, TOK), TOK)
        prob = probs[w]
        d_stacked = split_heads(datt_ref[rows, :], heads)
        d_prob = mm_nt(d_stacked, v_ref[rows, :])
        d_score = prob * (d_prob - jnp.sum(d_prob * prob, axis=-1, keepdims=True))
        for h in range(HEADS):
            group = pl.ds(pl.multiple_of((2 * h + w // 2) * TOK, TOK), TOK)
            part = d_score[h * TOK : (h + 1) * TOK, :]
            d_bias[0, group, :] += part[:, 0:128]
            d_bias[1, group, 0:16] += part[:, 128:144]
        d_score_b = d_score.astype(BF16)
        dv_ref[rows, :] = mm_tn(prob.astype(BF16), d_stacked).astype(BF16)
        dq_ref[rows, :] = (join_heads(mm(d_score_b, k_ref[rows, :]), heads32) * scale).astype(BF16)
        stacked = split_heads(q_ref[rows, :], heads)
        dk_ref[rows, :] = (mm_tn(d_score_b, stacked) * scale).astype(BF16)
        return carry

    lax.fori_loop(0, WIN, attend_back, 0, unroll=2)
    pieces = EARLY // net.n_lon // 16

    d_normed = None
    for i, ref in enumerate((dq_ref, dk_ref, dv_ref)):
        grad = mm_tn(n1_ref[...], ref[...])
        late_pack[i * TOK : (i + 1) * TOK, 0:C] = grad[0:TOK, :]
        for j in range(3):
            rows = slice(i * TOK + j * 48, i * TOK + (j + 1) * 48)
            late_pack[rows, C:256] = grad[TOK:C, j * 64 : (j + 1) * 64]
        term = mm_nt(ref[...], w_qkv[:, i * C : (i + 1) * C])
        d_normed = term if d_normed is None else d_normed + term
    unit, inverse = norm(x_ref[...])
    late_pack[448:449, 0:C] = jnp.sum(d_normed * unit, axis=0, keepdims=True)
    out_ref[...] = dbranch_ref[...] + norm_grad(d_normed, gain1, unit, inverse)
    reduce_table(d_bias, here["spread"], parts, flat, table)
    late.to_pair()
    scatter_all(
        out_ref, here["place_out"], here["pick_out"], own_out.at[1], full.at[1], edges_back.at[1]
    )
    late.to_lon()
    early.to_owner(pieces)
    out_copies += send_out(1)

    def merge(i, target):
        for c in out_copies[3 * i : 3 * i + 3]:
            c.wait_recv()
        place = here["place_end"][...].astype(BF16)
        for lev in range(4):
            rows = [
                below_out[i, lev].astype(F32).reshape(72, C),
                own_out[i, lev].astype(F32).reshape(72, C),
            ]
            value = mm(place, jnp.concatenate(rows, axis=0).astype(BF16))
            value = value + mm(here["edge_end"][lev].astype(BF16), edge_out[i])
            target[(lev + 1) % 4] = value.reshape(6, 24, C).astype(BF16)

    merge(0, block_out)
    early.from_owner(pieces)
    late.to_lat()
    early.after_owner(pieces)
    late.from_lat()
    early.spread_pair()
    late.spread_pair()
    merge(1, grad_fields)
    early.close()
    late.close()
    early.close_owner(pieces)
    for c in net.started:
        c.wait_send()


def finish_kernel(n_k, *refs):
    hbm, outs, here = refs[0:4], refs[4:13], refs[13:17]
    early_rows, late_rows = refs[17:19]
    g_gain_one, g_w_qkv, g_table, g_w_proj, g_gain_two = refs[19:24]
    load_sem, store_sem = refs[24:26]
    loads = [pltpu.make_async_copy(hbm[i], here[i], load_sem.at[i]) for i in range(4)]
    for c in loads:
        c.start()
    early, late = here[0:2]
    out_w_in, out_w_out = outs[7], outs[8]
    stores = []

    def store(source, target):
        c = pltpu.make_async_copy(source, target, store_sem.at[len(stores)])
        c.start()
        stores.append(c)

    n_lon = 2 * n_k
    chunk = EARLY // n_lon
    loads[0].wait()
    for part in range(n_lon):
        early_rows[part * chunk : (part + 1) * chunk, :] = early[part % 2, part // 2].astype(F32)
    for i in range(3):
        cols = slice(i * 256, (i + 1) * 256)
        store(early_rows.at[i * C : (i + 1) * C, :], out_w_out.at[:, cols])
        store(early_rows.at[576 + i * C : 576 + (i + 1) * C, :], out_w_in.at[:, cols])
    for i in range(2):
        loads[2 + i].wait()
        store(here[2 + i], outs[i])
    loads[1].wait()
    rest, chunk = TABLE // n_lon, LATE // n_lon
    for part in range(n_lon):
        late_rows[part * chunk : (part + 1) * chunk, :] = late[
            part % 2, part // 2, 0:chunk, :
        ].astype(F32)
    for i in range(3):
        g_w_qkv[0:TOK, i * C : (i + 1) * C] = late_rows[i * TOK : (i + 1) * TOK, 0:C]
        for j in range(3):
            cols = slice(i * C + j * 64, i * C + (j + 1) * 64)
            g_w_qkv[TOK:C, cols] = late_rows[i * TOK + j * 48 : i * TOK + (j + 1) * 48, C:256]
    store(g_w_qkv, outs[3])
    g_w_proj[0:128, :] = early_rows[1152:EARLY, 0:C]
    g_w_proj[128:TOK, :] = late_rows[432:448, 0:C]
    g_w_proj[TOK:C, 0:64] = early_rows[1152:1200, C:256]
    g_w_proj[TOK:C, 64:128] = early_rows[1200:1248, C:256]
    g_w_proj[TOK:176, 128:C] = early_rows[1248:EARLY, C:256]
    g_w_proj[176:C, 128:C] = late_rows[432:448, C:256]
    store(g_w_proj, outs[5])
    g_gain_one[...] = late_rows[448:449, 0:C]
    store(g_gain_one, outs[2])
    g_gain_two[...] = late_rows[456:457, 0:C]
    store(g_gain_two, outs[6])
    for part in range(13):
        width = min(256, POS - part * 256)
        place, offset = divmod(part * 16, rest)
        value = late[place % 2, place // 2, chunk + offset : chunk + offset + 16, :].astype(F32)
        for h in range(HEADS):
            g_table[0, h, :, part * 256 : part * 256 + width] = value[2 * h : 2 * h + 2, 0:width]
    store(g_table, outs[4])
    for c in stores:
        c.wait()


def local(n_k, n_l, fields, cotangent, bias_table, gain_one, w_qkv, w_proj, gain_two, w_in, w_out):
    n_lon = 2 * n_k
    sds = jax.ShapeDtypeStruct
    vmem = pltpu.VMEM
    dma = pltpu.SemaphoreType.DMA
    whole = pl.BlockSpec(memory_space=pltpu.VMEM)
    apart = pl.BlockSpec(memory_space=pl.ANY)
    early, late = EARLY // n_lon, LATE // n_lon
    both = late + TABLE // n_lon
    inputs = (
        fields,
        cotangent,
        bias_table.transpose(0, 2, 1, 3),
        gain_one.reshape(1, C),
        w_qkv,
        w_proj,
        gain_two.reshape(1, C),
        w_in,
        w_out.T,
        jnp.asarray(place_level_in()),
        jnp.asarray(place_edge_in()),
        jnp.asarray(pick_edge_in()),
        jnp.asarray(place_level_out()),
        jnp.asarray(pick_edge_out()),
        jnp.asarray(spread_matrix()),
        jnp.asarray(region_masks()),
        jnp.asarray(head_masks()),
        jnp.asarray(place_level_end()),
        jnp.asarray(place_edge_end()),
    )

    def buffers(chunk, kept):
        return [
            vmem((n_k, chunk, 256), BF16),
            vmem((n_k, chunk, 256), BF16),
            vmem((n_k - 1, chunk, 256), BF16),
            vmem((n_k - 1, chunk, 256), BF16),
            vmem((chunk, 256), F32),
            vmem((n_l, kept, 256), BF16),
            vmem((n_l, 16, 256), BF16),
        ]

    slots = max(n_k, n_l)
    results = pl.pallas_call(
        functools.partial(block_kernel, n_k, n_l),
        out_shape=(
            sds((2, n_k, early, 256), BF16),
            sds((2, n_k, both, 256), BF16),
            sds((4, 6, 24, C), BF16),
            sds((4, 6, 24, C), BF16),
        ),
        in_specs=[apart] * len(INPUTS),
        out_specs=[whole] * 4,
        scratch_shapes=[vmem(value.shape, value.dtype) for value in inputs]
        + [
            vmem((2, 4, 3, 24, C), BF16),
            vmem((2, 2 * EDGE, C), BF16),
            vmem((2, 2 * EDGE, C), BF16),
            vmem((2, 4, 3, 24, C), BF16),
            vmem((2, 2 * EDGE, C), BF16),
            vmem((2, 4, 3, 24, C), BF16),
            vmem((2, 4, 3, 24, C), BF16),
            vmem((2, 2 * EDGE, C), BF16),
            vmem((ROWS, C), F32),
            vmem((ROWS, C), BF16),
            vmem((ROWS, C), BF16),
            vmem((ROWS, C), BF16),
            vmem((ROWS, C), BF16),
            vmem((ROWS, C), BF16),
            vmem((2, STACK, TOK), F32),
            vmem((WIN, STACK, TOK), F32),
            vmem((ROWS, C), BF16),
            vmem((ROWS, FFH), BF16),
            vmem((ROWS, FFH), BF16),
            vmem((ROWS, C), BF16),
            vmem((ROWS, C), BF16),
            vmem((ROWS, C), F32),
            vmem((ROWS, C), BF16),
            vmem((ROWS, C), F32),
            vmem((ROWS, C), BF16),
            vmem((ROWS, C), BF16),
            vmem((ROWS, C), BF16),
            vmem((2, 2 * STACK, 128), F32),
            vmem((4, TOK, 128), F32),
            vmem((2, 2 * STACK, 128), F32),
            vmem((16, 4096), F32),
            vmem((EARLY, 256), F32),
            vmem((LATE, 256), F32),
            vmem((TABLE, 256), F32),
        ]
        + buffers(early, 16)
        + buffers(both, late)
        + [
            dma((len(INPUTS),)),
            dma((2, 2, 3)),
            dma((2, 2, 3)),
            dma((12, slots)),
            dma((12, slots)),
        ],
        compiler_params=pltpu.CompilerParams(
            collective_id=0, has_side_effects=True, vmem_limit_bytes=60 * 1024 * 1024
        ),
        name="block",
    )(*inputs)
    shapes = (
        sds((4, 6, 24, C), BF16),
        sds((4, 6, 24, C), BF16),
        sds((1, C), F32),
        sds((C, 3 * C), F32),
        sds((1, HEADS, 2, POS), F32),
        sds((C, C), F32),
        sds((1, C), F32),
        sds((C, FFH), F32),
        sds((C, FFH), F32),
    )
    outs = pl.pallas_call(
        functools.partial(finish_kernel, n_k),
        out_shape=shapes,
        in_specs=[apart] * 4,
        out_specs=[apart] * 9,
        scratch_shapes=[vmem(value.shape, value.dtype) for value in results]
        + [vmem((EARLY, 256), F32), vmem((LATE, 256), F32)]
        + [vmem(value.shape, value.dtype) for value in shapes[2:7]]
        + [dma((4,)), dma((13,))],
        compiler_params=pltpu.CompilerParams(vmem_limit_bytes=60 * 1024 * 1024),
        name="finish",
    )(*results)
    outs = list(outs)
    outs[2] = outs[2].reshape(C)
    outs[4] = outs[4].transpose(0, 2, 1, 3)
    outs[6] = outs[6].reshape(C)
    outs[8] = outs[8].T
    return tuple(outs)


def solution(mesh):
    n_k, n_l = mesh.shape["lon"] // 2, mesh.shape["lat"]
    placed = (
        P(None, "lat", "lon", None),
        P(None, "lat", "lon", None),
        P("lat", None, None, None),
    ) + (P(),) * 6
    return jax.shard_map(
        functools.partial(local, n_k, n_l),
        mesh=mesh,
        in_specs=placed,
        out_specs=(
            P(None, "lat", "lon", None),
            P(None, "lat", "lon", None),
            P(),
            P(),
            P("lat", None, None, None),
            P(),
            P(),
            P(),
            P(),
        ),
        check_vma=False,
    )
```

```python
import functools

import jax
import jax.numpy as jnp
import numpy as np
from jax import lax
from jax.experimental import pallas as pl
from jax.experimental.pallas import tpu as pltpu
from jax.sharding import PartitionSpec as P

HEADS = 6
C = 192
FFH = 768
TOK = 144
WIN = 4
ROWS = WIN * TOK
STACK = HEADS * TOK
POS = 3312
SEG = 138
EARLY = 1280
LATE = 512
TABLE = 256
EDGE = 80
MESH = pl.DeviceIdType.MESH
F32 = jnp.float32
BF16 = jnp.bfloat16


def window_row(lev, lat, col):
    return ((lev // 2) * 2 + col // 12) * TOK + (lev % 2) * 72 + lat * 12 + col % 12


def place_level_in():
    out = np.zeros((TOK, TOK), np.float32)
    for lat in range(6):
        for col in range(18):
            out[col // 12 * 72 + lat * 12 + col % 12, lat * 24 + col + 6] = 1
    return out


def edge_row(lev, lat, col):
    return (0 if lat < 3 else EDGE) + lev * 18 + lat % 3 * 6 + col


def place_edge_in():
    out = np.zeros((4, TOK, 2 * EDGE), np.float32)
    for lev in range(4):
        for lat in range(6):
            for col in range(6):
                out[lev, 72 + lat * 12 + 6 + col, edge_row((lev + 1) % 4, lat, col)] = 1
    return out


def pick_edge_in():
    out = np.zeros((2 * EDGE, ROWS), np.float32)
    for lev in range(4):
        for lat in range(6):
            for col in range(6):
                out[edge_row(lev, (lat + 3) % 6, col), (lev * 6 + lat) * 24 + col] = 1
    return out


def place_level_out():
    out = np.zeros((TOK, TOK), np.float32)
    for lat in range(6):
        for col in range(24):
            out[lat * 24 + col, col // 12 * 72 + lat * 12 + col % 12] = 1
    return out


def pick_edge_out():
    out = np.zeros((2 * EDGE, ROWS), np.float32)
    for lev in range(4):
        for lat in range(6):
            for col in range(6):
                out[edge_row(lev, lat, col), window_row(lev, lat, 18 + col)] = 1
    return out


def place_level_end():
    out = np.zeros((TOK, TOK), np.float32)
    for lat in range(6):
        for lon in range(6, 24):
            out[lat * 24 + lon, lat * 24 + lon - 6] = 1
    return out


def place_edge_end():
    out = np.zeros((4, TOK, 2 * EDGE), np.float32)
    for lev in range(4):
        for lat in range(6):
            for lon in range(6):
                out[lev, lat * 24 + lon, edge_row(lev, (lat + 3) % 6, lon)] = 1
    return out


def spread_matrix():
    out = np.zeros((512, 256), np.float32)
    for level in range(2):
        for lat in range(6):
            for col in range(12):
                out[level * 256 + lat * 23 + 11 - col, level * 72 + lat * 12 + col] = 1
    return out


def region_masks():
    ids = np.arange(TOK)
    level, lat = ids // 72, ids // 12 % 6 >= 3
    out = np.zeros((2, TOK, TOK), np.float32)
    out[0] = level[:, None] != level[None, :]
    out[1] = lat[:, None] != lat[None, :]
    return out


def head_masks():
    out = np.zeros((8, C), np.float32)
    for head in range(HEADS):
        out[head, head * 32 : head * 32 + 32] = 1
    return out


def mm(left, right):
    return lax.dot_general(left, right, (((1,), (0,)), ((), ())), preferred_element_type=F32)


def mm_nt(left, right):
    return lax.dot_general(left, right, (((1,), (1,)), ((), ())), preferred_element_type=F32)


def mm_tn(left, right):
    return lax.dot_general(left, right, (((0,), (0,)), ((), ())), preferred_element_type=F32)


def norm(values):
    center = values - jnp.mean(values, axis=-1, keepdims=True)
    spread = jnp.mean(center * center, axis=-1, keepdims=True)
    inverse = lax.rsqrt(spread + 1e-05)
    return center * inverse, inverse


def norm_grad(d_normed, gain, unit, inverse):
    d_unit = d_normed * gain
    mean_one = jnp.mean(d_unit, axis=-1, keepdims=True)
    mean_two = jnp.mean(d_unit * unit, axis=-1, keepdims=True)
    return inverse * (d_unit - mean_one - unit * mean_two)


def split_heads(value, heads):
    return jnp.concatenate([value * heads[h : h + 1, :] for h in range(HEADS)], axis=0)


def join_heads(stacked, heads):
    total = stacked[0:TOK, :] * heads[0:1, :]
    for h in range(1, HEADS):
        total = total + stacked[h * TOK : (h + 1) * TOK, :] * heads[h : h + 1, :]
    return total


def segment(cell, other):
    return ((2 * (cell // 6) + other) * 36 + 6 * (cell % 6)) * 23


def segment(cell, other):
    return ((2 * (cell // 6) + other) * 36 + 6 * (cell % 6)) * 23


def expand_bias(bias_ref, spread_ref, masks_ref, parts, flat, stage, bias, last):
    flat[...] = jnp.zeros_like(flat)
    for h in range(HEADS):
        flat[2 * h : 2 * h + 2, 0:POS] = bias_ref[0, h]
    for cell in range(12):
        for other in range(2):
            start = segment(cell, other)
            for half in range(2):
                parts[2 * other + half, pl.ds(cell, 12, stride=12), :] = flat[
                    0:12, start + half * 128 : start + half * 128 + 128
                ]
    for step in range(12):
        total = None
        for other in range(2):
            value = jnp.concatenate([parts[2 * other], parts[2 * other + 1]], axis=1)
            if step:
                value = pltpu.roll(value, 256 - step, 1)
            matrix = spread_ref[other * 256 : (other + 1) * 256, :].astype(BF16)
            for _ in range(3):
                part = value.astype(BF16)
                value = value - part.astype(F32)
                term = mm(part, matrix)
                total = term if total is None else total + term
        for half in range(2):
            stage[half, pl.ds(step, TOK, stride=12), :] = total[:, half * 128 : half * 128 + 128]
    for lev in range(2):
        closed = masks_ref[1] * last
        if lev == 1:
            closed = closed + masks_ref[0]
        for h in range(HEADS):
            rows = slice((2 * h + lev) * TOK, (2 * h + lev + 1) * TOK)
            value = jnp.concatenate([stage[0, rows, :], stage[1, rows, 0:16]], axis=1)
            bias[lev, h * TOK : (h + 1) * TOK, :] = jnp.where(closed > 0.5, -1000000000.0, value)


def reduce_table(d_bias, spread_ref, parts, flat, table):
    value = jnp.concatenate(
        [
            jnp.concatenate(
                [d_bias[half, pl.ds(step, TOK, stride=12), :] for half in range(2)], axis=1
            )
            for step in range(12)
        ],
        axis=0,
    ).astype(BF16)
    sums = []
    for other in range(2):
        terms = mm_nt(value, spread_ref[other * 256 : (other + 1) * 256, :].astype(BF16))
        total = terms[0:TOK, :]
        for step in range(1, 12):
            total = total + pltpu.roll(terms[step * TOK : (step + 1) * TOK, :], step, 1)
        sums.append(total)
    for other in range(2):
        for half in range(2):
            parts[2 * other + half] = sums[other][:, half * 128 : half * 128 + 128]
    flat[...] = jnp.zeros_like(flat)
    for cell in range(12):
        for other in range(2):
            start = segment(cell, other)
            rows = pl.ds(cell, 12, stride=12)
            flat[0:12, start : start + 128] = parts[2 * other, rows, :]
            flat[0:12, start + 128 : start + SEG] = parts[2 * other + 1, rows, :][:, 0 : SEG - 128]
    for part in range(16):
        table[part * 16 : (part + 1) * 16, :] = flat[:, part * 256 : (part + 1) * 256]


def gather_all(own, below, edges, place, place_edge, out):
    place = place[...].astype(BF16)
    for lev in range(4):
        source = (lev + 1) % 4
        parts = [
            own[source, 3:6].astype(F32).reshape(72, C),
            below[source].astype(F32).reshape(72, C),
        ]
        rows = mm(place, jnp.concatenate(parts, axis=0).astype(BF16))
        rows = rows + mm(place_edge[lev].astype(BF16), edges[...])
        for half in range(2):
            start = ((lev // 2) * 2 + half) * TOK + (lev % 2) * 72
            out[start : start + 72, :] = rows[half * 72 : (half + 1) * 72, :].astype(out.dtype)


def scatter_all(value, place, pick, own, full, edges):
    place = place[...].astype(BF16)
    for lev in range(4):
        parts = []
        for half in range(2):
            start = ((lev // 2) * 2 + half) * TOK + (lev % 2) * 72
            parts.append(value[start : start + 72, :])
        rows = mm(place, jnp.concatenate(parts, axis=0).astype(BF16))
        own[lev] = rows[0:72].reshape(3, 24, C).astype(BF16)
        full[lev] = rows[72:144].reshape(3, 24, C).astype(BF16)
    edges[...] = mm(pick[...].astype(BF16), value[...].astype(BF16)).astype(BF16)


INPUTS = (
    "fields",
    "cotangent",
    "bias_table",
    "gain_one",
    "w_qkv",
    "w_proj",
    "gain_two",
    "w_in",
    "w_out",
    "place_in",
    "edge_in",
    "pick_in",
    "place_out",
    "pick_out",
    "spread",
    "masks",
    "heads",
    "place_end",
    "edge_end",
)


class Section:
    def __init__(self, net, chunk, rest, refs):
        self.net, self.chunk, self.rest = net, chunk, rest
        (
            self.pack,
            self.table,
            self.send_pair,
            self.recv_pair,
            self.send_lon,
            self.recv_lon,
            self.total,
            self.by_lat,
            self.send_lat,
            self.gathered,
            self.sems,
        ) = refs
        self.pair, self.along_lon = [], []

    def rows(self, ref, size, core, k):
        start = pl.multiple_of((2 * k + core) * size, size)
        return ref[pl.ds(start, size), :]

    def sem(self, stage, slot):
        return (self.sems.at[stage, slot], self.sems.at[stage + 1, slot])

    def to_pair(self):
        net = self.net
        for d in range(1, net.n_k + 1):
            k = lax.rem(net.k + d, net.n_k)
            self.send_pair[d - 1, 0 : self.chunk, :] = self.rows(
                self.pack, self.chunk, net.other, k
            ).astype(BF16)
            if self.rest:
                self.send_pair[d - 1, self.chunk : self.chunk + self.rest, :] = self.rows(
                    self.table, self.rest, net.other, k
                ).astype(BF16)
            self.pair.append(
                net.start(
                    self.send_pair.at[d - 1],
                    self.recv_pair.at[d - 1],
                    self.sem(0, d - 1),
                    net.partner,
                )
            )

    def to_lon(self):
        net = self.net
        for d in range(1, net.n_k + 1):
            k = lax.rem(net.k + d, net.n_k)
            self.pair[d - 1].wait_recv()
            value = self.rows(self.pack, self.chunk, net.core, k)
            if self.rest:
                value = jnp.concatenate(
                    [value, self.rows(self.table, self.rest, net.core, k)], axis=0
                )
            value = value + self.recv_pair[d - 1].astype(F32)
            if d == net.n_k:
                self.total[...] = value
                continue
            self.send_lon[d - 1] = value.astype(BF16)
            self.along_lon.append(
                net.start(
                    self.send_lon.at[d - 1],
                    self.recv_lon.at[d - 1],
                    self.sem(2, d - 1),
                    net.along_lon(d),
                )
            )

    def sum_lon(self):
        value = self.total[...]
        for d in range(1, self.net.n_k):
            self.along_lon[d - 1].wait_recv()
            value = value + self.recv_lon[d - 1].astype(F32)
        return value.astype(BF16)

    def sum_lat(self):
        value = self.by_lat[0].astype(F32)
        for i in range(1, self.net.n_l):
            value = value + self.by_lat[i].astype(F32)
        return value.astype(BF16)

    def spread_lon(self):
        net = self.net
        mine = self.gathered.at[net.core, net.k]
        for d in range(1, net.n_k):
            net.start(mine, mine, self.sem(8, d - 1), net.along_lon(d))
        net.start(mine, mine, self.sem(10, 0), net.partner)

    def to_lat(self):
        net = self.net
        value = self.sum_lon()
        mine = self.by_lat.at[net.lat]
        mine[...] = value[0 : self.chunk, :]
        self.gathered[net.core, net.k, self.chunk : self.chunk + self.rest, :] = value[
            self.chunk : self.chunk + self.rest, :
        ]
        for d in range(1, net.n_l):
            net.start(mine, mine, self.sem(4, d - 1), net.along_lat(d))

    def from_lat(self):
        net = self.net
        for d in range(1, net.n_l):
            theirs = self.by_lat.at[lax.rem(net.lat - d + net.n_l, net.n_l)]
            net.copy(theirs, theirs, self.sem(4, d - 1), net.partner).wait_recv()
        self.gathered[net.core, net.k, 0 : self.chunk, :] = self.sum_lat()
        self.spread_lon()

    def to_owner(self, pieces):
        net = self.net
        value = self.sum_lon()
        for p in range(pieces):
            pieces_ref = self.send_lat.at[p]
            pieces_ref[...] = value[p * 16 : (p + 1) * 16, :]

            @pl.when(net.lat != p)
            def _(p=p):
                self.owner_copy(p).start()

    def owner_copy(self, p):
        net = self.net
        sems = (self.sems.at[4, p], self.sems.at[5, net.lat])
        return net.copy(self.send_lat.at[p], self.by_lat.at[net.lat], sems, (net.lon, p))

    def own_piece(self):
        net = self.net
        return self.gathered.at[net.core, net.k, pl.ds(pl.multiple_of(net.lat * 16, 16), 16), :]

    def back_copy(self, d):
        net = self.net
        sems = (self.sems.at[6, d - 1], self.sems.at[7, net.lat])
        return net.copy(self.own_piece(), self.own_piece(), sems, net.along_lat(d))

    def from_owner(self, pieces):
        net = self.net

        @pl.when(net.lat < pieces)
        def _():
            self.by_lat[net.lat] = self.send_lat[net.lat]
            for d in range(1, net.n_l):
                source = lax.rem(net.lat + d, net.n_l)
                theirs = self.by_lat.at[source]
                sems = (self.sems.at[4, 0], self.sems.at[5, source])
                net.copy(theirs, theirs, sems, net.partner).wait_recv()
            self.own_piece()[...] = self.sum_lat()
            for d in range(1, net.n_l):
                self.back_copy(d).start()

    def after_owner(self, pieces):
        net = self.net
        for p in range(pieces):

            @pl.when(net.lat != p)
            def _(p=p):
                theirs = self.gathered.at[net.core, net.k, p * 16 : (p + 1) * 16, :]
                sems = (self.sems.at[6, 0], self.sems.at[7, p])
                net.copy(theirs, theirs, sems, net.partner).wait_recv()

        self.spread_lon()

    def close_owner(self, pieces):
        net = self.net
        for p in range(pieces):

            @pl.when(net.lat != p)
            def _(p=p):
                self.owner_copy(p).wait_send()

        @pl.when(net.lat < pieces)
        def _():
            for d in range(1, net.n_l):
                self.back_copy(d).wait_send()

    def spread_pair(self):
        net = self.net
        for d in range(1, net.n_k):
            theirs = self.gathered.at[net.core, lax.rem(net.k - d + net.n_k, net.n_k)]
            net.copy(theirs, theirs, self.sem(8, d - 1), net.partner).wait_recv()
            net.start(theirs, theirs, self.sem(10, d), net.partner)

    def close(self):
        net = self.net
        for d in range(net.n_k):
            theirs = self.gathered.at[net.other, lax.rem(net.k - d + net.n_k, net.n_k)]
            net.copy(theirs, theirs, self.sem(10, d), net.partner).wait_recv()


class Net:
    def __init__(self, n_k, n_l):
        self.n_k, self.n_l = n_k, n_l
        self.n_lon = 2 * n_k
        self.lon, self.lat = lax.axis_index("lon"), lax.axis_index("lat")
        self.core, self.k = lax.rem(self.lon, 2), self.lon // 2
        self.other = 1 - self.core
        self.partner = (2 * self.k + self.other, self.lat)
        self.started = []

    def at(self, d_lon, d_lat):
        return (
            lax.rem(self.lon + d_lon + self.n_lon, self.n_lon),
            lax.rem(self.lat + d_lat + self.n_l, self.n_l),
        )

    def along_lon(self, d):
        return (2 * lax.rem(self.k + d, self.n_k) + self.core, self.lat)

    def along_lat(self, d):
        return self.at(0, d)

    def greet(self):
        far = lax.rem(self.lon + 2 * self.core - 1 + self.n_lon, self.n_lon)
        friends = [self.partner, (far, self.lat), self.at(1, 1), self.at(-1, -1)]
        friends += [self.along_lon(d) for d in range(1, self.n_k)]
        friends += [self.along_lat(d) for d in range(1, self.n_l)]
        barrier = pltpu.get_barrier_semaphore()
        for friend in friends:
            pl.semaphore_signal(barrier, inc=1, device_id=friend, device_id_type=MESH)
        return barrier, len(friends)

    def copy(self, source, target, sems, device):
        return pltpu.make_async_remote_copy(
            src_ref=source,
            dst_ref=target,
            send_sem=sems[0],
            recv_sem=sems[1],
            device_id=device,
            device_id_type=MESH,
        )

    def start(self, source, target, sems, device):
        c = self.copy(source, target, sems, device)
        c.start()
        self.started.append(c)
        return c


def block_kernel(n_k, n_l, *refs):
    refs = list(refs)

    def take(count):
        out = refs[:count]
        del refs[:count]
        return out

    hbm = dict(zip(INPUTS, take(len(INPUTS)), strict=True))
    early_out, late_out, block_out, grad_fields = take(4)
    here = dict(zip(INPUTS, take(len(INPUTS)), strict=True))
    below, edges, edges_send, full, edges_back = take(5)
    own_out, below_out, edge_out = take(3)
    x_ref, cot_ref, n1_ref, q_ref, k_ref, v_ref, bias, probs, att_ref = take(9)
    act_ref, dpre_ref, n2_ref, dbb_ref, dbranch_ref, datt_ref, out_ref = take(7)
    dq_ref, dk_ref, dv_ref, d_bias, parts, stage, flat = take(7)
    early_pack, late_pack, table = take(3)
    early_bufs, late_bufs = take(7), take(7)
    load_sem, in_sem, out_sem, early_sem, late_sem = take(5)

    net = Net(n_k, n_l)
    barrier, count = net.greet()
    loads = {
        name: pltpu.make_async_copy(hbm[name], here[name], load_sem.at[i])
        for i, name in enumerate(INPUTS)
    }
    for name in INPUTS:
        loads[name].start()

    early = Section(net, EARLY // net.n_lon, 0, [early_pack, None, *early_bufs, early_out, early_sem])
    late = Section(
        net,
        LATE // net.n_lon,
        TABLE // net.n_lon,
        [late_pack, table, *late_bufs, late_out, late_sem],
    )

    def pick_in(i, name):
        flat_rows = here[name][...].astype(F32).reshape(ROWS, C).astype(BF16)
        edges_send[i] = mm(here["pick_in"][...].astype(BF16), flat_rows).astype(BF16)

    def send_in(i, name):
        corner = net.start(
            edges_send.at[i, EDGE : 2 * EDGE],
            edges.at[i, EDGE : 2 * EDGE],
            (in_sem.at[0, i, 2], in_sem.at[1, i, 2]),
            net.at(-1, -1),
        )
        south = net.start(
            hbm[name].at[:, 0:3], below.at[i], (in_sem.at[0, i, 0], in_sem.at[1, i, 0]), net.at(0, -1)
        )
        east = net.start(
            edges_send.at[i, 0:EDGE],
            edges.at[i, 0:EDGE],
            (in_sem.at[0, i, 1], in_sem.at[1, i, 1]),
            net.at(-1, 0),
        )
        return [south, east, corner]

    def send_out(i):
        corner = net.start(
            edges_back.at[i, EDGE : 2 * EDGE],
            edge_out.at[i, EDGE : 2 * EDGE],
            (out_sem.at[0, i, 2], out_sem.at[1, i, 2]),
            net.at(1, 1),
        )
        north = net.start(
            full.at[i], below_out.at[i], (out_sem.at[0, i, 0], out_sem.at[1, i, 0]), net.at(0, 1)
        )
        west = net.start(
            edges_back.at[i, 0:EDGE],
            edge_out.at[i, 0:EDGE],
            (out_sem.at[0, i, 1], out_sem.at[1, i, 1]),
            net.at(1, 0),
        )
        return [north, west, corner]

    loads["fields"].wait()
    loads["pick_in"].wait()
    pick_in(0, "fields")
    pl.semaphore_wait(barrier, count)
    in_copies = [send_in(0, "fields")]
    for name in INPUTS:
        if name not in ("fields", "pick_in"):
            loads[name].wait()

    last = (net.lat == n_l - 1).astype(F32)
    expand_bias(here["bias_table"], here["spread"], here["masks"], parts, flat, stage, bias, last)

    pick_in(1, "cotangent")
    heads32 = here["heads"][...]
    heads = heads32.astype(BF16)
    scale = 32**-0.5
    gain1 = here["gain_one"][...]
    gain2 = here["gain_two"][...]
    w_qkv, w_proj, w_in, w_out = here["w_qkv"], here["w_proj"], here["w_in"], here["w_out"]

    for c in in_copies[0]:
        c.wait_recv()
    in_copies.append(send_in(1, "cotangent"))
    gather_all(here["fields"], below.at[0], edges.at[0], here["place_in"], here["edge_in"], x_ref)
    unit, _ = norm(x_ref[...])
    n1 = (unit * gain1).astype(BF16)
    n1_ref[...] = n1
    for i, ref in enumerate((q_ref, k_ref, v_ref)):
        ref[...] = mm(n1, w_qkv[:, i * C : (i + 1) * C]).astype(BF16)

    def attend(w, carry):
        rows = pl.ds(pl.multiple_of(w * TOK, TOK), TOK)
        stacked = split_heads(q_ref[rows, :], heads)
        scores = mm_nt(stacked, k_ref[rows, :]) * scale + bias[w // 2]
        top = jnp.max(scores, axis=-1, keepdims=True)
        exps = jnp.exp(scores - top)
        prob = exps * (1.0 / jnp.sum(exps, axis=-1, keepdims=True))
        probs[w] = prob
        mixed = mm(prob.astype(BF16), v_ref[rows, :])
        att_ref[rows, :] = join_heads(mixed, heads32).astype(BF16)
        return carry

    lax.fori_loop(0, WIN, attend, 0, unroll=True)

    for c in in_copies[1]:
        c.wait_recv()
    gather_all(
        here["cotangent"], below.at[1], edges.at[1], here["place_in"], here["edge_in"], cot_ref
    )
    half = ROWS // 2

    def feed(i, gain_sum):
        rows = pl.ds(pl.multiple_of(i * half, half), half)
        branch = x_ref[rows, :] + mm(att_ref[rows, :], w_proj[...])
        unit, inverse = norm(branch)
        n2 = (unit * gain2).astype(BF16)
        n2_ref[rows, :] = n2
        pre = mm(n2, w_in[...])
        cdf = 0.5 + 0.5 * lax.erf(pre * (0.5**0.5))
        slope = cdf + pre * (jnp.exp(-0.5 * pre * pre) * ((2.0 * np.pi) ** -0.5))
        act = (pre * cdf).astype(BF16)
        act_ref[rows, :] = act
        out_ref[rows, :] = branch + mm_nt(act, w_out[...])
        cot = cot_ref[rows, :]
        d_pre = (slope * mm(cot, w_out[...])).astype(BF16)
        dpre_ref[rows, :] = d_pre
        d_normed = mm_nt(d_pre, w_in[...])
        d_branch = cot.astype(F32) + norm_grad(d_normed, gain2, unit, inverse)
        dbranch_ref[rows, :] = d_branch
        dbb = d_branch.astype(BF16)
        dbb_ref[rows, :] = dbb
        datt_ref[rows, :] = mm_nt(dbb, w_proj[...]).astype(BF16)
        return gain_sum + jnp.sum(d_normed * unit, axis=0, keepdims=True)

    gain_sum2 = lax.fori_loop(0, 2, feed, jnp.zeros((1, C), F32), unroll=True)

    late_pack[448:LATE, :] = jnp.zeros((LATE - 448, 256), F32)
    late_pack[456:457, 0:C] = gain_sum2
    for i in range(3):
        cols = slice(i * 256, (i + 1) * 256)
        early_pack[i * C : (i + 1) * C, :] = mm_tn(cot_ref[...], act_ref[:, cols])
        early_pack[576 + i * C : 576 + (i + 1) * C, :] = mm_tn(n2_ref[...], dpre_ref[:, cols])
    grad = mm_tn(att_ref[...], dbb_ref[...])
    early_pack[1152:EARLY, 0:C] = grad[0:128, :]
    late_pack[432:448, 0:C] = grad[128:TOK, :]
    early_pack[1152:1200, C:256] = grad[TOK:C, 0:64]
    early_pack[1200:1248, C:256] = grad[TOK:C, 64:128]
    early_pack[1248:EARLY, C:256] = grad[TOK:176, 128:C]
    late_pack[432:448, C:256] = grad[176:C, 128:C]
    early.to_pair()
    scatter_all(
        out_ref, here["place_out"], here["pick_out"], own_out.at[0], full.at[0], edges_back.at[0]
    )
    out_copies = send_out(0)

    early.to_lon()
    d_bias[...] = jnp.zeros_like(d_bias)

    def attend_back(w, carry):
        rows = pl.ds(pl.multiple_of(w * TOK, TOK), TOK)
        prob = probs[w]
        d_stacked = split_heads(datt_ref[rows, :], heads)
        d_prob = mm_nt(d_stacked, v_ref[rows, :])
        d_score = prob * (d_prob - jnp.sum(d_prob * prob, axis=-1, keepdims=True))
        for h in range(HEADS):
            group = pl.ds(pl.multiple_of((2 * h + w // 2) * TOK, TOK), TOK)
            part = d_score[h * TOK : (h + 1) * TOK, :]
            d_bias[0, group, :] += part[:, 0:128]
            d_bias[1, group, 0:16] += part[:, 128:144]
        d_score_b = d_score.astype(BF16)
        dv_ref[rows, :] = mm_tn(prob.astype(BF16), d_stacked).astype(BF16)
        dq_ref[rows, :] = (join_heads(mm(d_score_b, k_ref[rows, :]), heads32) * scale).astype(BF16)
        stacked = split_heads(q_ref[rows, :], heads)
        dk_ref[rows, :] = (mm_tn(d_score_b, stacked) * scale).astype(BF16)
        return carry

    lax.fori_loop(0, WIN, attend_back, 0, unroll=2)
    pieces = EARLY // net.n_lon // 16

    d_normed = None
    for i, ref in enumerate((dq_ref, dk_ref, dv_ref)):
        grad = mm_tn(n1_ref[...], ref[...])
        late_pack[i * TOK : (i + 1) * TOK, 0:C] = grad[0:TOK, :]
        for j in range(3):
            rows = slice(i * TOK + j * 48, i * TOK + (j + 1) * 48)
            late_pack[rows, C:256] = grad[TOK:C, j * 64 : (j + 1) * 64]
        term = mm_nt(ref[...], w_qkv[:, i * C : (i + 1) * C])
        d_normed = term if d_normed is None else d_normed + term
    unit, inverse = norm(x_ref[...])
    late_pack[448:449, 0:C] = jnp.sum(d_normed * unit, axis=0, keepdims=True)
    out_ref[...] = dbranch_ref[...] + norm_grad(d_normed, gain1, unit, inverse)
    reduce_table(d_bias, here["spread"], parts, flat, table)
    late.to_pair()
    scatter_all(
        out_ref, here["place_out"], here["pick_out"], own_out.at[1], full.at[1], edges_back.at[1]
    )
    late.to_lon()
    early.to_owner(pieces)
    out_copies += send_out(1)

    def merge(i, target):
        for c in out_copies[3 * i : 3 * i + 3]:
            c.wait_recv()
        place = here["place_end"][...].astype(BF16)
        for lev in range(4):
            rows = [
                below_out[i, lev].astype(F32).reshape(72, C),
                own_out[i, lev].astype(F32).reshape(72, C),
            ]
            value = mm(place, jnp.concatenate(rows, axis=0).astype(BF16))
            value = value + mm(here["edge_end"][lev].astype(BF16), edge_out[i])
            target[(lev + 1) % 4] = value.reshape(6, 24, C).astype(BF16)

    merge(0, block_out)
    early.from_owner(pieces)
    late.to_lat()
    early.after_owner(pieces)
    late.from_lat()
    early.spread_pair()
    late.spread_pair()
    merge(1, grad_fields)
    early.close()
    late.close()
    early.close_owner(pieces)
    for c in net.started:
        c.wait_send()


def finish_kernel(n_k, *refs):
    hbm, outs, here = refs[0:4], refs[4:13], refs[13:17]
    early_rows, late_rows = refs[17:19]
    g_gain_one, g_w_qkv, g_table, g_w_proj, g_gain_two = refs[19:24]
    load_sem, store_sem = refs[24:26]
    loads = [pltpu.make_async_copy(hbm[i], here[i], load_sem.at[i]) for i in range(4)]
    for c in loads:
        c.start()
    early, late = here[0:2]
    out_w_in, out_w_out = outs[7], outs[8]
    stores = []

    def store(source, target):
        c = pltpu.make_async_copy(source, target, store_sem.at[len(stores)])
        c.start()
        stores.append(c)

    n_lon = 2 * n_k
    chunk = EARLY // n_lon
    loads[0].wait()
    for part in range(n_lon):
        early_rows[part * chunk : (part + 1) * chunk, :] = early[part % 2, part // 2].astype(F32)
    for i in range(3):
        cols = slice(i * 256, (i + 1) * 256)
        store(early_rows.at[i * C : (i + 1) * C, :], out_w_out.at[:, cols])
        store(early_rows.at[576 + i * C : 576 + (i + 1) * C, :], out_w_in.at[:, cols])
    for i in range(2):
        loads[2 + i].wait()
        store(here[2 + i], outs[i])
    loads[1].wait()
    rest, chunk = TABLE // n_lon, LATE // n_lon
    for part in range(n_lon):
        late_rows[part * chunk : (part + 1) * chunk, :] = late[
            part % 2, part // 2, 0:chunk, :
        ].astype(F32)
    for i in range(3):
        g_w_qkv[0:TOK, i * C : (i + 1) * C] = late_rows[i * TOK : (i + 1) * TOK, 0:C]
        for j in range(3):
            cols = slice(i * C + j * 64, i * C + (j + 1) * 64)
            g_w_qkv[TOK:C, cols] = late_rows[i * TOK + j * 48 : i * TOK + (j + 1) * 48, C:256]
    store(g_w_qkv, outs[3])
    g_w_proj[0:128, :] = early_rows[1152:EARLY, 0:C]
    g_w_proj[128:TOK, :] = late_rows[432:448, 0:C]
    g_w_proj[TOK:C, 0:64] = early_rows[1152:1200, C:256]
    g_w_proj[TOK:C, 64:128] = early_rows[1200:1248, C:256]
    g_w_proj[TOK:176, 128:C] = early_rows[1248:EARLY, C:256]
    g_w_proj[176:C, 128:C] = late_rows[432:448, C:256]
    store(g_w_proj, outs[5])
    g_gain_one[...] = late_rows[448:449, 0:C]
    store(g_gain_one, outs[2])
    g_gain_two[...] = late_rows[456:457, 0:C]
    store(g_gain_two, outs[6])
    for part in range(13):
        width = min(256, POS - part * 256)
        place, offset = divmod(part * 16, rest)
        value = late[place % 2, place // 2, chunk + offset : chunk + offset + 16, :].astype(F32)
        for h in range(HEADS):
            g_table[0, h, :, part * 256 : part * 256 + width] = value[2 * h : 2 * h + 2, 0:width]
    store(g_table, outs[4])
    for c in stores:
        c.wait()


def local(n_k, n_l, fields, cotangent, bias_table, gain_one, w_qkv, w_proj, gain_two, w_in, w_out):
    n_lon = 2 * n_k
    sds = jax.ShapeDtypeStruct
    vmem = pltpu.VMEM
    dma = pltpu.SemaphoreType.DMA
    whole = pl.BlockSpec(memory_space=pltpu.VMEM)
    apart = pl.BlockSpec(memory_space=pl.ANY)
    early, late = EARLY // n_lon, LATE // n_lon
    both = late + TABLE // n_lon
    inputs = (
        fields,
        cotangent,
        bias_table.transpose(0, 2, 1, 3),
        gain_one.reshape(1, C),
        w_qkv,
        w_proj,
        gain_two.reshape(1, C),
        w_in,
        w_out.T,
        jnp.asarray(place_level_in()),
        jnp.asarray(place_edge_in()),
        jnp.asarray(pick_edge_in()),
        jnp.asarray(place_level_out()),
        jnp.asarray(pick_edge_out()),
        jnp.asarray(spread_matrix()),
        jnp.asarray(region_masks()),
        jnp.asarray(head_masks()),
        jnp.asarray(place_level_end()),
        jnp.asarray(place_edge_end()),
    )

    def buffers(chunk, kept):
        return [
            vmem((n_k, chunk, 256), BF16),
            vmem((n_k, chunk, 256), BF16),
            vmem((n_k - 1, chunk, 256), BF16),
            vmem((n_k - 1, chunk, 256), BF16),
            vmem((chunk, 256), F32),
            vmem((n_l, kept, 256), BF16),
            vmem((n_l, 16, 256), BF16),
        ]

    slots = max(n_k, n_l)
    results = pl.pallas_call(
        functools.partial(block_kernel, n_k, n_l),
        out_shape=(
            sds((2, n_k, early, 256), BF16),
            sds((2, n_k, both, 256), BF16),
            sds((4, 6, 24, C), BF16),
            sds((4, 6, 24, C), BF16),
        ),
        in_specs=[apart] * len(INPUTS),
        out_specs=[whole] * 4,
        scratch_shapes=[vmem(value.shape, value.dtype) for value in inputs]
        + [
            vmem((2, 4, 3, 24, C), BF16),
            vmem((2, 2 * EDGE, C), BF16),
            vmem((2, 2 * EDGE, C), BF16),
            vmem((2, 4, 3, 24, C), BF16),
            vmem((2, 2 * EDGE, C), BF16),
            vmem((2, 4, 3, 24, C), BF16),
            vmem((2, 4, 3, 24, C), BF16),
            vmem((2, 2 * EDGE, C), BF16),
            vmem((ROWS, C), F32),
            vmem((ROWS, C), BF16),
            vmem((ROWS, C), BF16),
            vmem((ROWS, C), BF16),
            vmem((ROWS, C), BF16),
            vmem((ROWS, C), BF16),
            vmem((2, STACK, TOK), F32),
            vmem((WIN, STACK, TOK), F32),
            vmem((ROWS, C), BF16),
            vmem((ROWS, FFH), BF16),
            vmem((ROWS, FFH), BF16),
            vmem((ROWS, C), BF16),
            vmem((ROWS, C), BF16),
            vmem((ROWS, C), F32),
            vmem((ROWS, C), BF16),
            vmem((ROWS, C), F32),
            vmem((ROWS, C), BF16),
            vmem((ROWS, C), BF16),
            vmem((ROWS, C), BF16),
            vmem((2, 2 * STACK, 128), F32),
            vmem((4, TOK, 128), F32),
            vmem((2, 2 * STACK, 128), F32),
            vmem((16, 4096), F32),
            vmem((EARLY, 256), F32),
            vmem((LATE, 256), F32),
            vmem((TABLE, 256), F32),
        ]
        + buffers(early, 16)
        + buffers(both, late)
        + [
            dma((len(INPUTS),)),
            dma((2, 2, 3)),
            dma((2, 2, 3)),
            dma((12, slots)),
            dma((12, slots)),
        ],
        compiler_params=pltpu.CompilerParams(
            collective_id=0, has_side_effects=True, vmem_limit_bytes=60 * 1024 * 1024
        ),
        name="block",
    )(*inputs)
    shapes = (
        sds((4, 6, 24, C), BF16),
        sds((4, 6, 24, C), BF16),
        sds((1, C), F32),
        sds((C, 3 * C), F32),
        sds((1, HEADS, 2, POS), F32),
        sds((C, C), F32),
        sds((1, C), F32),
        sds((C, FFH), F32),
        sds((C, FFH), F32),
    )
    outs = pl.pallas_call(
        functools.partial(finish_kernel, n_k),
        out_shape=shapes,
        in_specs=[apart] * 4,
        out_specs=[apart] * 9,
        scratch_shapes=[vmem(value.shape, value.dtype) for value in results]
        + [vmem((EARLY, 256), F32), vmem((LATE, 256), F32)]
        + [vmem(value.shape, value.dtype) for value in shapes[2:7]]
        + [dma((4,)), dma((13,))],
        compiler_params=pltpu.CompilerParams(vmem_limit_bytes=60 * 1024 * 1024),
        name="finish",
    )(*results)
    outs = list(outs)
    outs[2] = outs[2].reshape(C)
    outs[4] = outs[4].transpose(0, 2, 1, 3)
    outs[6] = outs[6].reshape(C)
    outs[8] = outs[8].T
    return tuple(outs)


def solution(mesh):
    n_k, n_l = mesh.shape["lon"] // 2, mesh.shape["lat"]
    placed = (
        P(None, "lat", "lon", None),
        P(None, "lat", "lon", None),
        P("lat", None, None, None),
    ) + (P(),) * 6
    return jax.shard_map(
        functools.partial(local, n_k, n_l),
        mesh=mesh,
        in_specs=placed,
        out_specs=(
            P(None, "lat", "lon", None),
            P(None, "lat", "lon", None),
            P(),
            P(),
            P("lat", None, None, None),
            P(),
            P(),
            P(),
            P(),
        ),
        check_vma=False,
    )
```

```python
import functools

import jax
import jax.numpy as jnp
import numpy as np
from jax import lax
from jax.experimental import pallas as pl
from jax.experimental.pallas import tpu as pltpu
from jax.sharding import PartitionSpec as P

HEADS = 6
C = 192
FFH = 768
TOK = 144
WIN = 4
ROWS = WIN * TOK
STACK = HEADS * TOK
POS = 3312
SEG = 138
EARLY = 1280
LATE = 512
TABLE = 256
EDGE = 80
MESH = pl.DeviceIdType.MESH
F32 = jnp.float32
BF16 = jnp.bfloat16


def window_row(lev, lat, col):
    return ((lev // 2) * 2 + col // 12) * TOK + (lev % 2) * 72 + lat * 12 + col % 12


def place_level_in():
    out = np.zeros((TOK, TOK), np.float32)
    for lat in range(6):
        for col in range(18):
            out[col // 12 * 72 + lat * 12 + col % 12, lat * 24 + col + 6] = 1
    return out


def edge_row(lev, lat, col):
    return (0 if lat < 3 else EDGE) + lev * 18 + lat % 3 * 6 + col


def place_edge_in():
    out = np.zeros((4, TOK, 2 * EDGE), np.float32)
    for lev in range(4):
        for lat in range(6):
            for col in range(6):
                out[lev, 72 + lat * 12 + 6 + col, edge_row((lev + 1) % 4, lat, col)] = 1
    return out


def pick_edge_in():
    out = np.zeros((2 * EDGE, ROWS), np.float32)
    for lev in range(4):
        for lat in range(6):
            for col in range(6):
                out[edge_row(lev, (lat + 3) % 6, col), (lev * 6 + lat) * 24 + col] = 1
    return out


def place_level_out():
    out = np.zeros((TOK, TOK), np.float32)
    for lat in range(6):
        for col in range(24):
            out[lat * 24 + col, col // 12 * 72 + lat * 12 + col % 12] = 1
    return out


def pick_edge_out():
    out = np.zeros((2 * EDGE, ROWS), np.float32)
    for lev in range(4):
        for lat in range(6):
            for col in range(6):
                out[edge_row(lev, lat, col), window_row(lev, lat, 18 + col)] = 1
    return out


def place_level_end():
    out = np.zeros((TOK, TOK), np.float32)
    for lat in range(6):
        for lon in range(6, 24):
            out[lat * 24 + lon, lat * 24 + lon - 6] = 1
    return out


def place_edge_end():
    out = np.zeros((4, TOK, 2 * EDGE), np.float32)
    for lev in range(4):
        for lat in range(6):
            for lon in range(6):
                out[lev, lat * 24 + lon, edge_row(lev, (lat + 3) % 6, lon)] = 1
    return out


def spread_matrix():
    out = np.zeros((512, 256), np.float32)
    for level in range(2):
        for lat in range(6):
            for col in range(12):
                out[level * 256 + lat * 23 + 11 - col, level * 72 + lat * 12 + col] = 1
    return out


def region_masks():
    ids = np.arange(TOK)
    level, lat = ids // 72, ids // 12 % 6 >= 3
    out = np.zeros((2, TOK, TOK), np.float32)
    out[0] = level[:, None] != level[None, :]
    out[1] = lat[:, None] != lat[None, :]
    return out


def head_masks():
    out = np.zeros((8, C), np.float32)
    for head in range(HEADS):
        out[head, head * 32 : head * 32 + 32] = 1
    return out


def mm(left, right):
    return lax.dot_general(left, right, (((1,), (0,)), ((), ())), preferred_element_type=F32)


def mm_nt(left, right):
    return lax.dot_general(left, right, (((1,), (1,)), ((), ())), preferred_element_type=F32)


def mm_tn(left, right):
    return lax.dot_general(left, right, (((0,), (0,)), ((), ())), preferred_element_type=F32)


def norm(values):
    center = values - jnp.mean(values, axis=-1, keepdims=True)
    spread = jnp.mean(center * center, axis=-1, keepdims=True)
    inverse = lax.rsqrt(spread + 1e-05)
    return center * inverse, inverse


def norm_grad(d_normed, gain, unit, inverse):
    d_unit = d_normed * gain
    mean_one = jnp.mean(d_unit, axis=-1, keepdims=True)
    mean_two = jnp.mean(d_unit * unit, axis=-1, keepdims=True)
    return inverse * (d_unit - mean_one - unit * mean_two)


def split_heads(value, heads):
    return jnp.concatenate([value * heads[h : h + 1, :] for h in range(HEADS)], axis=0)


def join_heads(stacked, heads):
    total = stacked[0:TOK, :] * heads[0:1, :]
    for h in range(1, HEADS):
        total = total + stacked[h * TOK : (h + 1) * TOK, :] * heads[h : h + 1, :]
    return total


def segment(cell, other):
    return ((2 * (cell // 6) + other) * 36 + 6 * (cell % 6)) * 23


def segment(cell, other):
    return ((2 * (cell // 6) + other) * 36 + 6 * (cell % 6)) * 23


def expand_bias(bias_ref, spread_ref, masks_ref, parts, flat, stage, bias, last):
    flat[...] = jnp.zeros_like(flat)
    for h in range(HEADS):
        flat[2 * h : 2 * h + 2, 0:POS] = bias_ref[0, h]
    for cell in range(12):
        for other in range(2):
            start = segment(cell, other)
            for half in range(2):
                parts[2 * other + half, pl.ds(cell, 12, stride=12), :] = flat[
                    0:12, start + half * 128 : start + half * 128 + 128
                ]
    for step in range(12):
        total = None
        for other in range(2):
            value = jnp.concatenate([parts[2 * other], parts[2 * other + 1]], axis=1)
            if step:
                value = pltpu.roll(value, 256 - step, 1)
            matrix = spread_ref[other * 256 : (other + 1) * 256, :].astype(BF16)
            for _ in range(3):
                part = value.astype(BF16)
                value = value - part.astype(F32)
                term = mm(part, matrix)
                total = term if total is None else total + term
        for half in range(2):
            stage[half, pl.ds(step, TOK, stride=12), :] = total[:, half * 128 : half * 128 + 128]
    for lev in range(2):
        closed = masks_ref[1] * last
        if lev == 1:
            closed = closed + masks_ref[0]
        for h in range(HEADS):
            rows = slice((2 * h + lev) * TOK, (2 * h + lev + 1) * TOK)
            value = jnp.concatenate([stage[0, rows, :], stage[1, rows, 0:16]], axis=1)
            bias[lev, h * TOK : (h + 1) * TOK, :] = jnp.where(closed > 0.5, -1000000000.0, value)


def reduce_table(d_bias, spread_ref, parts, flat, table):
    value = jnp.concatenate(
        [
            jnp.concatenate(
                [d_bias[half, pl.ds(step, TOK, stride=12), :] for half in range(2)], axis=1
            )
            for step in range(12)
        ],
        axis=0,
    ).astype(BF16)
    sums = []
    for other in range(2):
        terms = mm_nt(value, spread_ref[other * 256 : (other + 1) * 256, :].astype(BF16))
        total = terms[0:TOK, :]
        for step in range(1, 12):
            total = total + pltpu.roll(terms[step * TOK : (step + 1) * TOK, :], step, 1)
        sums.append(total)
    for other in range(2):
        for half in range(2):
            parts[2 * other + half] = sums[other][:, half * 128 : half * 128 + 128]
    flat[...] = jnp.zeros_like(flat)
    for cell in range(12):
        for other in range(2):
            start = segment(cell, other)
            rows = pl.ds(cell, 12, stride=12)
            flat[0:12, start : start + 128] = parts[2 * other, rows, :]
            flat[0:12, start + 128 : start + SEG] = parts[2 * other + 1, rows, :][:, 0 : SEG - 128]
    for part in range(16):
        table[part * 16 : (part + 1) * 16, :] = flat[:, part * 256 : (part + 1) * 256]


def gather_all(own, below, edges, place, place_edge, out):
    place = place[...].astype(BF16)
    for lev in range(4):
        source = (lev + 1) % 4
        parts = [
            own[source, 3:6].astype(F32).reshape(72, C),
            below[source].astype(F32).reshape(72, C),
        ]
        rows = mm(place, jnp.concatenate(parts, axis=0).astype(BF16))
        rows = rows + mm(place_edge[lev].astype(BF16), edges[...])
        for half in range(2):
            start = ((lev // 2) * 2 + half) * TOK + (lev % 2) * 72
            out[start : start + 72, :] = rows[half * 72 : (half + 1) * 72, :].astype(out.dtype)


def scatter_all(value, place, pick, own, full, edges):
    place = place[...].astype(BF16)
    for lev in range(4):
        parts = []
        for half in range(2):
            start = ((lev // 2) * 2 + half) * TOK + (lev % 2) * 72
            parts.append(value[start : start + 72, :])
        rows = mm(place, jnp.concatenate(parts, axis=0).astype(BF16))
        own[lev] = rows[0:72].reshape(3, 24, C).astype(BF16)
        full[lev] = rows[72:144].reshape(3, 24, C).astype(BF16)
    edges[...] = mm(pick[...].astype(BF16), value[...].astype(BF16)).astype(BF16)


INPUTS = (
    "fields",
    "cotangent",
    "bias_table",
    "gain_one",
    "w_qkv",
    "w_proj",
    "gain_two",
    "w_in",
    "w_out",
    "place_in",
    "edge_in",
    "pick_in",
    "place_out",
    "pick_out",
    "spread",
    "masks",
    "heads",
    "place_end",
    "edge_end",
)


class Section:
    def __init__(self, net, chunk, rest, refs):
        self.net, self.chunk, self.rest = net, chunk, rest
        (
            self.pack,
            self.table,
            self.send_pair,
            self.recv_pair,
            self.send_lon,
            self.recv_lon,
            self.total,
            self.by_lat,
            self.send_lat,
            self.gathered,
            self.sems,
        ) = refs
        self.pair, self.along_lon = [], []

    def rows(self, ref, size, core, k):
        start = pl.multiple_of((2 * k + core) * size, size)
        return ref[pl.ds(start, size), :]

    def sem(self, stage, slot):
        return (self.sems.at[stage, slot], self.sems.at[stage + 1, slot])

    def to_pair(self):
        net = self.net
        for d in range(1, net.n_k + 1):
            k = lax.rem(net.k + d, net.n_k)
            self.send_pair[d - 1, 0 : self.chunk, :] = self.rows(
                self.pack, self.chunk, net.other, k
            ).astype(BF16)
            if self.rest:
                self.send_pair[d - 1, self.chunk : self.chunk + self.rest, :] = self.rows(
                    self.table, self.rest, net.other, k
                ).astype(BF16)
            self.pair.append(
                net.start(
                    self.send_pair.at[d - 1],
                    self.recv_pair.at[d - 1],
                    self.sem(0, d - 1),
                    net.partner,
                )
            )

    def to_lon(self):
        net = self.net
        for d in range(1, net.n_k + 1):
            k = lax.rem(net.k + d, net.n_k)
            self.pair[d - 1].wait_recv()
            value = self.rows(self.pack, self.chunk, net.core, k)
            if self.rest:
                value = jnp.concatenate(
                    [value, self.rows(self.table, self.rest, net.core, k)], axis=0
                )
            value = value + self.recv_pair[d - 1].astype(F32)
            if d == net.n_k:
                self.total[...] = value
                continue
            self.send_lon[d - 1] = value.astype(BF16)
            self.along_lon.append(
                net.start(
                    self.send_lon.at[d - 1],
                    self.recv_lon.at[d - 1],
                    self.sem(2, d - 1),
                    net.along_lon(d),
                )
            )

    def sum_lon(self):
        value = self.total[...]
        for d in range(1, self.net.n_k):
            self.along_lon[d - 1].wait_recv()
            value = value + self.recv_lon[d - 1].astype(F32)
        return value.astype(BF16)

    def sum_lat(self):
        value = self.by_lat[0].astype(F32)
        for i in range(1, self.net.n_l):
            value = value + self.by_lat[i].astype(F32)
        return value.astype(BF16)

    def spread_lon(self):
        net = self.net
        mine = self.gathered.at[net.core, net.k]
        for d in range(1, net.n_k):
            net.start(mine, mine, self.sem(8, d - 1), net.along_lon(d))
        net.start(mine, mine, self.sem(10, 0), net.partner)

    def to_lat(self):
        net = self.net
        value = self.sum_lon()
        mine = self.by_lat.at[net.lat]
        mine[...] = value[0 : self.chunk, :]
        self.gathered[net.core, net.k, self.chunk : self.chunk + self.rest, :] = value[
            self.chunk : self.chunk + self.rest, :
        ]
        for d in range(1, net.n_l):
            net.start(mine, mine, self.sem(4, d - 1), net.along_lat(d))

    def from_lat(self):
        net = self.net
        for d in range(1, net.n_l):
            theirs = self.by_lat.at[lax.rem(net.lat - d + net.n_l, net.n_l)]
            net.copy(theirs, theirs, self.sem(4, d - 1), net.partner).wait_recv()
        self.gathered[net.core, net.k, 0 : self.chunk, :] = self.sum_lat()
        self.spread_lon()

    def to_owner(self, pieces):
        net = self.net
        value = self.sum_lon()
        for p in range(pieces):
            pieces_ref = self.send_lat.at[p]
            pieces_ref[...] = value[p * 16 : (p + 1) * 16, :]

            @pl.when(net.lat != p)
            def _(p=p):
                self.owner_copy(p).start()

    def owner_copy(self, p):
        net = self.net
        sems = (self.sems.at[4, p], self.sems.at[5, net.lat])
        return net.copy(self.send_lat.at[p], self.by_lat.at[net.lat], sems, (net.lon, p))

    def own_piece(self):
        net = self.net
        return self.gathered.at[net.core, net.k, pl.ds(pl.multiple_of(net.lat * 16, 16), 16), :]

    def back_copy(self, d):
        net = self.net
        sems = (self.sems.at[6, d - 1], self.sems.at[7, net.lat])
        return net.copy(self.own_piece(), self.own_piece(), sems, net.along_lat(d))

    def from_owner(self, pieces):
        net = self.net

        @pl.when(net.lat < pieces)
        def _():
            self.by_lat[net.lat] = self.send_lat[net.lat]
            for d in range(1, net.n_l):
                source = lax.rem(net.lat + d, net.n_l)
                theirs = self.by_lat.at[source]
                sems = (self.sems.at[4, 0], self.sems.at[5, source])
                net.copy(theirs, theirs, sems, net.partner).wait_recv()
            self.own_piece()[...] = self.sum_lat()
            for d in range(1, net.n_l):
                self.back_copy(d).start()

    def after_owner(self, pieces):
        net = self.net
        for p in range(pieces):

            @pl.when(net.lat != p)
            def _(p=p):
                theirs = self.gathered.at[net.core, net.k, p * 16 : (p + 1) * 16, :]
                sems = (self.sems.at[6, 0], self.sems.at[7, p])
                net.copy(theirs, theirs, sems, net.partner).wait_recv()

        self.spread_lon()

    def close_owner(self, pieces):
        net = self.net
        for p in range(pieces):

            @pl.when(net.lat != p)
            def _(p=p):
                self.owner_copy(p).wait_send()

        @pl.when(net.lat < pieces)
        def _():
            for d in range(1, net.n_l):
                self.back_copy(d).wait_send()

    def spread_pair(self):
        net = self.net
        for d in range(1, net.n_k):
            theirs = self.gathered.at[net.core, lax.rem(net.k - d + net.n_k, net.n_k)]
            net.copy(theirs, theirs, self.sem(8, d - 1), net.partner).wait_recv()
            net.start(theirs, theirs, self.sem(10, d), net.partner)

    def close(self):
        net = self.net
        for d in range(net.n_k):
            theirs = self.gathered.at[net.other, lax.rem(net.k - d + net.n_k, net.n_k)]
            net.copy(theirs, theirs, self.sem(10, d), net.partner).wait_recv()


class Net:
    def __init__(self, n_k, n_l):
        self.n_k, self.n_l = n_k, n_l
        self.n_lon = 2 * n_k
        self.lon, self.lat = lax.axis_index("lon"), lax.axis_index("lat")
        self.core, self.k = lax.rem(self.lon, 2), self.lon // 2
        self.other = 1 - self.core
        self.partner = (2 * self.k + self.other, self.lat)
        self.started = []

    def at(self, d_lon, d_lat):
        return (
            lax.rem(self.lon + d_lon + self.n_lon, self.n_lon),
            lax.rem(self.lat + d_lat + self.n_l, self.n_l),
        )

    def along_lon(self, d):
        return (2 * lax.rem(self.k + d, self.n_k) + self.core, self.lat)

    def along_lat(self, d):
        return self.at(0, d)

    def greet(self):
        far = lax.rem(self.lon + 2 * self.core - 1 + self.n_lon, self.n_lon)
        friends = [self.partner, (far, self.lat), self.at(1, 1), self.at(-1, -1)]
        friends += [self.along_lon(d) for d in range(1, self.n_k)]
        friends += [self.along_lat(d) for d in range(1, self.n_l)]
        barrier = pltpu.get_barrier_semaphore()
        for friend in friends:
            pl.semaphore_signal(barrier, inc=1, device_id=friend, device_id_type=MESH)
        return barrier, len(friends)

    def copy(self, source, target, sems, device):
        return pltpu.make_async_remote_copy(
            src_ref=source,
            dst_ref=target,
            send_sem=sems[0],
            recv_sem=sems[1],
            device_id=device,
            device_id_type=MESH,
        )

    def start(self, source, target, sems, device):
        c = self.copy(source, target, sems, device)
        c.start()
        self.started.append(c)
        return c


def block_kernel(n_k, n_l, *refs):
    refs = list(refs)

    def take(count):
        out = refs[:count]
        del refs[:count]
        return out

    hbm = dict(zip(INPUTS, take(len(INPUTS)), strict=True))
    early_out, late_out, block_out, grad_fields = take(4)
    here = dict(zip(INPUTS, take(len(INPUTS)), strict=True))
    below, edges, edges_send, full, edges_back = take(5)
    own_out, below_out, edge_out = take(3)
    x_ref, cot_ref, n1_ref, q_ref, k_ref, v_ref, bias, probs, att_ref = take(9)
    act_ref, dpre_ref, n2_ref, dbb_ref, dbranch_ref, datt_ref, out_ref = take(7)
    dq_ref, dk_ref, dv_ref, d_bias, parts, stage, flat = take(7)
    early_pack, late_pack, table = take(3)
    early_bufs, late_bufs = take(7), take(7)
    load_sem, in_sem, out_sem, early_sem, late_sem = take(5)

    net = Net(n_k, n_l)
    barrier, count = net.greet()
    loads = {
        name: pltpu.make_async_copy(hbm[name], here[name], load_sem.at[i])
        for i, name in enumerate(INPUTS)
    }
    for name in INPUTS:
        loads[name].start()

    early = Section(net, EARLY // net.n_lon, 0, [early_pack, None, *early_bufs, early_out, early_sem])
    late = Section(
        net,
        LATE // net.n_lon,
        TABLE // net.n_lon,
        [late_pack, table, *late_bufs, late_out, late_sem],
    )

    def pick_in(i, name):
        flat_rows = here[name][...].astype(F32).reshape(ROWS, C).astype(BF16)
        edges_send[i] = mm(here["pick_in"][...].astype(BF16), flat_rows).astype(BF16)

    def send_in(i, name):
        corner = net.start(
            edges_send.at[i, EDGE : 2 * EDGE],
            edges.at[i, EDGE : 2 * EDGE],
            (in_sem.at[0, i, 2], in_sem.at[1, i, 2]),
            net.at(-1, -1),
        )
        south = net.start(
            hbm[name].at[:, 0:3], below.at[i], (in_sem.at[0, i, 0], in_sem.at[1, i, 0]), net.at(0, -1)
        )
        east = net.start(
            edges_send.at[i, 0:EDGE],
            edges.at[i, 0:EDGE],
            (in_sem.at[0, i, 1], in_sem.at[1, i, 1]),
            net.at(-1, 0),
        )
        return [south, east, corner]

    def send_out(i):
        corner = net.start(
            edges_back.at[i, EDGE : 2 * EDGE],
            edge_out.at[i, EDGE : 2 * EDGE],
            (out_sem.at[0, i, 2], out_sem.at[1, i, 2]),
            net.at(1, 1),
        )
        north = net.start(
            full.at[i], below_out.at[i], (out_sem.at[0, i, 0], out_sem.at[1, i, 0]), net.at(0, 1)
        )
        west = net.start(
            edges_back.at[i, 0:EDGE],
            edge_out.at[i, 0:EDGE],
            (out_sem.at[0, i, 1], out_sem.at[1, i, 1]),
            net.at(1, 0),
        )
        return [north, west, corner]

    loads["fields"].wait()
    loads["pick_in"].wait()
    pick_in(0, "fields")
    pl.semaphore_wait(barrier, count)
    in_copies = [send_in(0, "fields")]
    loads["cotangent"].wait()
    pick_in(1, "cotangent")
    in_copies.append(send_in(1, "cotangent"))
    for name in INPUTS:
        if name not in ("fields", "cotangent", "pick_in"):
            loads[name].wait()

    last = (net.lat == n_l - 1).astype(F32)
    expand_bias(here["bias_table"], here["spread"], here["masks"], parts, flat, stage, bias, last)

    heads32 = here["heads"][...]
    heads = heads32.astype(BF16)
    scale = 32**-0.5
    gain1 = here["gain_one"][...]
    gain2 = here["gain_two"][...]
    w_qkv, w_proj, w_in, w_out = here["w_qkv"], here["w_proj"], here["w_in"], here["w_out"]

    for c in in_copies[0]:
        c.wait_recv()
    gather_all(here["fields"], below.at[0], edges.at[0], here["place_in"], here["edge_in"], x_ref)
    unit, _ = norm(x_ref[...])
    n1 = (unit * gain1).astype(BF16)
    n1_ref[...] = n1
    for i, ref in enumerate((q_ref, k_ref, v_ref)):
        ref[...] = mm(n1, w_qkv[:, i * C : (i + 1) * C]).astype(BF16)

    def attend(w, carry):
        rows = pl.ds(pl.multiple_of(w * TOK, TOK), TOK)
        stacked = split_heads(q_ref[rows, :], heads)
        scores = mm_nt(stacked, k_ref[rows, :]) * scale + bias[w // 2]
        top = jnp.max(scores, axis=-1, keepdims=True)
        exps = jnp.exp(scores - top)
        prob = exps * (1.0 / jnp.sum(exps, axis=-1, keepdims=True))
        probs[w] = prob
        mixed = mm(prob.astype(BF16), v_ref[rows, :])
        att_ref[rows, :] = join_heads(mixed, heads32).astype(BF16)
        return carry

    lax.fori_loop(0, WIN, attend, 0, unroll=True)

    for c in in_copies[1]:
        c.wait_recv()
    gather_all(
        here["cotangent"], below.at[1], edges.at[1], here["place_in"], here["edge_in"], cot_ref
    )
    half = ROWS // 2

    def feed(i, gain_sum):
        rows = pl.ds(pl.multiple_of(i * half, half), half)
        branch = x_ref[rows, :] + mm(att_ref[rows, :], w_proj[...])
        unit, inverse = norm(branch)
        n2 = (unit * gain2).astype(BF16)
        n2_ref[rows, :] = n2
        pre = mm(n2, w_in[...])
        cdf = 0.5 + 0.5 * lax.erf(pre * (0.5**0.5))
        slope = cdf + pre * (jnp.exp(-0.5 * pre * pre) * ((2.0 * np.pi) ** -0.5))
        act = (pre * cdf).astype(BF16)
        act_ref[rows, :] = act
        out_ref[rows, :] = branch + mm_nt(act, w_out[...])
        cot = cot_ref[rows, :]
        d_pre = (slope * mm(cot, w_out[...])).astype(BF16)
        dpre_ref[rows, :] = d_pre
        d_normed = mm_nt(d_pre, w_in[...])
        d_branch = cot.astype(F32) + norm_grad(d_normed, gain2, unit, inverse)
        dbranch_ref[rows, :] = d_branch
        dbb = d_branch.astype(BF16)
        dbb_ref[rows, :] = dbb
        datt_ref[rows, :] = mm_nt(dbb, w_proj[...]).astype(BF16)
        return gain_sum + jnp.sum(d_normed * unit, axis=0, keepdims=True)

    gain_sum2 = lax.fori_loop(0, 2, feed, jnp.zeros((1, C), F32), unroll=True)

    late_pack[448:LATE, :] = jnp.zeros((LATE - 448, 256), F32)
    late_pack[456:457, 0:C] = gain_sum2
    for i in range(3):
        cols = slice(i * 256, (i + 1) * 256)
        early_pack[i * C : (i + 1) * C, :] = mm_tn(cot_ref[...], act_ref[:, cols])
        early_pack[576 + i * C : 576 + (i + 1) * C, :] = mm_tn(n2_ref[...], dpre_ref[:, cols])
    grad = mm_tn(att_ref[...], dbb_ref[...])
    early_pack[1152:EARLY, 0:C] = grad[0:128, :]
    late_pack[432:448, 0:C] = grad[128:TOK, :]
    early_pack[1152:1200, C:256] = grad[TOK:C, 0:64]
    early_pack[1200:1248, C:256] = grad[TOK:C, 64:128]
    early_pack[1248:EARLY, C:256] = grad[TOK:176, 128:C]
    late_pack[432:448, C:256] = grad[176:C, 128:C]
    early.to_pair()
    scatter_all(
        out_ref, here["place_out"], here["pick_out"], own_out.at[0], full.at[0], edges_back.at[0]
    )
    out_copies = send_out(0)

    early.to_lon()
    d_bias[...] = jnp.zeros_like(d_bias)

    def attend_back(w, carry):
        rows = pl.ds(pl.multiple_of(w * TOK, TOK), TOK)
        prob = probs[w]
        d_stacked = split_heads(datt_ref[rows, :], heads)
        d_prob = mm_nt(d_stacked, v_ref[rows, :])
        d_score = prob * (d_prob - jnp.sum(d_prob * prob, axis=-1, keepdims=True))
        for h in range(HEADS):
            group = pl.ds(pl.multiple_of((2 * h + w // 2) * TOK, TOK), TOK)
            part = d_score[h * TOK : (h + 1) * TOK, :]
            d_bias[0, group, :] += part[:, 0:128]
            d_bias[1, group, 0:16] += part[:, 128:144]
        d_score_b = d_score.astype(BF16)
        dv_ref[rows, :] = mm_tn(prob.astype(BF16), d_stacked).astype(BF16)
        dq_ref[rows, :] = (join_heads(mm(d_score_b, k_ref[rows, :]), heads32) * scale).astype(BF16)
        stacked = split_heads(q_ref[rows, :], heads)
        dk_ref[rows, :] = (mm_tn(d_score_b, stacked) * scale).astype(BF16)
        return carry

    lax.fori_loop(0, WIN, attend_back, 0, unroll=2)
    pieces = EARLY // net.n_lon // 16

    d_normed = None
    for i, ref in enumerate((dq_ref, dk_ref, dv_ref)):
        grad = mm_tn(n1_ref[...], ref[...])
        late_pack[i * TOK : (i + 1) * TOK, 0:C] = grad[0:TOK, :]
        for j in range(3):
            rows = slice(i * TOK + j * 48, i * TOK + (j + 1) * 48)
            late_pack[rows, C:256] = grad[TOK:C, j * 64 : (j + 1) * 64]
        term = mm_nt(ref[...], w_qkv[:, i * C : (i + 1) * C])
        d_normed = term if d_normed is None else d_normed + term
    unit, inverse = norm(x_ref[...])
    late_pack[448:449, 0:C] = jnp.sum(d_normed * unit, axis=0, keepdims=True)
    out_ref[...] = dbranch_ref[...] + norm_grad(d_normed, gain1, unit, inverse)
    reduce_table(d_bias, here["spread"], parts, flat, table)
    late.to_pair()
    scatter_all(
        out_ref, here["place_out"], here["pick_out"], own_out.at[1], full.at[1], edges_back.at[1]
    )
    late.to_lon()
    early.to_owner(pieces)
    out_copies += send_out(1)

    def merge(i, target):
        for c in out_copies[3 * i : 3 * i + 3]:
            c.wait_recv()
        place = here["place_end"][...].astype(BF16)
        for lev in range(4):
            rows = [
                below_out[i, lev].astype(F32).reshape(72, C),
                own_out[i, lev].astype(F32).reshape(72, C),
            ]
            value = mm(place, jnp.concatenate(rows, axis=0).astype(BF16))
            value = value + mm(here["edge_end"][lev].astype(BF16), edge_out[i])
            target[(lev + 1) % 4] = value.reshape(6, 24, C).astype(BF16)

    merge(0, block_out)
    early.from_owner(pieces)
    late.to_lat()
    early.after_owner(pieces)
    late.from_lat()
    early.spread_pair()
    late.spread_pair()
    merge(1, grad_fields)
    early.close()
    late.close()
    early.close_owner(pieces)
    for c in net.started:
        c.wait_send()


def finish_kernel(n_k, *refs):
    hbm, outs, here = refs[0:4], refs[4:13], refs[13:17]
    early_rows, late_rows = refs[17:19]
    g_gain_one, g_w_qkv, g_table, g_w_proj, g_gain_two = refs[19:24]
    load_sem, store_sem = refs[24:26]
    loads = [pltpu.make_async_copy(hbm[i], here[i], load_sem.at[i]) for i in range(4)]
    for c in loads:
        c.start()
    early, late = here[0:2]
    out_w_in, out_w_out = outs[7], outs[8]
    stores = []

    def store(source, target):
        c = pltpu.make_async_copy(source, target, store_sem.at[len(stores)])
        c.start()
        stores.append(c)

    n_lon = 2 * n_k
    chunk = EARLY // n_lon
    loads[0].wait()
    for part in range(n_lon):
        early_rows[part * chunk : (part + 1) * chunk, :] = early[part % 2, part // 2].astype(F32)
    for i in range(3):
        cols = slice(i * 256, (i + 1) * 256)
        store(early_rows.at[i * C : (i + 1) * C, :], out_w_out.at[:, cols])
        store(early_rows.at[576 + i * C : 576 + (i + 1) * C, :], out_w_in.at[:, cols])
    for i in range(2):
        loads[2 + i].wait()
        store(here[2 + i], outs[i])
    loads[1].wait()
    rest, chunk = TABLE // n_lon, LATE // n_lon
    for part in range(n_lon):
        late_rows[part * chunk : (part + 1) * chunk, :] = late[
            part % 2, part // 2, 0:chunk, :
        ].astype(F32)
    for i in range(3):
        g_w_qkv[0:TOK, i * C : (i + 1) * C] = late_rows[i * TOK : (i + 1) * TOK, 0:C]
        for j in range(3):
            cols = slice(i * C + j * 64, i * C + (j + 1) * 64)
            g_w_qkv[TOK:C, cols] = late_rows[i * TOK + j * 48 : i * TOK + (j + 1) * 48, C:256]
    store(g_w_qkv, outs[3])
    g_w_proj[0:128, :] = early_rows[1152:EARLY, 0:C]
    g_w_proj[128:TOK, :] = late_rows[432:448, 0:C]
    g_w_proj[TOK:C, 0:64] = early_rows[1152:1200, C:256]
    g_w_proj[TOK:C, 64:128] = early_rows[1200:1248, C:256]
    g_w_proj[TOK:176, 128:C] = early_rows[1248:EARLY, C:256]
    g_w_proj[176:C, 128:C] = late_rows[432:448, C:256]
    store(g_w_proj, outs[5])
    g_gain_one[...] = late_rows[448:449, 0:C]
    store(g_gain_one, outs[2])
    g_gain_two[...] = late_rows[456:457, 0:C]
    store(g_gain_two, outs[6])
    for part in range(13):
        width = min(256, POS - part * 256)
        place, offset = divmod(part * 16, rest)
        value = late[place % 2, place // 2, chunk + offset : chunk + offset + 16, :].astype(F32)
        for h in range(HEADS):
            g_table[0, h, :, part * 256 : part * 256 + width] = value[2 * h : 2 * h + 2, 0:width]
    store(g_table, outs[4])
    for c in stores:
        c.wait()


def local(n_k, n_l, fields, cotangent, bias_table, gain_one, w_qkv, w_proj, gain_two, w_in, w_out):
    n_lon = 2 * n_k
    sds = jax.ShapeDtypeStruct
    vmem = pltpu.VMEM
    dma = pltpu.SemaphoreType.DMA
    whole = pl.BlockSpec(memory_space=pltpu.VMEM)
    apart = pl.BlockSpec(memory_space=pl.ANY)
    early, late = EARLY // n_lon, LATE // n_lon
    both = late + TABLE // n_lon
    inputs = (
        fields,
        cotangent,
        bias_table.transpose(0, 2, 1, 3),
        gain_one.reshape(1, C),
        w_qkv,
        w_proj,
        gain_two.reshape(1, C),
        w_in,
        w_out.T,
        jnp.asarray(place_level_in()),
        jnp.asarray(place_edge_in()),
        jnp.asarray(pick_edge_in()),
        jnp.asarray(place_level_out()),
        jnp.asarray(pick_edge_out()),
        jnp.asarray(spread_matrix()),
        jnp.asarray(region_masks()),
        jnp.asarray(head_masks()),
        jnp.asarray(place_level_end()),
        jnp.asarray(place_edge_end()),
    )

    def buffers(chunk, kept):
        return [
            vmem((n_k, chunk, 256), BF16),
            vmem((n_k, chunk, 256), BF16),
            vmem((n_k - 1, chunk, 256), BF16),
            vmem((n_k - 1, chunk, 256), BF16),
            vmem((chunk, 256), F32),
            vmem((n_l, kept, 256), BF16),
            vmem((n_l, 16, 256), BF16),
        ]

    slots = max(n_k, n_l)
    results = pl.pallas_call(
        functools.partial(block_kernel, n_k, n_l),
        out_shape=(
            sds((2, n_k, early, 256), BF16),
            sds((2, n_k, both, 256), BF16),
            sds((4, 6, 24, C), BF16),
            sds((4, 6, 24, C), BF16),
        ),
        in_specs=[apart] * len(INPUTS),
        out_specs=[whole] * 4,
        scratch_shapes=[vmem(value.shape, value.dtype) for value in inputs]
        + [
            vmem((2, 4, 3, 24, C), BF16),
            vmem((2, 2 * EDGE, C), BF16),
            vmem((2, 2 * EDGE, C), BF16),
            vmem((2, 4, 3, 24, C), BF16),
            vmem((2, 2 * EDGE, C), BF16),
            vmem((2, 4, 3, 24, C), BF16),
            vmem((2, 4, 3, 24, C), BF16),
            vmem((2, 2 * EDGE, C), BF16),
            vmem((ROWS, C), F32),
            vmem((ROWS, C), BF16),
            vmem((ROWS, C), BF16),
            vmem((ROWS, C), BF16),
            vmem((ROWS, C), BF16),
            vmem((ROWS, C), BF16),
            vmem((2, STACK, TOK), F32),
            vmem((WIN, STACK, TOK), F32),
            vmem((ROWS, C), BF16),
            vmem((ROWS, FFH), BF16),
            vmem((ROWS, FFH), BF16),
            vmem((ROWS, C), BF16),
            vmem((ROWS, C), BF16),
            vmem((ROWS, C), F32),
            vmem((ROWS, C), BF16),
            vmem((ROWS, C), F32),
            vmem((ROWS, C), BF16),
            vmem((ROWS, C), BF16),
            vmem((ROWS, C), BF16),
            vmem((2, 2 * STACK, 128), F32),
            vmem((4, TOK, 128), F32),
            vmem((2, 2 * STACK, 128), F32),
            vmem((16, 4096), F32),
            vmem((EARLY, 256), F32),
            vmem((LATE, 256), F32),
            vmem((TABLE, 256), F32),
        ]
        + buffers(early, 16)
        + buffers(both, late)
        + [
            dma((len(INPUTS),)),
            dma((2, 2, 3)),
            dma((2, 2, 3)),
            dma((12, slots)),
            dma((12, slots)),
        ],
        compiler_params=pltpu.CompilerParams(
            collective_id=0, has_side_effects=True, vmem_limit_bytes=60 * 1024 * 1024
        ),
        name="block",
    )(*inputs)
    shapes = (
        sds((4, 6, 24, C), BF16),
        sds((4, 6, 24, C), BF16),
        sds((1, C), F32),
        sds((C, 3 * C), F32),
        sds((1, HEADS, 2, POS), F32),
        sds((C, C), F32),
        sds((1, C), F32),
        sds((C, FFH), F32),
        sds((C, FFH), F32),
    )
    outs = pl.pallas_call(
        functools.partial(finish_kernel, n_k),
        out_shape=shapes,
        in_specs=[apart] * 4,
        out_specs=[apart] * 9,
        scratch_shapes=[vmem(value.shape, value.dtype) for value in results]
        + [vmem((EARLY, 256), F32), vmem((LATE, 256), F32)]
        + [vmem(value.shape, value.dtype) for value in shapes[2:7]]
        + [dma((4,)), dma((13,))],
        compiler_params=pltpu.CompilerParams(vmem_limit_bytes=60 * 1024 * 1024),
        name="finish",
    )(*results)
    outs = list(outs)
    outs[2] = outs[2].reshape(C)
    outs[4] = outs[4].transpose(0, 2, 1, 3)
    outs[6] = outs[6].reshape(C)
    outs[8] = outs[8].T
    return tuple(outs)


def solution(mesh):
    n_k, n_l = mesh.shape["lon"] // 2, mesh.shape["lat"]
    placed = (
        P(None, "lat", "lon", None),
        P(None, "lat", "lon", None),
        P("lat", None, None, None),
    ) + (P(),) * 6
    return jax.shard_map(
        functools.partial(local, n_k, n_l),
        mesh=mesh,
        in_specs=placed,
        out_specs=(
            P(None, "lat", "lon", None),
            P(None, "lat", "lon", None),
            P(),
            P(),
            P("lat", None, None, None),
            P(),
            P(),
            P(),
            P(),
        ),
        check_vma=False,
    )
```
